256 devices in a mesh: grp: 8 (over y, core), dev: 32 (over x, z).
Axes of the slice: x: 4, y: 4, z: 8, core: 2. Of those that a mesh axis runs over, the one named last changes fastest.
Arguments:
- residual_edges: float32 [16, 1376256], P(None, ('grp', 'dev')), may hold values from -6 to 6
- pi_block: float32 [144, 192], replicated, may hold values from -0.4375 to 0.4375
- stiff_block: float32 [64, 64], replicated, may hold values from -0.05 to 5.15, as said below
- mass_block: float32 [64, 64], replicated, may hold values from -0.03 to 3.89, as said below
- permittivity: float32 [6, 16384], P(None, ('grp', 'dev')), may hold values from -1.6 to 4, as said below
- curl_coef: float32 [16384], P(('grp', 'dev')), may hold values from 0.02 to 2
- edge_map: int32 [144, 16384], P(None, ('grp', 'dev')), may hold values from 0 to 6719, as said below
- local_map: int32 [64, 16384], P(None, ('grp', 'dev')), may hold values from 0 to 2047
- node_owner: int32 [524288], P(('grp', 'dev')), may hold values from 0 to 31, as said below
- node_slot: int32 [524288], P(('grp', 'dev')), may hold values from 0 to 1727
Outputs:
- correction: float32 [16, 1376256], P(None, ('grp', 'dev'))
The draws below stay inside these ranges and needn't reach their ends.
Inputs may be any that keep to these rules, and one draw needn't show every extreme that they name: `edge_map`: entries of one device's elements (aligned blocks of 64 columns) below 672 or at 6048 or above occur only where the neighbouring block along grp+dev order exists; both ends of the range are reached wherever that neighbour exists. `node_owner`: among the 2048 touched nodes of one device at most 128 have the same owner; in every group one owner has exactly 128 from every device of that group. `stiff_block`: Symmetric; diagonal entries between 4.15 and 5.15, the others within 0.05 of zero. `mass_block`: Symmetric; diagonal entries between 2.89 and 3.89, the others within 0.03 of zero. `permittivity`: rows 0 to 2 lie between 0.05 and 4; rows 3 to 5 within 1.6 of zero.
All inputs are finite; a program needn't handle non-finite values.
Results may differ from the reference program's by a relative error of at most 0.0003.
Values sent between devices are 32-bit elements; how exact they have to be, the bound alone decides.
No kernel may reach another device: no remote copies, remote signals or barrier semaphores. Data moves between devices by JAX's collectives and lax.ppermute only.
A program may use at most 128 MiB of HBM per device.

```python
import math
import jax
import jax.numpy as jnp
from jax import lax

RHS = 16
ED = 144
NN = 64
NC = 192
EL = 64
E_LOC = 5376
RIM = 672
N_LOC = 1728
U_LOC = 2048
ELEMS = 16384
EDGES = 1376256
TOUCHED = 524288
N_DEV = 32


def symmetric_block(key, spread):
    upper = jax.random.uniform(key, (NN, NN), jnp.float32, -spread, spread)
    sym = 0.5 * (upper + upper.T)
    diag_key = jax.random.fold_in(key, 7)
    base = jax.random.uniform(diag_key, (NN,), jnp.float32, 1.0, 2.0) + spread * (NN - 1)
    return jnp.where(jnp.eye(NN, dtype=bool), base[:, None], sym)


def draw_stiff_block(key, part):
    key = jax.random.fold_in(key, 11)
    return symmetric_block(key, 0.05)


def draw_mass_block(key, part):
    key = jax.random.fold_in(key, 12)
    return symmetric_block(key, 0.03)


def draw_permittivity(key, part):
    key = jax.random.fold_in(key, 13)
    diag_key, off_key = jax.random.split(key)
    diag_part = jnp.exp(jax.random.uniform(diag_key, (3, ELEMS), jnp.float32, -2.9957323, 1.3862944))
    factor = jax.random.uniform(off_key, (3, ELEMS), jnp.float32, -0.4, 0.4)
    off_xy = factor[0] * jnp.sqrt(diag_part[0] * diag_part[1])
    off_xz = factor[1] * jnp.sqrt(diag_part[0] * diag_part[2])
    off_yz = factor[2] * jnp.sqrt(diag_part[1] * diag_part[2])
    return jnp.concatenate([diag_part, jnp.stack([off_xy, off_xz, off_yz], axis=0)], axis=0)


def draw_edge_map(key, part):
    key = jax.random.fold_in(key, 14)
    blocks = ELEMS // EL
    element = jnp.arange(ELEMS, dtype=jnp.int32)
    block = element // EL
    within = element % EL
    base_start = block * E_LOC
    own = jax.random.randint(jax.random.fold_in(key, 1), (ED, ELEMS), 0, E_LOC) + base_start[None, :]
    pick = jax.random.randint(jax.random.fold_in(key, 2), (ED, ELEMS), 0, 2) == 1
    depth = jax.random.randint(jax.random.fold_in(key, 3), (ED, ELEMS), 0, RIM)
    lower = base_start[None, :] - 1 - depth
    upper = base_start[None, :] + E_LOC + depth
    use_low = pick & ((within < EL // 4) & (block > 0))[None, :]
    use_up = pick & ((within >= EL - EL // 4) & (block < blocks - 1))[None, :]
    result = jnp.where(use_low, lower, jnp.where(use_up, upper, own))
    first_cond = (within == 0) & (block > 0)
    last_cond = (within == EL - 1) & (block < blocks - 1)
    top_row = jnp.where(first_cond, base_start - RIM, jnp.where(last_cond, base_start + E_LOC + RIM - 1, result[0]))
    result = result.at[0].set(top_row)
    return result - base_start[None, :] + RIM


def draw_node_owner(key, part):
    key = jax.random.fold_in(key, 15)
    blocks = TOUCHED // U_LOC
    capacity = 2 * U_LOC // N_DEV
    remain = U_LOC - capacity
    heavy_count = (N_DEV - 1) // 2
    light_count = N_DEV - 1 - heavy_count
    heavy_rows = 2 * remain // 3
    hot = jax.random.randint(jax.random.fold_in(key, 1), (blocks // N_DEV,), 0, N_DEV)
    hot_each = hot[jnp.arange(blocks, dtype=jnp.int32) // N_DEV]
    row_keys = jax.random.split(jax.random.fold_in(key, 2), blocks)
    row_perms = jax.vmap(lambda sub_key: jax.random.permutation(sub_key, U_LOC))(row_keys)
    peer_keys = jax.random.split(jax.random.fold_in(key, 3), blocks)
    peer_perms = jax.vmap(lambda sub_key: jax.random.permutation(sub_key, N_DEV - 1))(peer_keys)
    ranks = jnp.arange(U_LOC, dtype=jnp.int32)
    beyond = jnp.maximum(ranks - capacity, 0)
    place = jnp.where(beyond < heavy_rows, beyond % heavy_count, heavy_count + (beyond - heavy_rows) % light_count)
    others = jnp.take_along_axis(peer_perms, jnp.broadcast_to(place[None, :], (blocks, U_LOC)), axis=1)
    others = jnp.where(others >= hot_each[:, None], others + 1, others)
    ranked_owner = jnp.where(ranks[None, :] < capacity, hot_each[:, None], others)
    owner = jax.vmap(lambda perm_row, owner_row: jnp.zeros((U_LOC,), jnp.int32).at[perm_row].set(owner_row))(row_perms, ranked_owner)
    return owner.reshape(TOUCHED)


def set_ends(values, stream_key, low, largest):
    index_at = [jax.random.randint(jax.random.fold_in(stream_key, axis), (), 0, length) for axis, length in enumerate(values.shape)]
    main_axis = values.shape.index(max(values.shape))
    neighbour = index_at[:main_axis] + [(index_at[main_axis] + 1) % values.shape[main_axis]] + index_at[main_axis + 1:]
    return values.at[tuple(index_at)].set(low).at[tuple(neighbour)].set(largest)


def steps_of(own_key, extent, cuts, least, top_value):
    gain, own = 1.0, jax.random.fold_in(own_key, 6)
    for axis_at, parts in cuts:
        steps = jnp.exp(jax.random.uniform(jax.random.fold_in(own, axis_at), (parts,), jnp.float32, least / len(cuts), top_value / len(cuts)))
        gain = gain * jnp.repeat(steps, extent[axis_at] // parts).reshape([-1 if axis == axis_at else 1 for axis in range(len(extent))])
    return gain


def gaussian(stream_key, dims, deviation, reach, shards=(), kind=jnp.bfloat16):
    drawn = jax.random.normal(stream_key, dims, jnp.float32) * deviation
    if len(shards) > 0:
        drawn = steps_of(stream_key, dims, shards, -0.22, 0.18) * drawn
    return jnp.clip(drawn, min=-reach, max=reach).astype(kind)


def setup_inputs(seed: int = 0) -> dict:
    splits = jax.random.split(jax.random.key(seed), 11)
    residual_edges = gaussian(splits[0], (RHS, EDGES), 1.0, 6.0, ((1, 256),), jnp.float32)
    pi_block = gaussian(splits[1], (ED, NC), NC ** -0.5, 0.4375, (), jnp.float32)
    stiff_block = draw_stiff_block(jax.random.fold_in(splits[10], 71), 0)
    mass_block = draw_mass_block(jax.random.fold_in(splits[10], 71), 0)
    permittivity = draw_permittivity(jax.random.fold_in(splits[10], 71), 0)
    curl_coef = jnp.clip(jnp.exp(math.log(2.0) - 4.6051702 * jax.random.uniform(splits[5], (ELEMS,), jnp.float32) ** steps_of(splits[5], (ELEMS,), ((0, 256),), -0.2, 0.2)), 0.02, 2.0)
    edge_map = draw_edge_map(jax.random.fold_in(splits[10], 71), 0)
    local_map = set_ends(jax.random.randint(splits[7], (NN, ELEMS), 0, U_LOC), jax.random.fold_in(splits[7], 1), 0, U_LOC - 1).astype(jnp.int32)
    node_owner = draw_node_owner(jax.random.fold_in(splits[10], 71), 0)
    node_slot = set_ends(jax.random.randint(splits[9], (TOUCHED,), 0, N_LOC), jax.random.fold_in(splits[9], 1), 0, N_LOC - 1).astype(jnp.int32)
    return dict(residual_edges=residual_edges, pi_block=pi_block, stiff_block=stiff_block, mass_block=mass_block, permittivity=permittivity, curl_coef=curl_coef, edge_map=edge_map, local_map=local_map, node_owner=node_owner, node_slot=node_slot)


HIGH = lax.Precision.HIGHEST
CHEB_LOW = 0.3
CHEB_HIGH = 2.0


def cheb_factors():
    center = 0.5 * (CHEB_HIGH + CHEB_LOW)
    half_width = 0.5 * (CHEB_HIGH - CHEB_LOW)
    sigma_ratio = center / half_width
    rho_first = 1.0 / sigma_ratio
    rho_second = 1.0 / (2.0 * sigma_ratio - rho_first)
    return 1.0 / center, 1.0 + rho_second * rho_first, 2.0 * rho_second / half_width


def mixed_terms(stiff_part, mass_part, curl_scale, tensor):
    row_x = curl_scale * stiff_part[:, 0] + tensor[0] * mass_part[:, 0] + tensor[3] * mass_part[:, 1] + tensor[4] * mass_part[:, 2]
    row_y = curl_scale * stiff_part[:, 1] + tensor[3] * mass_part[:, 0] + tensor[1] * mass_part[:, 1] + tensor[5] * mass_part[:, 2]
    row_z = curl_scale * stiff_part[:, 2] + tensor[4] * mass_part[:, 0] + tensor[5] * mass_part[:, 1] + tensor[2] * mass_part[:, 2]
    return jnp.stack([row_x, row_y, row_z], axis=1)


def element_apply(values, stiff_block, mass_block, curl_scale, tensor):
    stiff_part = jnp.einsum("kj,rcje->rcke", stiff_block, values, precision=HIGH)
    mass_part = jnp.einsum("kj,rcje->rcke", mass_block, values, precision=HIGH)
    return mixed_terms(stiff_part, mass_part, curl_scale, tensor)


def diag_terms(stiff_block, mass_block, curl_scale, tensor):
    stiff_diag = jnp.diagonal(stiff_block)[:, None]
    mass_diag = jnp.diagonal(mass_block)[:, None]
    base = curl_scale[None, :] * stiff_diag
    return jnp.stack([base + mass_diag * tensor[0][None, :], base + mass_diag * tensor[1][None, :], base + mass_diag * tensor[2][None, :]], axis=0)


def reference(residual_edges, pi_block, stiff_block, mass_block, permittivity, curl_coef, edge_map, local_map, node_owner, node_slot):
    blocks = ELEMS // EL
    node_total = blocks * N_LOC
    holder = jnp.arange(TOUCHED, dtype=jnp.int32) // U_LOC
    global_ids = ((holder // N_DEV) * N_DEV + node_owner) * N_LOC + node_slot
    first, keep, step = cheb_factors()
    block_list = jnp.arange(blocks, dtype=jnp.int32)

    def block_data(block):
        offset = block * EL
        edges = lax.dynamic_slice_in_dim(edge_map, offset, EL, 1) + (block * E_LOC - RIM).astype(jnp.int32)
        local_ids = lax.dynamic_slice_in_dim(local_map, offset, EL, 1)
        node_ids = global_ids[block * U_LOC + local_ids]
        tensor = lax.dynamic_slice_in_dim(permittivity, offset, EL, 1)
        curl_scale = lax.dynamic_slice_in_dim(curl_coef, offset, EL, 0)
        return edges, node_ids, tensor, curl_scale

    def restrict(carry, block):
        node_sum, diag_sum = carry
        edges, node_ids, tensor, curl_scale = block_data(block)
        edge_values = residual_edges[:, edges]
        node_terms = jnp.einsum("dp,rde->rpe", pi_block, edge_values, precision=HIGH).reshape(RHS, 3, NN, EL)
        node_sum = node_sum.at[:, :, node_ids].add(node_terms)
        diag_sum = diag_sum.at[:, node_ids].add(diag_terms(stiff_block, mass_block, curl_scale, tensor))
        return (node_sum, diag_sum), None

    start_nodes = jnp.zeros((RHS, 3, node_total), jnp.float32)
    start_diag = jnp.zeros((3, node_total), jnp.float32)
    (rhs_nodes, diag_nodes), _ = lax.scan(restrict, (start_nodes, start_diag), block_list)
    floored = jnp.maximum(diag_nodes, 1.0)
    first_iter = first * rhs_nodes / floored[None]

    def operate(carry, block):
        edges, node_ids, tensor, curl_scale = block_data(block)
        values = first_iter[:, :, node_ids]
        return carry.at[:, :, node_ids].add(element_apply(values, stiff_block, mass_block, curl_scale, tensor)), None

    applied, _ = lax.scan(operate, jnp.zeros((RHS, 3, node_total), jnp.float32), block_list)
    second_iter = keep * first_iter + step * (rhs_nodes - applied) / floored[None]

    def prolong(carry, block):
        edges, node_ids, tensor, curl_scale = block_data(block)
        values = second_iter[:, :, node_ids].reshape(RHS, 3 * NN, EL)
        edge_terms = jnp.einsum("dp,rpe->rde", pi_block, values, precision=HIGH)
        return carry.at[:, edges].add(edge_terms), None

    correction, _ = lax.scan(prolong, jnp.zeros((RHS, EDGES), jnp.float32), block_list)
    return correction
```

```python
import jax
import jax.numpy as jnp
from jax import lax
from jax.experimental import pallas as pl
from jax.experimental.pallas import tpu as pltpu
from jax.sharding import PartitionSpec as P

RHS = 16
ED = 144
NN = 64
EL = 64
E_LOC = 5376
RIM = 672
U_LOC = 2048
PEERS = 32
CAP = 128
ROWS = 3 * RHS
SENT = ROWS + 4
SLOTS = PEERS * CAP
ELN = NN * EL
LANE = 128
WIDE = 256
RIM_W = 768
H_OWN = E_LOC // WIDE
H_RIM = RIM_W // WIDE
H_EDGE = H_OWN + 2 * H_RIM
H_POS = SLOTS // WIDE
H_NODE = 7
E_TILES = 72
N_TILES = ELN // LANE
BF = jnp.bfloat16
F32 = jnp.float32
I32 = jnp.int32

CHEB_LOW = 0.3
CHEB_HIGH = 2.0


def cheb_factors():
    center = 0.5 * (CHEB_HIGH + CHEB_LOW)
    half_width = 0.5 * (CHEB_HIGH - CHEB_LOW)
    sigma_ratio = center / half_width
    rho_first = 1.0 / sigma_ratio
    rho_second = 1.0 / (2.0 * sigma_ratio - rho_first)
    return (1.0 / center, 1.0 + rho_second * rho_first, 2.0 * rho_second / half_width)


def split(x):
    high = x.astype(BF)
    return high, (x - high.astype(F32)).astype(BF)


def iota(shape, dim):
    return lax.broadcasted_iota(I32, shape, dim)


def spread(index_rows, height):
    return jnp.concatenate(
        [jnp.broadcast_to(index_rows[i : i + 1], (height, LANE)) for i in range(index_rows.shape[0])],
        axis=1,
    )


def one_hot_low(index_rows):
    low = spread(index_rows & (WIDE - 1), WIDE)
    return jnp.where(low == iota(low.shape, 0), 1.0, 0.0).astype(BF)


def gather_tile(table, index_rows, rows, count):
    hot = one_hot_low(index_rows)
    found = jnp.dot(table, jnp.concatenate([hot, hot], axis=0), preferred_element_type=F32)
    high = spread(index_rows >> 8, rows)
    out = found[:rows]
    for h in range(1, count):
        out = jnp.where(high == h, found[h * rows : (h + 1) * rows], out)
    return out


def fill_table(table, source, rows, count):
    for h in range(count):
        high, low = split(source(h))
        table[h * rows : (h + 1) * rows, :WIDE] = high
        table[h * rows : (h + 1) * rows, WIDE:] = low


def mask_rows(left, base, x, high_part, count):
    rows, width = x[0].shape
    high_b = jnp.broadcast_to(high_part, (rows, width))
    for h in range(count):
        here = high_b == float(h)
        for k in (0, 1):
            left[base + h * rows : base + (h + 1) * rows, k * width : (k + 1) * width] = jnp.where(
                here, x[k], jnp.zeros_like(x[k])
            )


def high_bf(index_rows):
    return spread((index_rows >> 8), 1).astype(F32).astype(BF)


def mask_diag(left, base, diag, index_rows):
    width = diag[0].shape[1]
    here = spread(index_rows >> 8, 16) == iota((16, width), 0)
    for c in range(3):
        high, low = split(jnp.where(here, jnp.broadcast_to(diag[c], (16, width)), 0.0))
        left[base + c * 16 : base + (c + 1) * 16, :width] = high
        left[base + c * 16 : base + (c + 1) * 16, width:] = low


def accumulate(acc, step, left, index_rows):
    hot = one_hot_low(index_rows)
    part = lax.dot_general(
        left[...],
        jnp.concatenate([hot, hot], axis=1),
        (((1,), (1,)), ((), ())),
        preferred_element_type=F32,
    )

    @pl.when(step == 0)
    def _():
        acc[...] = part

    @pl.when(step > 0)
    def _():
        acc[...] += part


def rows8(step):
    return pl.ds(pl.multiple_of(step * 8, 8), 8)


def lanes(step, width):
    return pl.ds(pl.multiple_of(step * width, width), width)


def prep_kernel(res, em, lm, owner, slot, epos_out, pos_out, slot_out, ev_out, table, hots, rank_s, pos_s):
    m = em[...]
    epos_out[...] = jnp.where(
        m < RIM,
        m + (E_LOC + RIM_W - RIM),
        jnp.where(m < RIM + E_LOC, m - RIM, m - (RIM + E_LOC) + E_LOC + RIM_W),
    )
    chunks = U_LOC // LANE
    for t in range(chunks):
        o = jnp.broadcast_to(owner[t : t + 1, :], (PEERS, LANE))
        hots[t * PEERS : (t + 1) * PEERS, :] = jnp.where(o == iota((PEERS, LANE), 0), 1.0, 0.0).astype(BF)
    before = jnp.where(iota((LANE, LANE), 0) < iota((LANE, LANE), 1), 1.0, 0.0)
    tri = jnp.concatenate([before, jnp.ones((LANE, LANE), F32)], axis=1).astype(BF)
    ranks = jnp.dot(hots[...], tri, preferred_element_type=F32)
    base = jnp.zeros((PEERS, LANE), F32)
    for t in range(chunks):
        hot = hots[t * PEERS : (t + 1) * PEERS, :].astype(F32)
        here = ranks[t * PEERS : (t + 1) * PEERS]
        rank = jnp.sum(hot * (here[:, :LANE] + base), axis=0, keepdims=True).astype(I32)
        base = base + here[:, LANE:]
        rank_s[t : t + 1, :] = rank
        pos_s[t : t + 1, :] = owner[t : t + 1, :] * CAP + rank
    left = []
    right = []
    for t in range(chunks):
        hot = hots[t * PEERS : (t + 1) * PEERS, :].astype(F32)
        s = slot[t : t + 1, :] + 1
        left.append(
            jnp.concatenate([hot * (s >> 6).astype(F32), hot * (s & 63).astype(F32)], axis=0).astype(BF)
        )
        r = jnp.broadcast_to(rank_s[t : t + 1, :], (LANE, LANE))
        right.append(jnp.where(r == iota((LANE, LANE), 0), 1.0, 0.0).astype(BF))
    packed = lax.dot_general(
        jnp.concatenate(left, axis=1),
        jnp.concatenate(right, axis=1),
        (((1,), (1,)), ((), ())),
        preferred_element_type=F32,
    )
    slot_out[...] = packed[:PEERS] * 64.0 + packed[PEERS:] - 1.0
    idx = lm[...]
    high, low = idx >> 7, idx & (LANE - 1)
    pos = jnp.zeros((N_TILES, LANE), I32)
    for t in range(chunks):
        row = jnp.broadcast_to(pos_s[t : t + 1, :], (N_TILES, LANE))
        pos = jnp.where(high == t, jnp.take_along_axis(row, low, axis=1), pos)
    pos_out[...] = pos
    fill_table(table, lambda h: res[:, h * WIDE : (h + 1) * WIDE], RHS, H_OWN)

    def body(step, carry):
        ev_out[:, lanes(step, 1024)] = gather_tile(table[...], epos_out[rows8(step), :], RHS, H_OWN)
        return carry

    lax.fori_loop(0, E_TILES // 8, body, 0)


def fill_pi(w, pi):
    zero = jnp.zeros((384, 384), BF)
    for v in range(4):
        for k in (0, 1):
            w[v, k] = zero
    for c in range(3):
        part = split(pi[:, c * NN : (c + 1) * NN])
        for k in (0, 1):
            for e2 in (0, 1):
                cols = slice(c * LANE + e2 * NN, c * LANE + (e2 + 1) * NN)
                for v in range(4):
                    w[v, k, e2 * LANE : (e2 + 1) * LANE, cols] = part[k][:LANE]
                    at = 2 * LANE + (2 * v + e2) * 16
                    w[v, k, at : at + 16, cols] = part[k][LANE:]


def fill_coefs(coef, wide, perm, curl):
    coef[...] = jnp.zeros((8, LANE), F32)
    coef[0:6, 0:EL] = perm[...]
    coef[6:7, 0:EL] = curl[...]
    c = coef[...]
    second = jnp.where(iota((8, LANE), 1) >= NN, 1, 0)
    for t in range(N_TILES):
        wide[:, t * LANE : (t + 1) * LANE] = jnp.take_along_axis(c, second + 2 * t, axis=1)


def restrict_kernel(
    ev_own, before, after, epos, pos, slots, pi, stiff, mass, perm, curl,
    out, table, ev, w, coef, wide, xs, diag, left, acc,
):
    def rim(h):
        ref = before if h < H_RIM else after
        at = h % H_RIM * WIDE
        return ref[:, at : at + WIDE]

    fill_table(table, rim, RHS, 2 * H_RIM)

    def rim_body(step, carry):
        idx = epos[rows8(step), :] - E_LOC
        found = gather_tile(table[...], idx, RHS, 2 * H_RIM)
        at = lanes(step, 1024)
        ev[:, at] = jnp.where(spread(idx, RHS) >= 0, found, ev_own[:, at])
        return carry

    lax.fori_loop(0, E_TILES // 8, rim_body, 0)
    fill_pi(w, pi)
    for v in range(4):
        blocks = []
        for g in range(8):
            t = 4 * g + v
            blocks.append(
                jnp.concatenate(
                    [ev[:, 2 * t * LANE : (2 * t + 2) * LANE], ev[:, (EL + g) * LANE : (EL + g + 1) * LANE]],
                    axis=1,
                )
            )
        high, low = split(jnp.concatenate(blocks, axis=0))
        y = (
            jnp.dot(high, w[v, 0], preferred_element_type=F32)
            + jnp.dot(high, w[v, 1], preferred_element_type=F32)
            + jnp.dot(low, w[v, 0], preferred_element_type=F32)
        )
        for g in range(8):
            t = 4 * g + v
            for c in range(3):
                part = split(y[g * RHS : (g + 1) * RHS, c * LANE : (c + 1) * LANE])
                for k in (0, 1):
                    xs[k, c * RHS : (c + 1) * RHS, t * LANE : (t + 1) * LANE] = part[k]
    fill_coefs(coef, wide, perm, curl)
    eye = iota((NN, NN), 0) == iota((NN, NN), 1)

    def diagonal(ref):
        d = jnp.sum(jnp.where(eye, ref[...], 0.0), axis=0, keepdims=True)
        return jnp.concatenate([d, d], axis=1)

    sd, md = diagonal(stiff), diagonal(mass)
    for t in range(N_TILES):
        at = slice(t * LANE, (t + 1) * LANE)
        diag[:, at] = wide[6:7, at] * sd + md * wide[0:3, at]

    def body(step, carry):
        at = lanes(step, 1024)
        idx = pos[rows8(step), :]
        mask_rows(left, 0, (xs[0, :, at], xs[1, :, at]), high_bf(idx), H_POS)
        mask_diag(left, H_POS * ROWS, [diag[c : c + 1, at] for c in range(3)], idx)
        accumulate(acc, step, left, idx)
        return carry

    lax.fori_loop(0, ELN // 1024, body, 0)
    unpack(out, acc)
    for p in range(PEERS):
        h, at = p // 2, slice(p % 2 * LANE, (p % 2 + 1) * LANE)
        for c in range(3):
            row = H_POS * ROWS + c * 16 + h
            out[p, ROWS + c : ROWS + c + 1, :] = acc[row : row + 1, at]
        out[p, SENT - 1 : SENT, :] = slots[p : p + 1, :]


def unpack(out, acc):
    for p in range(PEERS):
        h, at = p // 2, slice(p % 2 * LANE, (p % 2 + 1) * LANE)
        out[p, 0:ROWS, :] = acc[h * ROWS : (h + 1) * ROWS, at]


def collect(arrived, slots, left, acc, with_diag):
    def body(step, carry):
        idx = slots[rows8(step), :]
        block = arrived[rows8(step)]
        x = jnp.concatenate([block[i, 0:ROWS] for i in range(8)], axis=1)
        mask_rows(left, 0, split(x), high_bf(idx), H_NODE)
        if with_diag:
            diag = [
                jnp.concatenate([block[i, ROWS + c : ROWS + c + 1] for i in range(8)], axis=1)
                for c in range(3)
            ]
            mask_diag(left, H_NODE * ROWS, diag, idx)
        accumulate(acc, step, left, idx)
        return carry

    lax.fori_loop(0, PEERS // 8, body, 0)


def serve(out, table, slots):
    def body(step, carry):
        found = gather_tile(table[...], slots[rows8(step), :], ROWS, H_NODE)
        for i in range(8):
            out[step * 8 + i] = found[:, i * LANE : (i + 1) * LANE]
        return carry

    lax.fori_loop(0, PEERS // 8, body, 0)


def first_kernel(arrived, out, rhs_out, floor_out, slot_out, table, left, acc):
    first = cheb_factors()[0]
    for p in range(PEERS):
        slot_out[p : p + 1, :] = arrived[p, SENT - 1 : SENT, :].astype(I32)
    collect(arrived, slot_out, left, acc, True)
    for h in range(H_NODE):
        rhs_out[h] = acc[h * ROWS : (h + 1) * ROWS, :]
        for c in range(3):
            row = H_NODE * ROWS + c * 16 + h
            floor_out[h, c : c + 1, :] = jnp.maximum(acc[row : row + 1, :], 1.0)

    def value(h):
        parts = []
        for c in range(3):
            part = rhs_out[h, c * RHS : (c + 1) * RHS, :]
            parts.append(first * part / floor_out[h, c : c + 1, :])
        return jnp.concatenate(parts, axis=0)

    fill_table(table, value, ROWS, H_NODE)
    serve(out, table, slot_out)


def second_kernel(arrived, rhs, floor, slots, out, table, left, acc):
    first, keep, step = cheb_factors()
    collect(arrived, slots, left, acc, False)

    def value(h):
        parts = []
        for c in range(3):
            at = slice(c * RHS, (c + 1) * RHS)
            part = rhs[h, at, :]
            applied = acc[h * ROWS + c * RHS : h * ROWS + (c + 1) * RHS, :]
            low = floor[h, c : c + 1, :]
            parts.append(keep * (first * part / low) + step * (part - applied) / low)
        return jnp.concatenate(parts, axis=0)

    fill_table(table, value, ROWS, H_NODE)
    serve(out, table, slots)


def pair(arrived):
    return lambda h: jnp.concatenate([arrived[2 * h], arrived[2 * h + 1]], axis=1)


def apply_kernel(arrived, pos, stiff, mass, perm, curl, out, table, op, coef, wide, left, acc):
    fill_table(table, pair(arrived), ROWS, H_POS)
    fill_coefs(coef, wide, perm, curl)
    op[...] = jnp.zeros((2, LANE, 2 * LANE), BF)
    for m, ref in enumerate((stiff, mass)):
        part = split(ref[...].T)
        for k in (0, 1):
            for e2 in (0, 1):
                at = slice(m * LANE + e2 * NN, m * LANE + (e2 + 1) * NN)
                op[k, e2 * NN : (e2 + 1) * NN, at] = part[k]

    def body(step, carry):
        idx = pos[rows8(step), :]
        values = gather_tile(table[...], idx, ROWS, H_POS)
        high, low = split(
            jnp.concatenate([values[:, i * LANE : (i + 1) * LANE] for i in range(8)], axis=0)
        )
        y = (
            jnp.dot(high, op[0], preferred_element_type=F32)
            + jnp.dot(high, op[1], preferred_element_type=F32)
            + jnp.dot(low, op[0], preferred_element_type=F32)
        )
        cols = wide[:, lanes(step, 1024)]
        tiles = []
        for i in range(8):
            k = cols[:, i * LANE : (i + 1) * LANE]
            s = [y[i * ROWS + c * RHS : i * ROWS + (c + 1) * RHS, :LANE] for c in range(3)]
            m = [y[i * ROWS + c * RHS : i * ROWS + (c + 1) * RHS, LANE:] for c in range(3)]
            tensor = ((0, 3, 4), (3, 1, 5), (4, 5, 2))
            tiles.append(
                jnp.concatenate(
                    [
                        k[6:7] * s[c]
                        + k[tensor[c][0]][None] * m[0]
                        + k[tensor[c][1]][None] * m[1]
                        + k[tensor[c][2]][None] * m[2]
                        for c in range(3)
                    ],
                    axis=0,
                )
            )
        mask_rows(left, 0, split(jnp.concatenate(tiles, axis=1)), high_bf(idx), H_POS)
        accumulate(acc, step, left, idx)
        return carry

    lax.fori_loop(0, ELN // 1024, body, 0)
    unpack(out, acc)


def prolong_kernel(arrived, pos, epos, pi, own, low_out, high_out, table, w, values, terms, left, acc):
    fill_table(table, pair(arrived), ROWS, H_POS)
    fill_pi(w, pi)

    def gather_body(step, carry):
        values[:, lanes(step, 1024)] = gather_tile(table[...], pos[rows8(step), :], ROWS, H_POS)
        return carry

    lax.fori_loop(0, ELN // 1024, gather_body, 0)
    dims = (((1,), (1,)), ((), ()))
    rest = None
    for v in range(4):
        blocks = []
        for g in range(8):
            at = slice((4 * g + v) * LANE, (4 * g + v + 1) * LANE)
            blocks.append(
                jnp.concatenate([values[c * RHS : (c + 1) * RHS, at] for c in range(3)], axis=1)
            )
        high, low = split(jnp.concatenate(blocks, axis=0))
        y = (
            lax.dot_general(high, w[v, 0], dims, preferred_element_type=F32)
            + lax.dot_general(high, w[v, 1], dims, preferred_element_type=F32)
            + lax.dot_general(low, w[v, 0], dims, preferred_element_type=F32)
        )
        for g in range(8):
            t = 4 * g + v
            part = split(y[g * RHS : (g + 1) * RHS, : 2 * LANE])
            for k in (0, 1):
                terms[k, :, 2 * t * LANE : (2 * t + 2) * LANE] = part[k]
        rest = y[:, 2 * LANE :] if rest is None else rest + y[:, 2 * LANE :]
    for g in range(8):
        part = split(rest[g * RHS : (g + 1) * RHS])
        for k in (0, 1):
            terms[k, :, (EL + g) * LANE : (EL + g + 1) * LANE] = part[k]

    def body(step, carry):
        at = lanes(step, 1024)
        idx = epos[rows8(step), :]
        mask_rows(left, 0, (terms[0, :, at], terms[1, :, at]), high_bf(idx), H_EDGE)
        accumulate(acc, step, left, idx)
        return carry

    lax.fori_loop(0, E_TILES // 8, body, 0)
    for h in range(H_EDGE):
        if h < H_OWN:
            ref, at = own, h
        elif h < H_OWN + H_RIM:
            ref, at = low_out, h - H_OWN
        else:
            ref, at = high_out, h - H_OWN - H_RIM
        ref[:, at * WIDE : (at + 1) * WIDE] = acc[h * RHS : (h + 1) * RHS, :]


VM = pl.BlockSpec(memory_space=pltpu.VMEM)


def call(kernel, name, outs, scratch, *args):
    return pl.pallas_call(
        kernel,
        out_shape=[jax.ShapeDtypeStruct(s, t) for s, t in outs],
        in_specs=[VM] * len(args),
        out_specs=[VM] * len(outs),
        scratch_shapes=[pltpu.VMEM(s, t) for s, t in scratch],
        compiler_params=pltpu.CompilerParams(vmem_limit_bytes=40 << 20),
        name=name,
    )(*args)


def exchange(x):
    return lax.all_to_all(x, "dev", split_axis=0, concat_axis=0, tiled=True)


def per_device(
    residual_edges,
    pi_block,
    stiff_block,
    mass_block,
    permittivity,
    curl_coef,
    edge_map,
    local_map,
    node_owner,
    node_slot,
):
    axes = ("grp", "dev")
    size = lax.axis_size(axes)
    up = [(i, i + 1) for i in range(size - 1)]
    down = [(i + 1, i) for i in range(size - 1)]
    before = lax.ppermute(residual_edges[:, E_LOC - RIM_W :], axes, up)
    after = lax.ppermute(residual_edges[:, :RIM_W], axes, down)
    em = edge_map.T
    em = jnp.concatenate([em[:, :LANE], em[:, LANE:].reshape(8, LANE)], axis=0)
    lm = local_map.T.reshape(N_TILES, LANE)
    curl = curl_coef.reshape(1, EL)
    epos, pos, slot_rows, ev_own = call(
        prep_kernel,
        "index_prep",
        [((E_TILES, LANE), I32), ((N_TILES, LANE), I32), ((PEERS, CAP), F32), ((RHS, E_TILES * LANE), F32)],
        [
            ((H_OWN * RHS, 2 * WIDE), BF),
            ((U_LOC // LANE * PEERS, LANE), BF),
            ((U_LOC // LANE, LANE), I32),
            ((U_LOC // LANE, LANE), I32),
        ],
        residual_edges,
        em,
        lm,
        node_owner.reshape(U_LOC // LANE, LANE),
        node_slot.reshape(U_LOC // LANE, LANE),
    )
    (packed,) = call(
        restrict_kernel,
        "restrict",
        [((PEERS, SENT, CAP), F32)],
        [
            ((2 * H_RIM * RHS, 2 * WIDE), BF),
            ((RHS, E_TILES * LANE), F32),
            ((4, 2, 384, 384), BF),
            ((8, LANE), F32),
            ((8, ELN), F32),
            ((2, ROWS, ELN), BF),
            ((3, ELN), F32),
            ((H_POS * ROWS + 48, 2048), BF),
            ((H_POS * ROWS + 48, WIDE), F32),
        ],
        ev_own, before, after, epos, pos, slot_rows, pi_block, stiff_block, mass_block, permittivity, curl,
    )
    wanted, rhs, floor, slots = call(
        first_kernel,
        "first_iter",
        [
            ((PEERS, ROWS, CAP), F32),
            ((H_NODE, ROWS, WIDE), F32),
            ((H_NODE, 3, WIDE), F32),
            ((PEERS, CAP), I32),
        ],
        [
            ((H_NODE * ROWS, 2 * WIDE), BF),
            ((H_NODE * ROWS + 48, 2048), BF),
            ((H_NODE * ROWS + 48, WIDE), F32),
        ],
        exchange(packed),
    )
    (applied,) = call(
        apply_kernel,
        "operator",
        [((PEERS, ROWS, CAP), F32)],
        [
            ((H_POS * ROWS, 2 * WIDE), BF),
            ((2, LANE, 2 * LANE), BF),
            ((8, LANE), F32),
            ((8, ELN), F32),
            ((H_POS * ROWS, 2048), BF),
            ((H_POS * ROWS, WIDE), F32),
        ],
        exchange(wanted), pos, stiff_block, mass_block, permittivity, curl,
    )
    (wanted,) = call(
        second_kernel,
        "second_iter",
        [((PEERS, ROWS, CAP), F32)],
        [
            ((H_NODE * ROWS, 2 * WIDE), BF),
            ((H_NODE * ROWS, 2048), BF),
            ((H_NODE * ROWS, WIDE), F32),
        ],
        exchange(applied), rhs, floor, slots,
    )
    own, low_out, high_out = call(
        prolong_kernel,
        "prolong",
        [((RHS, E_LOC), F32), ((RHS, RIM_W), F32), ((RHS, RIM_W), F32)],
        [
            ((H_POS * ROWS, 2 * WIDE), BF),
            ((4, 2, 384, 384), BF),
            ((ROWS, ELN), F32),
            ((2, RHS, E_TILES * LANE), BF),
            ((H_EDGE * RHS, 2048), BF),
            ((H_EDGE * RHS, WIDE), F32),
        ],
        exchange(wanted), pos, epos, pi_block,
    )
    from_before = lax.ppermute(high_out, axes, up)
    from_after = lax.ppermute(low_out, axes, down)
    own = own.at[:, :RIM_W].add(from_before)
    return own.at[:, E_LOC - RIM_W :].add(from_after)


def solution(mesh):
    in_specs = (
        P(None, ("grp", "dev")),
        P(),
        P(),
        P(),
        P(None, ("grp", "dev")),
        P(("grp", "dev")),
        P(None, ("grp", "dev")),
        P(None, ("grp", "dev")),
        P(("grp", "dev")),
        P(("grp", "dev")),
    )
    out_specs = P(None, ("grp", "dev"))
    return jax.shard_map(
        per_device, mesh=mesh, in_specs=in_specs, out_specs=out_specs, check_vma=False
    )
```

```python
import jax
import jax.numpy as jnp
from jax import lax
from jax.experimental import pallas as pl
from jax.experimental.pallas import tpu as pltpu
from jax.sharding import PartitionSpec as P

RHS = 16
ED = 144
NN = 64
EL = 64
E_LOC = 5376
RIM = 672
U_LOC = 2048
PEERS = 32
CAP = 128
ROWS = 3 * RHS
PAIR = 2 * ROWS
SENT = ROWS + 4
SLOTS = PEERS * CAP
ELN = NN * EL
LANE = 128
WIDE = 256
RIM_W = 768
H_OWN = E_LOC // WIDE
H_RIM = RIM_W // WIDE
H_EDGE = H_OWN + 2 * H_RIM
H_POS = U_LOC // WIDE
H_NODE = 7
E_TILES = 72
N_TILES = ELN // LANE
BF = jnp.bfloat16
F32 = jnp.float32
I32 = jnp.int32

CHEB_LOW = 0.3
CHEB_HIGH = 2.0


def cheb_factors():
    center = 0.5 * (CHEB_HIGH + CHEB_LOW)
    half_width = 0.5 * (CHEB_HIGH - CHEB_LOW)
    sigma_ratio = center / half_width
    rho_first = 1.0 / sigma_ratio
    rho_second = 1.0 / (2.0 * sigma_ratio - rho_first)
    return (1.0 / center, 1.0 + rho_second * rho_first, 2.0 * rho_second / half_width)


def split(x):
    high = x.astype(BF)
    return high, (x - high.astype(F32)).astype(BF)


def stack(x):
    return jnp.concatenate([x, x - x.astype(BF).astype(F32)], axis=0).astype(BF)


def iota(shape, dim):
    return lax.broadcasted_iota(I32, shape, dim)


def spread(index_rows, height):
    return jnp.concatenate(
        [jnp.broadcast_to(index_rows[i : i + 1], (height, LANE)) for i in range(index_rows.shape[0])],
        axis=1,
    )


def one_hot_low(index_rows):
    low = spread(index_rows & (WIDE - 1), WIDE)
    return jnp.where(low == iota(low.shape, 0), 1.0, 0.0).astype(BF)


def gather_tile(table, index_rows, rows, count):
    hot = one_hot_low(index_rows)
    found = jnp.dot(table, jnp.concatenate([hot, hot], axis=0), preferred_element_type=F32)
    high = spread(index_rows >> 8, rows)
    out = found[:rows]
    for h in range(1, count):
        out = jnp.where(high == h, found[h * rows : (h + 1) * rows], out)
    return out


def fill_table(table, source, rows, count):
    each = 1 if rows % 16 == 0 else 2
    for h in range(0, count, each):
        high, low = split(jnp.concatenate([source(h + i) for i in range(each)], axis=0))
        table[h * rows : (h + each) * rows, :WIDE] = high
        table[h * rows : (h + each) * rows, WIDE:] = low


def mask_rows(left, x, index_rows, first, count):
    rows, width = x.shape
    high = spread(index_rows >> 8, 1).astype(F32).astype(BF)
    high = jnp.broadcast_to(high, (rows, width))
    for h in range(count):
        left[h * rows : (h + 1) * rows, :] = jnp.where(high == float(first + h), x, jnp.zeros_like(x))


def mask_diag(left, base, diag, index_rows):
    width = diag[0].shape[1]
    here = spread(index_rows >> 8, 16) == iota((16, width), 0)
    for c in range(3):
        left[base + c * 32 : base + (c + 1) * 32, :] = stack(
            jnp.where(here, jnp.broadcast_to(diag[c], (16, width)), 0.0)
        )


def accumulate(acc, step, left, index_rows):
    part = lax.dot_general(
        left[...], one_hot_low(index_rows), (((1,), (1,)), ((), ())), preferred_element_type=F32
    )

    @pl.when(step == 0)
    def _():
        acc[...] = part

    @pl.when(step > 0)
    def _():
        acc[...] += part


def summed(acc, h, rows, at=slice(None)):
    base = h * 2 * rows
    return acc[base : base + rows, at] + acc[base + rows : base + 2 * rows, at]


def diag_summed(acc, base, c, h, at=slice(None)):
    row = base + c * 32 + h
    return acc[row : row + 1, at] + acc[row + 16 : row + 17, at]


def rows_of(step, count):
    return pl.ds(pl.multiple_of(step * count, count), count)


def lanes(step, width):
    return pl.ds(pl.multiple_of(step * width, width), width)


def prep_kernel(
    res, em, lm, owner, slot, epos_out, pos_out, slot_out, start_out, low_out, high_out, hots, rank_s, pos_s, tr
):
    low_out[...] = res[:, :RIM_W]
    high_out[...] = res[:, E_LOC - RIM_W :]
    tr[:, : ED - LANE] = em[:, LANE:]
    rest = [tr[pl.ds(i, 8, stride=8), :][:, : ED - LANE] for i in range(8)]
    m = jnp.concatenate([em[:, :LANE], jnp.concatenate(rest, axis=1)], axis=0)
    epos_out[...] = jnp.where(
        m < RIM,
        m + (E_LOC + RIM_W - RIM),
        jnp.where(m < RIM + E_LOC, m - RIM, m - (RIM + E_LOC) + E_LOC + RIM_W),
    )
    chunks = U_LOC // LANE
    for t in range(chunks):
        o = jnp.broadcast_to(owner[t : t + 1, :], (PEERS, LANE))
        hots[t * PEERS : (t + 1) * PEERS, :] = jnp.where(o == iota((PEERS, LANE), 0), 1.0, 0.0).astype(BF)
    before = jnp.where(iota((LANE, LANE), 0) < iota((LANE, LANE), 1), 1.0, 0.0)
    tri = jnp.concatenate([before, jnp.ones((LANE, LANE), F32)], axis=1).astype(BF)
    ranks = jnp.dot(hots[...], tri, preferred_element_type=F32)
    counts = ranks[:PEERS, LANE:]
    for t in range(1, chunks):
        counts = counts + ranks[t * PEERS : (t + 1) * PEERS, LANE:]
    below = jnp.where(iota((PEERS, PEERS), 1) < iota((PEERS, PEERS), 0), 1.0, 0.0).astype(BF)
    starts = jnp.dot(below, counts.astype(BF), preferred_element_type=F32)
    start_out[...] = starts.astype(I32)
    base = jnp.zeros((PEERS, LANE), F32)
    for t in range(chunks):
        hot = hots[t * PEERS : (t + 1) * PEERS, :].astype(F32)
        here = ranks[t * PEERS : (t + 1) * PEERS]
        rank = here[:, :LANE] + base
        base = base + here[:, LANE:]
        rank_s[t : t + 1, :] = jnp.sum(hot * rank, axis=0, keepdims=True).astype(I32)
        pos_s[t : t + 1, :] = jnp.sum(hot * (rank + starts), axis=0, keepdims=True).astype(I32)
    left = []
    right = []
    for t in range(chunks):
        hot = hots[t * PEERS : (t + 1) * PEERS, :].astype(F32)
        s = slot[t : t + 1, :] + 1
        left.append(
            jnp.concatenate([hot * (s >> 6).astype(F32), hot * (s & 63).astype(F32)], axis=0).astype(BF)
        )
        r = jnp.broadcast_to(rank_s[t : t + 1, :], (LANE, LANE))
        right.append(jnp.where(r == iota((LANE, LANE), 0), 1.0, 0.0).astype(BF))
    packed = lax.dot_general(
        jnp.concatenate(left, axis=1),
        jnp.concatenate(right, axis=1),
        (((1,), (1,)), ((), ())),
        preferred_element_type=F32,
    )
    slot_out[...] = packed[:PEERS] * 64.0 + packed[PEERS:] - 1.0
    tr[:, :NN] = lm[...].T
    idx = jnp.concatenate([tr[pl.ds(i, N_TILES, stride=2), :][:, :NN] for i in (0, 1)], axis=1)
    high, low = idx >> 7, idx & (LANE - 1)
    pos = jnp.zeros((N_TILES, LANE), I32)
    for t in range(chunks):
        row = jnp.broadcast_to(pos_s[t : t + 1, :], (N_TILES, LANE))
        pos = jnp.where(high == t, jnp.take_along_axis(row, low, axis=1), pos)
    pos_out[...] = pos


def own_edges_kernel(res, epos, ev_out, table):
    fill_table(table, lambda h: res[:, h * WIDE : (h + 1) * WIDE], RHS, H_OWN)

    def body(step, carry):
        ev_out[:, lanes(step, 1024)] = gather_tile(table[...], epos[rows_of(step, 8), :], RHS, H_OWN)
        return carry

    lax.fori_loop(0, E_TILES // 8, body, 0)


def fill_pi(w, pi):
    zero = jnp.zeros((384, 384), BF)
    for v in range(4):
        for k in (0, 1):
            w[v, k] = zero
    for c in range(3):
        part = split(pi[:, c * NN : (c + 1) * NN])
        for k in (0, 1):
            for e2 in (0, 1):
                cols = slice(c * LANE + e2 * NN, c * LANE + (e2 + 1) * NN)
                for v in range(4):
                    w[v, k, e2 * LANE : (e2 + 1) * LANE, cols] = part[k][:LANE]
                    at = 2 * LANE + (2 * v + e2) * 16
                    w[v, k, at : at + 16, cols] = part[k][LANE:]


def fill_coefs(coef, wide, perm, curl):
    coef[...] = jnp.zeros((8, LANE), F32)
    coef[0:6, 0:EL] = perm[...]
    coef[6:7, 0:EL] = curl[...]
    c = coef[...]
    second = jnp.where(iota((8, LANE), 1) >= NN, 1, 0)
    for t in range(N_TILES):
        wide[:, t * LANE : (t + 1) * LANE] = jnp.take_along_axis(c, second + 2 * t, axis=1)


NODE_STEP = 2048
NODE_ROWS = NODE_STEP // LANE
EDGE_STEP = 3072
EDGE_ROWS = EDGE_STEP // LANE


def from_acc(compact, acc):
    compact[:, U_LOC:] = jnp.zeros((compact.shape[0], 2 * LANE), F32)
    for h in range(H_POS):
        compact[0:ROWS, h * WIDE : (h + 1) * WIDE] = summed(acc, h, ROWS)


def expand(out, compact, starts, rows):
    lane = iota((rows, LANE), 1)
    for p in range(PEERS):
        start = starts[p, 0]
        shift = start & (LANE - 1)
        base = start - shift
        back = lax.rem(LANE - shift, LANE)
        one = pltpu.roll(compact[0:rows, lanes(base // LANE, LANE)], back, 1)
        two = pltpu.roll(compact[0:rows, lanes(base // LANE + 1, LANE)], back, 1)
        out[p] = jnp.where(lane < LANE - shift, one, two)[: out.shape[1]]


def shrink(compact, arrived, starts):
    lane = iota((ROWS, LANE), 1)
    for p in range(PEERS):
        start = starts[p, 0]
        shift = start & (LANE - 1)
        base = (start - shift) // LANE
        block = pltpu.roll(arrived[p], shift, 1)
        at = lanes(base, LANE)
        compact[:, at] = jnp.where(lane >= shift, block, compact[:, at])
        compact[:, lanes(base + 1, LANE)] = block


def restrict_kernel(
    ev_own, before, after, epos, pos, slots, pi, stiff, mass, perm, curl, starts,
    out, table, ev, w, coef, wide, xs, diag, left, acc, compact,
):
    def rim(h):
        ref = before if h < H_RIM else after
        at = h % H_RIM * WIDE
        return ref[:, at : at + WIDE]

    fill_table(table, rim, RHS, 2 * H_RIM)

    def rim_body(step, carry):
        idx = epos[rows_of(step, 8), :] - E_LOC
        found = gather_tile(table[...], idx, RHS, 2 * H_RIM)
        at = lanes(step, 1024)
        ev[:, at] = jnp.where(spread(idx, RHS) >= 0, found, ev_own[:, at])
        return carry

    lax.fori_loop(0, E_TILES // 8, rim_body, 0)
    fill_pi(w, pi)
    for v in range(4):
        blocks = []
        for g in range(8):
            t = 4 * g + v
            blocks.append(
                jnp.concatenate(
                    [ev[:, 2 * t * LANE : (2 * t + 2) * LANE], ev[:, (EL + g) * LANE : (EL + g + 1) * LANE]],
                    axis=1,
                )
            )
        high, low = split(jnp.concatenate(blocks, axis=0))
        y = (
            jnp.dot(high, w[v, 0], preferred_element_type=F32)
            + jnp.dot(high, w[v, 1], preferred_element_type=F32)
            + jnp.dot(low, w[v, 0], preferred_element_type=F32)
        )
        for g in range(8):
            t = 4 * g + v
            xs[:, t * LANE : (t + 1) * LANE] = stack(
                jnp.concatenate(
                    [y[g * RHS : (g + 1) * RHS, c * LANE : (c + 1) * LANE] for c in range(3)], axis=0
                )
            )
    fill_coefs(coef, wide, perm, curl)
    eye = iota((NN, NN), 0) == iota((NN, NN), 1)

    def diagonal(ref):
        d = jnp.sum(jnp.where(eye, ref[...], 0.0), axis=0, keepdims=True)
        return jnp.concatenate([d, d], axis=1)

    sd, md = diagonal(stiff), diagonal(mass)
    for t in range(N_TILES):
        at = slice(t * LANE, (t + 1) * LANE)
        diag[:, at] = wide[6:7, at] * sd + md * wide[0:3, at]

    def body(step, carry):
        at = lanes(step, NODE_STEP)
        idx = pos[rows_of(step, NODE_ROWS), :]
        mask_rows(left, xs[:, at], idx, 0, H_POS)
        mask_diag(left, H_POS * PAIR, [diag[c : c + 1, at] for c in range(3)], idx)
        accumulate(acc, step, left, idx)
        return carry

    lax.fori_loop(0, ELN // NODE_STEP, body, 0)
    from_acc(compact, acc)
    for h in range(H_POS):
        for c in range(3):
            compact[ROWS + c : ROWS + c + 1, h * WIDE : (h + 1) * WIDE] = diag_summed(
                acc, H_POS * PAIR, c, h
            )
    expand(out, compact, starts, SENT + 4)
    for p in range(PEERS):
        out[p, SENT - 1 : SENT, :] = slots[p : p + 1, :]


def collect(arrived, slots, left, acc, with_diag):
    def body(step, carry):
        idx = slots[rows_of(step, NODE_ROWS), :]
        block = arrived[rows_of(step, NODE_ROWS)]
        x = jnp.concatenate([block[i, 0:ROWS] for i in range(NODE_ROWS)], axis=1)
        mask_rows(left, stack(x), idx, 0, H_NODE)
        if with_diag:
            diag = [
                jnp.concatenate([block[i, ROWS + c : ROWS + c + 1] for i in range(NODE_ROWS)], axis=1)
                for c in range(3)
            ]
            mask_diag(left, H_NODE * PAIR, diag, idx)
        accumulate(acc, step, left, idx)
        return carry

    lax.fori_loop(0, PEERS // NODE_ROWS, body, 0)


def serve(out, table, slots):
    def body(step, carry):
        found = gather_tile(table[...], slots[rows_of(step, 8), :], ROWS, H_NODE)
        for i in range(8):
            out[step * 8 + i] = found[:, i * LANE : (i + 1) * LANE]
        return carry

    lax.fori_loop(0, PEERS // 8, body, 0)


def first_values(rhs, floor):
    first = cheb_factors()[0]

    def value(h):
        if h >= H_NODE:
            return jnp.zeros((ROWS, WIDE), F32)
        return jnp.concatenate(
            [
                first * rhs[h, c * RHS : (c + 1) * RHS, :] / floor[h, c : c + 1, :]
                for c in range(3)
            ],
            axis=0,
        )

    return value


def first_kernel(arrived, out, rhs_out, floor_out, slot_out, table, left, acc):
    for p in range(PEERS):
        slot_out[p : p + 1, :] = arrived[p, SENT - 1 : SENT, :].astype(I32)
    collect(arrived, slot_out, left, acc, True)
    for h in range(H_NODE):
        rhs_out[h] = summed(acc, h, ROWS)
        for c in range(3):
            floor_out[h, c : c + 1, :] = jnp.maximum(diag_summed(acc, H_NODE * PAIR, c, h), 1.0)
    fill_table(table, first_values(rhs_out, floor_out), ROWS, H_NODE + 1)
    serve(out, table, slot_out)


def second_kernel(arrived, rhs, floor, slots, out, table, left, acc):
    first, keep, step = cheb_factors()
    collect(arrived, slots, left, acc, False)

    def value(h):
        if h >= H_NODE:
            return jnp.zeros((ROWS, WIDE), F32)
        applied = summed(acc, h, ROWS)
        parts = []
        for c in range(3):
            at = slice(c * RHS, (c + 1) * RHS)
            part = rhs[h, at, :]
            low = floor[h, c : c + 1, :]
            parts.append(keep * (first * part / low) + step * (part - applied[at]) / low)
        return jnp.concatenate(parts, axis=0)

    fill_table(table, value, ROWS, H_NODE + 1)
    serve(out, table, slots)


def touched_table(table, compact, arrived, starts):
    shrink(compact, arrived, starts)
    fill_table(table, lambda h: compact[:, h * WIDE : (h + 1) * WIDE], ROWS, H_POS)


def apply_kernel(
    arrived, pos, stiff, mass, perm, curl, starts, out, table, op, coef, wide, xs, left, acc, compact
):
    touched_table(table, compact, arrived, starts)
    fill_coefs(coef, wide, perm, curl)
    op[...] = jnp.zeros((2, LANE, 2 * LANE), BF)
    for m, ref in enumerate((stiff, mass)):
        part = split(ref[...].T)
        for k in (0, 1):
            for e2 in (0, 1):
                at = slice(m * LANE + e2 * NN, m * LANE + (e2 + 1) * NN)
                op[k, e2 * NN : (e2 + 1) * NN, at] = part[k]

    def element_body(step, carry):
        values = gather_tile(table[...], pos[rows_of(step, 8), :], ROWS, H_POS)
        high, low = split(
            jnp.concatenate([values[:, i * LANE : (i + 1) * LANE] for i in range(8)], axis=0)
        )
        y = (
            jnp.dot(high, op[0], preferred_element_type=F32)
            + jnp.dot(high, op[1], preferred_element_type=F32)
            + jnp.dot(low, op[0], preferred_element_type=F32)
        )
        cols = wide[:, lanes(step, 1024)]
        tensor = ((0, 3, 4), (3, 1, 5), (4, 5, 2))
        tiles = []
        for i in range(8):
            k = cols[:, i * LANE : (i + 1) * LANE]
            rows = [slice(i * ROWS + c * RHS, i * ROWS + (c + 1) * RHS) for c in range(3)]
            s = [y[r, :LANE] for r in rows]
            m = [y[r, LANE:] for r in rows]
            tiles.append(
                jnp.concatenate(
                    [
                        k[6:7] * s[c]
                        + k[tensor[c][0]][None] * m[0]
                        + k[tensor[c][1]][None] * m[1]
                        + k[tensor[c][2]][None] * m[2]
                        for c in range(3)
                    ],
                    axis=0,
                )
            )
        xs[:, lanes(step, 1024)] = stack(jnp.concatenate(tiles, axis=1))
        return carry

    lax.fori_loop(0, ELN // 1024, element_body, 0)

    def body(step, carry):
        idx = pos[rows_of(step, NODE_ROWS), :]
        mask_rows(left, xs[:, lanes(step, NODE_STEP)], idx, 0, H_POS)
        accumulate(acc, step, left, idx)
        return carry

    lax.fori_loop(0, ELN // NODE_STEP, body, 0)
    from_acc(compact, acc)
    expand(out, compact, starts, ROWS)


def edge_terms(arrived, pos, pi, starts, terms, table, w, values, compact):
    touched_table(table, compact, arrived, starts)
    fill_pi(w, pi)

    def gather_body(step, carry):
        values[:, lanes(step, 1024)] = gather_tile(table[...], pos[rows_of(step, 8), :], ROWS, H_POS)
        return carry

    lax.fori_loop(0, ELN // 1024, gather_body, 0)
    dims = (((1,), (1,)), ((), ()))
    rest = None
    for v in range(4):
        blocks = []
        for g in range(8):
            at = slice((4 * g + v) * LANE, (4 * g + v + 1) * LANE)
            blocks.append(
                jnp.concatenate([values[c * RHS : (c + 1) * RHS, at] for c in range(3)], axis=1)
            )
        high, low = split(jnp.concatenate(blocks, axis=0))
        y = (
            lax.dot_general(high, w[v, 0], dims, preferred_element_type=F32)
            + lax.dot_general(high, w[v, 1], dims, preferred_element_type=F32)
            + lax.dot_general(low, w[v, 0], dims, preferred_element_type=F32)
        )
        for g in range(8):
            t = 4 * g + v
            terms[:, 2 * t * LANE : (2 * t + 2) * LANE] = stack(y[g * RHS : (g + 1) * RHS, : 2 * LANE])
        rest = y[:, 2 * LANE :] if rest is None else rest + y[:, 2 * LANE :]
    for g in range(8):
        terms[:, (EL + g) * LANE : (EL + g + 1) * LANE] = stack(rest[g * RHS : (g + 1) * RHS])


def edge_scatter(terms, epos, left, acc, first, count):
    def body(step, carry):
        idx = epos[rows_of(step, EDGE_ROWS), :]
        mask_rows(left, terms[:, lanes(step, EDGE_STEP)], idx, first, count)
        accumulate(acc, step, left, idx)
        return carry

    lax.fori_loop(0, E_TILES // EDGE_ROWS, body, 0)


def prolong_rim_kernel(
    arrived, pos, epos, pi, starts, terms, low_out, high_out, table, w, values, compact, left, acc
):
    edge_terms(arrived, pos, pi, starts, terms, table, w, values, compact)
    edge_scatter(terms, epos, left, acc, H_OWN, 2 * H_RIM)
    for h in range(H_RIM):
        at = slice(h * WIDE, (h + 1) * WIDE)
        low_out[:, at] = summed(acc, h, RHS)
        high_out[:, at] = summed(acc, H_RIM + h, RHS)


def prolong_own_kernel(terms, epos, own, left, acc):
    edge_scatter(terms, epos, left, acc, 0, H_OWN)
    for h in range(H_OWN):
        own[:, h * WIDE : (h + 1) * WIDE] = summed(acc, h, RHS)


def finish_kernel(own, before, after, out):
    out[...] = own[...]
    out[:, :RIM_W] += before[...]
    out[:, E_LOC - RIM_W :] += after[...]


VM = pl.BlockSpec(memory_space=pltpu.VMEM)


SM = pl.BlockSpec(memory_space=pltpu.SMEM)


def call(kernel, name, micros, outs, scratch, *args, scalars=0):
    return pl.pallas_call(
        kernel,
        out_shape=[jax.ShapeDtypeStruct(s, t) for s, t in outs],
        in_specs=[VM] * (len(args) - scalars) + [SM] * scalars,
        out_specs=[VM] * len(outs),
        scratch_shapes=[pltpu.VMEM(s, t) for s, t in scratch],
        compiler_params=pltpu.CompilerParams(vmem_limit_bytes=40 << 20),
        cost_estimate=pl.CostEstimate(flops=0, bytes_accessed=micros * 3600000, transcendentals=0),
        name=name,
    )(*args)


def exchange(x):
    return lax.all_to_all(x, "dev", split_axis=0, concat_axis=0, tiled=True)


def per_device(
    residual_edges,
    pi_block,
    stiff_block,
    mass_block,
    permittivity,
    curl_coef,
    edge_map,
    local_map,
    node_owner,
    node_slot,
):
    axes = ("grp", "dev")
    size = lax.axis_size(axes)
    up = [(i, i + 1) for i in range(size - 1)]
    down = [(i + 1, i) for i in range(size - 1)]
    curl = curl_coef.reshape(1, EL)
    chunks = U_LOC // LANE
    rim = ((RHS, RIM_W), F32)
    epos, pos, slot_rows, starts, low, high = call(
        prep_kernel,
        "index_prep",
        2,
        [
            ((E_TILES, LANE), I32),
            ((N_TILES, LANE), I32),
            ((PEERS, CAP), F32),
            ((PEERS, LANE), I32),
            rim,
            rim,
        ],
        [((chunks * PEERS, LANE), BF), ((chunks, LANE), I32), ((chunks, LANE), I32), ((EL, LANE), I32)],
        residual_edges,
        edge_map.T,
        local_map,
        node_owner.reshape(chunks, LANE),
        node_slot.reshape(chunks, LANE),
    )
    before = lax.ppermute(high, axes, up)
    after = lax.ppermute(low, axes, down)
    edge_rows = ((RHS, E_TILES * LANE), F32)
    (ev_own,) = call(
        own_edges_kernel, "own_edges", 4, [edge_rows], [((H_OWN * RHS, 2 * WIDE), BF)], residual_edges, epos
    )
    pi_scratch = ((4, 2, 384, 384), BF)
    coefs = [((8, LANE), F32), ((8, ELN), F32)]
    served = ((PEERS, ROWS, CAP), F32)
    compact = ((ROWS, U_LOC + 2 * LANE), F32)
    (packed,) = call(
        restrict_kernel,
        "restrict",
        6,
        [((PEERS, SENT, CAP), F32)],
        [
            ((2 * H_RIM * RHS, 2 * WIDE), BF),
            edge_rows,
            pi_scratch,
            *coefs,
            ((PAIR, ELN), BF),
            ((3, ELN), F32),
            ((H_POS * PAIR + 96, NODE_STEP), BF),
            ((H_POS * PAIR + 96, WIDE), F32),
            ((SENT + 4, U_LOC + 2 * LANE), F32),
        ],
        ev_own, before, after, epos, pos, slot_rows, pi_block, stiff_block, mass_block, permittivity, curl, starts,
        scalars=1,
    )
    table = (((H_NODE + 1) * ROWS, 2 * WIDE), BF)
    wanted, rhs, floor, slots = call(
        first_kernel,
        "first_iter",
        5,
        [served, ((H_NODE, ROWS, WIDE), F32), ((H_NODE, 3, WIDE), F32), ((PEERS, CAP), I32)],
        [table, ((H_NODE * PAIR + 96, NODE_STEP), BF), ((H_NODE * PAIR + 96, WIDE), F32)],
        exchange(packed),
    )
    position_table = ((H_POS * ROWS, 2 * WIDE), BF)
    (applied,) = call(
        apply_kernel,
        "operator",
        8,
        [served],
        [
            position_table,
            ((2, LANE, 2 * LANE), BF),
            *coefs,
            ((PAIR, ELN), BF),
            ((H_POS * PAIR, NODE_STEP), BF),
            ((H_POS * PAIR, WIDE), F32),
            compact,
        ],
        exchange(wanted), pos, stiff_block, mass_block, permittivity, curl, starts,
        scalars=1,
    )
    (wanted,) = call(
        second_kernel,
        "second_iter",
        5,
        [served],
        [table, ((H_NODE * PAIR, NODE_STEP), BF), ((H_NODE * PAIR, WIDE), F32)],
        exchange(applied), rhs, floor, slots,
    )
    terms, low, high = call(
        prolong_rim_kernel,
        "prolong_rim",
        6,
        [((2 * RHS, E_TILES * LANE), BF), rim, rim],
        [
            position_table,
            pi_scratch,
            ((ROWS, ELN), F32),
            compact,
            ((2 * H_RIM * 2 * RHS, EDGE_STEP), BF),
            ((2 * H_RIM * 2 * RHS, WIDE), F32),
        ],
        exchange(wanted), pos, epos, pi_block, starts,
        scalars=1,
    )
    from_before = lax.ppermute(high, axes, up)
    from_after = lax.ppermute(low, axes, down)
    (own,) = call(
        prolong_own_kernel,
        "prolong_own",
        5,
        [((RHS, E_LOC), F32)],
        [((H_OWN * 2 * RHS, EDGE_STEP), BF), ((H_OWN * 2 * RHS, WIDE), F32)],
        terms, epos,
    )
    (out,) = call(finish_kernel, "finish", 1, [((RHS, E_LOC), F32)], [], own, from_before, from_after)
    return out


def solution(mesh):
    in_specs = (
        P(None, ("grp", "dev")),
        P(),
        P(),
        P(),
        P(None, ("grp", "dev")),
        P(("grp", "dev")),
        P(None, ("grp", "dev")),
        P(None, ("grp", "dev")),
        P(("grp", "dev")),
        P(("grp", "dev")),
    )
    out_specs = P(None, ("grp", "dev"))
    return jax.shard_map(
        per_device, mesh=mesh, in_specs=in_specs, out_specs=out_specs, check_vma=False
    )
```

```python
import jax
import jax.numpy as jnp
from jax import lax
from jax.experimental import pallas as pl
from jax.experimental.pallas import tpu as pltpu
from jax.sharding import PartitionSpec as P

RHS = 16
ED = 144
NN = 64
EL = 64
E_LOC = 5376
RIM = 672
U_LOC = 2048
PEERS = 32
CAP = 128
ROWS = 3 * RHS
PAIR = 2 * ROWS
SENT = ROWS + 4
SLOTS = PEERS * CAP
ELN = NN * EL
LANE = 128
WIDE = 256
RIM_W = 768
H_OWN = E_LOC // WIDE
H_RIM = RIM_W // WIDE
H_EDGE = H_OWN + 2 * H_RIM
H_POS = U_LOC // WIDE
H_NODE = 7
TAIL = 4
TAIL_H = TAIL // 2
GATHER_STEP = 512
GATHER_ROWS = GATHER_STEP // LANE
E_TILES = 72
N_TILES = ELN // LANE
BF = jnp.bfloat16
F32 = jnp.float32
I32 = jnp.int32

CHEB_LOW = 0.3
CHEB_HIGH = 2.0


def cheb_factors():
    center = 0.5 * (CHEB_HIGH + CHEB_LOW)
    half_width = 0.5 * (CHEB_HIGH - CHEB_LOW)
    sigma_ratio = center / half_width
    rho_first = 1.0 / sigma_ratio
    rho_second = 1.0 / (2.0 * sigma_ratio - rho_first)
    return (1.0 / center, 1.0 + rho_second * rho_first, 2.0 * rho_second / half_width)


def split(x):
    high = x.astype(BF)
    return high, (x - high.astype(F32)).astype(BF)


def stack(x):
    return jnp.concatenate([x, x - x.astype(BF).astype(F32)], axis=0).astype(BF)


def iota(shape, dim):
    return lax.broadcasted_iota(I32, shape, dim)


def spread(index_rows, height):
    return jnp.concatenate(
        [jnp.broadcast_to(index_rows[i : i + 1], (height, LANE)) for i in range(index_rows.shape[0])],
        axis=1,
    )


def low_part(index_rows):
    return spread(index_rows & (WIDE - 1), 1).astype(F32).astype(BF)


def one_hot_low(index_rows):
    low = low_part(index_rows)
    shape = (WIDE, low.shape[1])
    here = jnp.broadcast_to(low, shape) == iota(shape, 0).astype(F32).astype(BF)
    return jnp.where(here, jnp.ones(shape, BF), jnp.zeros(shape, BF))


def gather_tile(table, index_rows, rows, count, tail):
    found = jnp.dot(table, one_hot_low(index_rows), preferred_element_type=F32)
    high = spread(index_rows >> 8, 2 * rows)
    out = found[: 2 * rows]
    for h in range(1, count):
        out = jnp.where(high == h, found[h * 2 * rows : (h + 1) * 2 * rows], out)
    out = out[:rows] + out[rows:]
    tiles = []
    for i in range(index_rows.shape[0]):
        index = jnp.broadcast_to(index_rows[i : i + 1], (rows, LANE))
        part = out[:, i * LANE : (i + 1) * LANE]
        for k in range(TAIL):
            picked = jnp.take_along_axis(tail(k), index & (LANE - 1), axis=1)
            part = jnp.where((index >> 7) == 2 * count + k, picked, part)
        tiles.append(part)
    return jnp.concatenate(tiles, axis=1)


def fill_table(table, source, rows, count):
    for h in range(count):
        table[h * 2 * rows : (h + 1) * 2 * rows, :] = stack(source(h))


def mask_rows(left, x, index_rows, first, count):
    rows, width = x.shape
    high = spread(index_rows >> 8, 1).astype(F32).astype(BF)
    high = jnp.broadcast_to(high, (rows, width))
    for h in range(count):
        left[h * rows : (h + 1) * rows, :] = jnp.where(high == float(first + h), x, jnp.zeros_like(x))


def mask_diag(left, base, diag, index_rows):
    width = diag[0].shape[1]
    here = spread(index_rows >> 8, 16) == iota((16, width), 0)
    for c in range(3):
        left[base + c * 32 : base + (c + 1) * 32, :] = stack(
            jnp.where(here, jnp.broadcast_to(diag[c], (16, width)), 0.0)
        )


def accumulate(acc, step, left, index_rows):
    part = lax.dot_general(
        left[...], one_hot_low(index_rows), (((1,), (1,)), ((), ())), preferred_element_type=F32
    )
    acc[...] = part if step == 0 else acc[...] + part


def summed(acc, h, rows, at=slice(None)):
    base = h * 2 * rows
    return acc[base : base + rows, at] + acc[base + rows : base + 2 * rows, at]


def diag_summed(acc, base, c, h, at=slice(None)):
    row = base + c * 32 + h
    return acc[row : row + 1, at] + acc[row + 16 : row + 17, at]


def rows_of(step, count):
    return slice(step * count, (step + 1) * count)


def cols_of(step, width):
    return slice(step * width, (step + 1) * width)


def lanes(step, width):
    return pl.ds(pl.multiple_of(step * width, width), width)


def prep_kernel(
    res, em_in, lm_in, owner_in, slot_in,
    epos_out, pos_out, slot_out, start_out, low_out, high_out,
    em, lm, owner, slot, hots, rank_s, pos_s, tr, sems,
):
    moves = [
        (owner_in, owner),
        (em_in, em),
        (lm_in, lm),
        (slot_in, slot),
        (res.at[:, :RIM_W], low_out),
        (res.at[:, E_LOC - RIM_W :], high_out),
    ]
    moves = [pltpu.make_async_copy(a, b, sems.at[i]) for i, (a, b) in enumerate(moves)]
    for move in moves:
        move.start()
    for move in moves:
        move.wait()
    tr[:, : ED - LANE] = em[:, LANE:]
    rest = [tr[pl.ds(i, 8, stride=8), :][:, : ED - LANE] for i in range(8)]
    m = jnp.concatenate([em[:, :LANE], jnp.concatenate(rest, axis=1)], axis=0)
    epos_out[...] = jnp.where(
        m < RIM,
        m + (E_LOC + RIM_W - RIM),
        jnp.where(m < RIM + E_LOC, m - RIM, m - (RIM + E_LOC) + E_LOC + RIM_W),
    )
    chunks = U_LOC // LANE
    for t in range(chunks):
        o = jnp.broadcast_to(owner[t : t + 1, :], (PEERS, LANE))
        hots[t * PEERS : (t + 1) * PEERS, :] = jnp.where(o == iota((PEERS, LANE), 0), 1.0, 0.0).astype(BF)
    before = jnp.where(iota((LANE, LANE), 0) < iota((LANE, LANE), 1), 1.0, 0.0)
    tri = jnp.concatenate([before, jnp.ones((LANE, LANE), F32)], axis=1).astype(BF)
    ranks = jnp.dot(hots[...], tri, preferred_element_type=F32)
    counts = ranks[:PEERS, LANE:]
    for t in range(1, chunks):
        counts = counts + ranks[t * PEERS : (t + 1) * PEERS, LANE:]
    below = jnp.where(iota((PEERS, PEERS), 1) < iota((PEERS, PEERS), 0), 1.0, 0.0).astype(BF)
    starts = jnp.dot(below, counts.astype(BF), preferred_element_type=F32)
    start_out[...] = starts.astype(I32)
    base = jnp.zeros((PEERS, LANE), F32)
    for t in range(chunks):
        hot = hots[t * PEERS : (t + 1) * PEERS, :].astype(F32)
        here = ranks[t * PEERS : (t + 1) * PEERS]
        rank = here[:, :LANE] + base
        base = base + here[:, LANE:]
        rank_s[t : t + 1, :] = jnp.sum(hot * rank, axis=0, keepdims=True).astype(I32)
        pos_s[t : t + 1, :] = jnp.sum(hot * (rank + starts), axis=0, keepdims=True).astype(I32)
    left = []
    right = []
    for t in range(chunks):
        hot = hots[t * PEERS : (t + 1) * PEERS, :].astype(F32)
        s = slot[t : t + 1, :] + 1
        left.append(
            jnp.concatenate([hot * (s >> 6).astype(F32), hot * (s & 63).astype(F32)], axis=0).astype(BF)
        )
        r = jnp.broadcast_to(rank_s[t : t + 1, :], (LANE, LANE))
        right.append(jnp.where(r == iota((LANE, LANE), 0), 1.0, 0.0).astype(BF))
    packed = lax.dot_general(
        jnp.concatenate(left, axis=1),
        jnp.concatenate(right, axis=1),
        (((1,), (1,)), ((), ())),
        preferred_element_type=F32,
    )
    slot_out[...] = packed[:PEERS] * 64.0 + packed[PEERS:] - 1.0
    tr[:, :NN] = lm[...].T
    idx = jnp.concatenate([tr[pl.ds(i, N_TILES, stride=2), :][:, :NN] for i in (0, 1)], axis=1)
    high, low = idx >> 7, idx & (LANE - 1)
    pos = jnp.zeros((N_TILES, LANE), I32)
    for t in range(chunks):
        row = jnp.broadcast_to(pos_s[t : t + 1, :], (N_TILES, LANE))
        pos = jnp.where(high == t, jnp.take_along_axis(row, low, axis=1), pos)
    pos_out[...] = pos


def own_edges_kernel(res, epos, ev_out, table):
    count = H_OWN - TAIL_H
    fill_table(table, lambda h: res[:, cols_of(h, WIDE)], RHS, count)
    for step in range(E_TILES * LANE // GATHER_STEP):
        ev_out[:, cols_of(step, GATHER_STEP)] = gather_tile(
            table[...],
            epos[rows_of(step, GATHER_ROWS), :],
            RHS,
            count,
            lambda k: res[:, cols_of(2 * count + k, LANE)],
        )


def fill_pi(w, pi):
    zero = jnp.zeros((384, 384), BF)
    for v in range(4):
        for k in (0, 1):
            w[v, k] = zero
    for c in range(3):
        part = split(pi[:, c * NN : (c + 1) * NN])
        for k in (0, 1):
            for e2 in (0, 1):
                cols = slice(c * LANE + e2 * NN, c * LANE + (e2 + 1) * NN)
                for v in range(4):
                    w[v, k, e2 * LANE : (e2 + 1) * LANE, cols] = part[k][:LANE]
                    at = 2 * LANE + (2 * v + e2) * 16
                    w[v, k, at : at + 16, cols] = part[k][LANE:]


def fill_coefs(coef, wide, perm, curl):
    coef[...] = jnp.zeros((8, LANE), F32)
    coef[0:6, 0:EL] = perm[...]
    coef[6:7, 0:EL] = curl[...]
    c = coef[...]
    second = jnp.where(iota((8, LANE), 1) >= NN, 1, 0)
    for t in range(N_TILES):
        wide[:, t * LANE : (t + 1) * LANE] = jnp.take_along_axis(c, second + 2 * t, axis=1)


NODE_STEP = 1024
NODE_ROWS = NODE_STEP // LANE
NODE_STEPS = ELN // NODE_STEP
EDGE_STEP = 1024
EDGE_ROWS = EDGE_STEP // LANE
EDGE_STEPS = E_TILES * LANE // EDGE_STEP
BUFFERS = 3


def from_acc(compact, acc):
    compact[:, U_LOC:] = jnp.zeros((compact.shape[0], 2 * LANE), F32)
    for h in range(H_POS):
        compact[0:ROWS, h * WIDE : (h + 1) * WIDE] = summed(acc, h, ROWS)


def expand(out, compact, starts, rows):
    lane = iota((rows, LANE), 1)
    for p in range(PEERS):
        start = starts[p, 0]
        shift = start & (LANE - 1)
        base = (start - shift) // LANE
        both = jnp.where(lane >= shift, compact[0:rows, lanes(base, LANE)], compact[0:rows, lanes(base + 1, LANE)])
        out[p] = pltpu.roll(both, lax.rem(LANE - shift, LANE), 1)[: out.shape[1]]


def shrink(compact, arrived, starts):
    lane = iota((ROWS, LANE), 1)
    for p in range(PEERS):
        start = starts[p, 0]
        shift = start & (LANE - 1)
        base = (start - shift) // LANE
        block = pltpu.roll(arrived[p], shift, 1)
        pltpu.store(compact.at[:, lanes(base, LANE)], block, mask=lane >= shift)
        compact[:, lanes(base + 1, LANE)] = block


def restrict_kernel(
    ev_own, before, after, epos, pos, slots, pi, stiff, mass, perm, curl, starts_in,
    out, starts, sem, table, ev, w, coef, wide, xs, diag, left, acc, compact,
):
    move = pltpu.make_async_copy(starts_in, starts, sem)
    move.start()
    count = 2 * H_RIM - TAIL_H

    def rim(h):
        ref = before if h < H_RIM else after
        return ref[:, cols_of(h % H_RIM, WIDE)]

    fill_table(table, rim, RHS, count)
    for step in range(EDGE_STEPS):
        idx = epos[rows_of(step, EDGE_ROWS), :] - E_LOC
        found = gather_tile(
            table[...], idx, RHS, count, lambda k: after[:, cols_of(2 * (count - H_RIM) + k, LANE)]
        )
        at = cols_of(step, EDGE_STEP)
        ev[:, at] = jnp.where(spread(idx, RHS) >= 0, found, ev_own[:, at])
    fill_pi(w, pi)
    for v in range(4):
        blocks = []
        for g in range(8):
            t = 4 * g + v
            blocks.append(
                jnp.concatenate(
                    [ev[:, 2 * t * LANE : (2 * t + 2) * LANE], ev[:, (EL + g) * LANE : (EL + g + 1) * LANE]],
                    axis=1,
                )
            )
        high, low = split(jnp.concatenate(blocks, axis=0))
        y = (
            jnp.dot(high, w[v, 0], preferred_element_type=F32)
            + jnp.dot(high, w[v, 1], preferred_element_type=F32)
            + jnp.dot(low, w[v, 0], preferred_element_type=F32)
        )
        for g in range(8):
            t = 4 * g + v
            xs[:, t * LANE : (t + 1) * LANE] = stack(
                jnp.concatenate(
                    [y[g * RHS : (g + 1) * RHS, c * LANE : (c + 1) * LANE] for c in range(3)], axis=0
                )
            )
    fill_coefs(coef, wide, perm, curl)
    eye = iota((NN, NN), 0) == iota((NN, NN), 1)

    def diagonal(ref):
        d = jnp.sum(jnp.where(eye, ref[...], 0.0), axis=0, keepdims=True)
        return jnp.concatenate([d, d], axis=1)

    sd, md = diagonal(stiff), diagonal(mass)
    for t in range(N_TILES):
        at = slice(t * LANE, (t + 1) * LANE)
        diag[:, at] = wide[6:7, at] * sd + md * wide[0:3, at]

    for step in range(NODE_STEPS):
        at = cols_of(step, NODE_STEP)
        idx = pos[rows_of(step, NODE_ROWS), :]
        now = left.at[step % BUFFERS]
        mask_rows(now, xs[:, at], idx, 0, H_POS)
        mask_diag(now, H_POS * PAIR, [diag[c : c + 1, at] for c in range(3)], idx)
        accumulate(acc, step, now, idx)
    move.wait()
    from_acc(compact, acc)
    for h in range(H_POS):
        for c in range(3):
            compact[ROWS + c : ROWS + c + 1, h * WIDE : (h + 1) * WIDE] = diag_summed(
                acc, H_POS * PAIR, c, h
            )
    expand(out, compact, starts, SENT + 4)
    for p in range(PEERS):
        out[p, SENT - 1 : SENT, :] = slots[p : p + 1, :]


def collect(arrived, slots, left, acc, with_diag):
    for step in range(SLOTS // NODE_STEP):
        idx = slots[rows_of(step, NODE_ROWS), :]
        block = arrived[rows_of(step, NODE_ROWS)]
        x = jnp.concatenate([block[i, 0:ROWS] for i in range(NODE_ROWS)], axis=1)
        now = left.at[step % BUFFERS]
        mask_rows(now, stack(x), idx, 0, H_NODE)
        if with_diag:
            diag = [
                jnp.concatenate([block[i, ROWS + c : ROWS + c + 1] for i in range(NODE_ROWS)], axis=1)
                for c in range(3)
            ]
            mask_diag(now, H_NODE * PAIR, diag, idx)
        accumulate(acc, step, now, idx)


def serve(out, table, last, value, slots):
    count = H_NODE - TAIL_H
    fill_table(table, value, ROWS, count)
    for k in range(TAIL_H):
        last[:, cols_of(k, WIDE)] = value(count + k)
    for step in range(SLOTS // GATHER_STEP):
        found = gather_tile(
            table[...],
            slots[rows_of(step, GATHER_ROWS), :],
            ROWS,
            count,
            lambda k: last[:, cols_of(k, LANE)],
        )
        for i in range(GATHER_ROWS):
            out[step * GATHER_ROWS + i] = found[:, cols_of(i, LANE)]


def first_values(rhs, floor):
    first = cheb_factors()[0]

    def value(h):
        return jnp.concatenate(
            [
                first * rhs[h, c * RHS : (c + 1) * RHS, :] / floor[h, c : c + 1, :]
                for c in range(3)
            ],
            axis=0,
        )

    return value


def first_kernel(arrived, out, rhs_out, floor_out, slot_out, table, last, left, acc):
    for p in range(PEERS):
        slot_out[p : p + 1, :] = arrived[p, SENT - 1 : SENT, :].astype(I32)
    collect(arrived, slot_out, left, acc, True)
    for h in range(H_NODE):
        rhs_out[h] = summed(acc, h, ROWS)
        for c in range(3):
            floor_out[h, c : c + 1, :] = jnp.maximum(diag_summed(acc, H_NODE * PAIR, c, h), 1.0)
    serve(out, table, last, first_values(rhs_out, floor_out), slot_out)


def second_kernel(arrived, rhs, floor, slots, out, table, last, left, acc):
    first, keep, step = cheb_factors()
    collect(arrived, slots, left, acc, False)

    def value(h):
        applied = summed(acc, h, ROWS)
        parts = []
        for c in range(3):
            at = slice(c * RHS, (c + 1) * RHS)
            part = rhs[h, at, :]
            low = floor[h, c : c + 1, :]
            parts.append(keep * (first * part / low) + step * (part - applied[at]) / low)
        return jnp.concatenate(parts, axis=0)

    serve(out, table, last, value, slots)


def touched_table(table, compact, arrived, starts):
    shrink(compact, arrived, starts)
    fill_table(table, lambda h: compact[:, cols_of(h, WIDE)], ROWS, H_POS - TAIL_H)


def touched_tile(table, compact, pos, step):
    count = H_POS - TAIL_H
    return gather_tile(
        table[...],
        pos[rows_of(step, GATHER_ROWS), :],
        ROWS,
        count,
        lambda k: compact[:, cols_of(2 * count + k, LANE)],
    )


def apply_kernel(
    arrived, pos, stiff, mass, perm, curl, starts, out, table, op, coef, wide, xs, left, acc, compact
):
    touched_table(table, compact, arrived, starts)
    fill_coefs(coef, wide, perm, curl)
    op[...] = jnp.zeros((2, LANE, 2 * LANE), BF)
    for m, ref in enumerate((stiff, mass)):
        part = split(ref[...].T)
        for k in (0, 1):
            for e2 in (0, 1):
                at = slice(m * LANE + e2 * NN, m * LANE + (e2 + 1) * NN)
                op[k, e2 * NN : (e2 + 1) * NN, at] = part[k]

    tensor = ((0, 3, 4), (3, 1, 5), (4, 5, 2))
    for step in range(ELN // GATHER_STEP):
        values = touched_tile(table, compact, pos, step)
        high, low = split(
            jnp.concatenate([values[:, cols_of(i, LANE)] for i in range(GATHER_ROWS)], axis=0)
        )
        y = (
            jnp.dot(high, op[0], preferred_element_type=F32)
            + jnp.dot(high, op[1], preferred_element_type=F32)
            + jnp.dot(low, op[0], preferred_element_type=F32)
        )
        cols = wide[:, cols_of(step, GATHER_STEP)]
        tiles = []
        for i in range(GATHER_ROWS):
            k = cols[:, cols_of(i, LANE)]
            rows = [slice(i * ROWS + c * RHS, i * ROWS + (c + 1) * RHS) for c in range(3)]
            s = [y[r, :LANE] for r in rows]
            m = [y[r, LANE:] for r in rows]
            tiles.append(
                jnp.concatenate(
                    [
                        k[6:7] * s[c]
                        + k[tensor[c][0]][None] * m[0]
                        + k[tensor[c][1]][None] * m[1]
                        + k[tensor[c][2]][None] * m[2]
                        for c in range(3)
                    ],
                    axis=0,
                )
            )
        xs[:, cols_of(step, GATHER_STEP)] = stack(jnp.concatenate(tiles, axis=1))
    for step in range(NODE_STEPS):
        idx = pos[rows_of(step, NODE_ROWS), :]
        now = left.at[step % BUFFERS]
        mask_rows(now, xs[:, cols_of(step, NODE_STEP)], idx, 0, H_POS)
        accumulate(acc, step, now, idx)
    from_acc(compact, acc)
    expand(out, compact, starts, ROWS)


def edge_terms(arrived, pos, pi, starts, terms, table, w, values, compact):
    touched_table(table, compact, arrived, starts)
    fill_pi(w, pi)

    for step in range(ELN // GATHER_STEP):
        values[:, cols_of(step, GATHER_STEP)] = touched_tile(table, compact, pos, step)
    dims = (((1,), (1,)), ((), ()))
    rest = None
    for v in range(4):
        blocks = []
        for g in range(8):
            at = slice((4 * g + v) * LANE, (4 * g + v + 1) * LANE)
            blocks.append(
                jnp.concatenate([values[c * RHS : (c + 1) * RHS, at] for c in range(3)], axis=1)
            )
        high, low = split(jnp.concatenate(blocks, axis=0))
        y = (
            lax.dot_general(high, w[v, 0], dims, preferred_element_type=F32)
            + lax.dot_general(high, w[v, 1], dims, preferred_element_type=F32)
            + lax.dot_general(low, w[v, 0], dims, preferred_element_type=F32)
        )
        for g in range(8):
            t = 4 * g + v
            terms[:, 2 * t * LANE : (2 * t + 2) * LANE] = stack(y[g * RHS : (g + 1) * RHS, : 2 * LANE])
        rest = y[:, 2 * LANE :] if rest is None else rest + y[:, 2 * LANE :]
    for g in range(8):
        terms[:, (EL + g) * LANE : (EL + g + 1) * LANE] = stack(rest[g * RHS : (g + 1) * RHS])


def edge_scatter(terms, epos, left, acc, first, count):
    for step in range(EDGE_STEPS):
        idx = epos[rows_of(step, EDGE_ROWS), :]
        now = left.at[step % BUFFERS]
        mask_rows(now, terms[:, cols_of(step, EDGE_STEP)], idx, first, count)
        accumulate(acc, step, now, idx)


def prolong_rim_kernel(
    arrived, pos, epos, pi, starts, terms, low_out, high_out, table, w, values, compact, left, acc
):
    edge_terms(arrived, pos, pi, starts, terms, table, w, values, compact)
    edge_scatter(terms, epos, left, acc, H_OWN, 2 * H_RIM)
    for h in range(H_RIM):
        at = slice(h * WIDE, (h + 1) * WIDE)
        low_out[:, at] = summed(acc, h, RHS)
        high_out[:, at] = summed(acc, H_RIM + h, RHS)


def prolong_own_kernel(terms, epos, own, left, acc):
    edge_scatter(terms, epos, left, acc, 0, H_OWN)
    for h in range(H_OWN):
        own[:, h * WIDE : (h + 1) * WIDE] = summed(acc, h, RHS)


def finish_kernel(own, before, after, out):
    out[...] = own[...]
    out[:, :RIM_W] += before[...]
    out[:, E_LOC - RIM_W :] += after[...]


VM = pl.BlockSpec(memory_space=pltpu.VMEM)


SM = pl.BlockSpec(memory_space=pltpu.SMEM)
ANY = pl.BlockSpec(memory_space=pl.ANY)


def call(kernel, name, micros, outs, scratch, *args, scalars=0, outside=0):
    inside = len(args) - scalars - outside
    return pl.pallas_call(
        kernel,
        out_shape=[jax.ShapeDtypeStruct(s, t) for s, t in outs],
        in_specs=[ANY] * outside + [VM] * inside + [SM] * scalars,
        out_specs=[VM] * len(outs),
        scratch_shapes=[x if not isinstance(x, tuple) else pltpu.VMEM(*x) for x in scratch],
        compiler_params=pltpu.CompilerParams(vmem_limit_bytes=40 << 20),
        cost_estimate=pl.CostEstimate(flops=0, bytes_accessed=micros * 3600000, transcendentals=0),
        name=name,
    )(*args)


def exchange(x):
    return lax.all_to_all(x, "dev", split_axis=0, concat_axis=0, tiled=True)


def per_device(
    residual_edges,
    pi_block,
    stiff_block,
    mass_block,
    permittivity,
    curl_coef,
    edge_map,
    local_map,
    node_owner,
    node_slot,
):
    axes = ("grp", "dev")
    size = lax.axis_size(axes)
    up = [(i, i + 1) for i in range(size - 1)]
    down = [(i + 1, i) for i in range(size - 1)]
    curl = curl_coef.reshape(1, EL)
    chunks = U_LOC // LANE
    rim = ((RHS, RIM_W), F32)
    epos, pos, slot_rows, starts, low, high = call(
        prep_kernel,
        "index_prep",
        2,
        [
            ((E_TILES, LANE), I32),
            ((N_TILES, LANE), I32),
            ((PEERS, CAP), F32),
            ((PEERS, LANE), I32),
            rim,
            rim,
        ],
        [
            ((EL, ED), I32),
            ((NN, EL), I32),
            ((chunks, LANE), I32),
            ((chunks, LANE), I32),
            ((chunks * PEERS, LANE), BF),
            ((chunks, LANE), I32),
            ((chunks, LANE), I32),
            ((EL, LANE), I32),
            pltpu.SemaphoreType.DMA((6,)),
        ],
        residual_edges,
        edge_map.T,
        local_map,
        node_owner.reshape(chunks, LANE),
        node_slot.reshape(chunks, LANE),
        outside=5,
    )
    before = lax.ppermute(high, axes, up)
    after = lax.ppermute(low, axes, down)
    edge_rows = ((RHS, E_TILES * LANE), F32)
    (ev_own,) = call(
        own_edges_kernel, "own_edges", 4, [edge_rows], [(((H_OWN - TAIL_H) * 2 * RHS, WIDE), BF)], residual_edges, epos
    )
    pi_scratch = ((4, 2, 384, 384), BF)
    coefs = [((8, LANE), F32), ((8, ELN), F32)]
    served = ((PEERS, ROWS, CAP), F32)
    compact = ((ROWS, U_LOC + 2 * LANE), F32)
    (packed,) = call(
        restrict_kernel,
        "restrict",
        6,
        [((PEERS, SENT, CAP), F32)],
        [
            pltpu.SMEM((PEERS, LANE), I32),
            pltpu.SemaphoreType.DMA,
            (((2 * H_RIM - TAIL_H) * 2 * RHS, WIDE), BF),
            edge_rows,
            pi_scratch,
            *coefs,
            ((PAIR, ELN), BF),
            ((3, ELN), F32),
            ((BUFFERS, H_POS * PAIR + 96, NODE_STEP), BF),
            ((H_POS * PAIR + 96, WIDE), F32),
            ((SENT + 4, U_LOC + 2 * LANE), F32),
        ],
        ev_own, before, after, epos, pos, slot_rows, pi_block, stiff_block, mass_block, permittivity, curl, starts,
    )
    served_scratch = [(((H_NODE - TAIL_H) * PAIR, WIDE), BF), ((ROWS, TAIL_H * WIDE), F32)]
    wanted, rhs, floor, slots = call(
        first_kernel,
        "first_iter",
        5,
        [served, ((H_NODE, ROWS, WIDE), F32), ((H_NODE, 3, WIDE), F32), ((PEERS, CAP), I32)],
        [*served_scratch, ((BUFFERS, H_NODE * PAIR + 96, NODE_STEP), BF), ((H_NODE * PAIR + 96, WIDE), F32)],
        exchange(packed),
    )
    position_table = (((H_POS - TAIL_H) * PAIR, WIDE), BF)
    (applied,) = call(
        apply_kernel,
        "operator",
        8,
        [served],
        [
            position_table,
            ((2, LANE, 2 * LANE), BF),
            *coefs,
            ((PAIR, ELN), BF),
            ((BUFFERS, H_POS * PAIR, NODE_STEP), BF),
            ((H_POS * PAIR, WIDE), F32),
            compact,
        ],
        exchange(wanted), pos, stiff_block, mass_block, permittivity, curl, starts,
        scalars=1,
    )
    (wanted,) = call(
        second_kernel,
        "second_iter",
        5,
        [served],
        [*served_scratch, ((BUFFERS, H_NODE * PAIR, NODE_STEP), BF), ((H_NODE * PAIR, WIDE), F32)],
        exchange(applied), rhs, floor, slots,
    )
    terms, low, high = call(
        prolong_rim_kernel,
        "prolong_rim",
        6,
        [((2 * RHS, E_TILES * LANE), BF), rim, rim],
        [
            position_table,
            pi_scratch,
            ((ROWS, ELN), F32),
            compact,
            ((BUFFERS, 2 * H_RIM * 2 * RHS, EDGE_STEP), BF),
            ((2 * H_RIM * 2 * RHS, WIDE), F32),
        ],
        exchange(wanted), pos, epos, pi_block, starts,
        scalars=1,
    )
    from_before = lax.ppermute(high, axes, up)
    from_after = lax.ppermute(low, axes, down)
    (own,) = call(
        prolong_own_kernel,
        "prolong_own",
        5,
        [((RHS, E_LOC), F32)],
        [((BUFFERS, H_OWN * 2 * RHS, EDGE_STEP), BF), ((H_OWN * 2 * RHS, WIDE), F32)],
        terms, epos,
    )
    (out,) = call(finish_kernel, "finish", 1, [((RHS, E_LOC), F32)], [], own, from_before, from_after)
    return out


def solution(mesh):
    in_specs = (
        P(None, ("grp", "dev")),
        P(),
        P(),
        P(),
        P(None, ("grp", "dev")),
        P(("grp", "dev")),
        P(None, ("grp", "dev")),
        P(None, ("grp", "dev")),
        P(("grp", "dev")),
        P(("grp", "dev")),
    )
    out_specs = P(None, ("grp", "dev"))
    return jax.shard_map(
        per_device, mesh=mesh, in_specs=in_specs, out_specs=out_specs, check_vma=False
    )
```

```python
import jax
import jax.numpy as jnp
from jax import lax
from jax.experimental import pallas as pl
from jax.experimental.pallas import tpu as pltpu
from jax.sharding import PartitionSpec as P

RHS = 16
ED = 144
NN = 64
EL = 64
E_LOC = 5376
RIM = 672
U_LOC = 2048
PEERS = 32
CAP = 128
ROWS = 3 * RHS
PAIR = 2 * ROWS
SENT = ROWS + 4
SLOTS = PEERS * CAP
ELN = NN * EL
LANE = 128
WIDE = 256
RIM_W = 768
H_OWN = E_LOC // WIDE
H_RIM = RIM_W // WIDE
H_EDGE = H_OWN + 2 * H_RIM
H_POS = U_LOC // WIDE
H_NODE = 7
TAIL = 4
TAIL_H = TAIL // 2
GATHER_STEP = 1024
GATHER_ROWS = GATHER_STEP // LANE
E_TILES = 72
N_TILES = ELN // LANE
BF = jnp.bfloat16
F32 = jnp.float32
I32 = jnp.int32

CHEB_LOW = 0.3
CHEB_HIGH = 2.0


def cheb_factors():
    center = 0.5 * (CHEB_HIGH + CHEB_LOW)
    half_width = 0.5 * (CHEB_HIGH - CHEB_LOW)
    sigma_ratio = center / half_width
    rho_first = 1.0 / sigma_ratio
    rho_second = 1.0 / (2.0 * sigma_ratio - rho_first)
    return (1.0 / center, 1.0 + rho_second * rho_first, 2.0 * rho_second / half_width)


def split(x):
    high = x.astype(BF)
    return high, (x - high.astype(F32)).astype(BF)


def stack(x):
    return jnp.concatenate([x, x - x.astype(BF).astype(F32)], axis=0).astype(BF)


def iota(shape, dim):
    return lax.broadcasted_iota(I32, shape, dim)


def spread(index_rows, height):
    return jnp.concatenate(
        [jnp.broadcast_to(index_rows[i : i + 1], (height, LANE)) for i in range(index_rows.shape[0])],
        axis=1,
    )


def low_part(index_rows):
    return spread(index_rows & (WIDE - 1), 1).astype(F32).astype(BF)


def one_hot_low(index_rows):
    low = low_part(index_rows)
    shape = (WIDE, low.shape[1])
    here = jnp.broadcast_to(low, shape) == iota(shape, 0).astype(F32).astype(BF)
    return jnp.where(here, jnp.ones(shape, BF), jnp.zeros(shape, BF))


def gather_tile(table, index_rows, rows, count, tail):
    found = jnp.dot(table, one_hot_low(index_rows), preferred_element_type=F32)
    high = spread(index_rows >> 8, 2 * rows)
    out = found[: 2 * rows]
    for h in range(1, count):
        out = jnp.where(high == h, found[h * 2 * rows : (h + 1) * 2 * rows], out)
    out = out[:rows] + out[rows:]
    tiles = []
    for i in range(index_rows.shape[0]):
        index = jnp.broadcast_to(index_rows[i : i + 1], (rows, LANE))
        part = out[:, i * LANE : (i + 1) * LANE]
        for k in range(TAIL):
            picked = jnp.take_along_axis(tail(k), index & (LANE - 1), axis=1)
            part = jnp.where((index >> 7) == 2 * count + k, picked, part)
        tiles.append(part)
    return jnp.concatenate(tiles, axis=1)


def fill_table(table, source, rows, count):
    for h in range(count):
        table[h * 2 * rows : (h + 1) * 2 * rows, :] = stack(source(h))


def mask_rows(left, x, index_rows, first, count):
    rows, width = x.shape
    high = spread(index_rows >> 8, 1).astype(F32).astype(BF)
    high = jnp.broadcast_to(high, (rows, width))
    for h in range(count):
        left[h * rows : (h + 1) * rows, :] = jnp.where(high == float(first + h), x, jnp.zeros_like(x))


def mask_diag(left, base, diag, index_rows):
    width = diag[0].shape[1]
    here = spread(index_rows >> 8, 16) == iota((16, width), 0)
    for c in range(3):
        left[base + c * 32 : base + (c + 1) * 32, :] = stack(
            jnp.where(here, jnp.broadcast_to(diag[c], (16, width)), 0.0)
        )


def accumulate(acc, step, left, index_rows):
    part = lax.dot_general(
        left[...], one_hot_low(index_rows), (((1,), (1,)), ((), ())), preferred_element_type=F32
    )
    if isinstance(step, int):
        acc[...] = part if step == 0 else acc[...] + part
        return

    @pl.when(step == 0)
    def _():
        acc[...] = part

    @pl.when(step > 0)
    def _():
        acc[...] += part


def summed(acc, h, rows, at=slice(None)):
    base = h * 2 * rows
    return acc[base : base + rows, at] + acc[base + rows : base + 2 * rows, at]


def diag_summed(acc, base, c, h, at=slice(None)):
    row = base + c * 32 + h
    return acc[row : row + 1, at] + acc[row + 16 : row + 17, at]


def over(count, body, loop):
    if loop:
        lax.fori_loop(0, count, lambda step, carry: (body(step), carry)[1], 0)
    else:
        for step in range(count):
            body(step)


def rows_of(step, count):
    if isinstance(step, int):
        return slice(step * count, (step + 1) * count)
    return pl.ds(pl.multiple_of(step * count, count), count)


def cols_of(step, width):
    return rows_of(step, width)


def lanes(step, width):
    return pl.ds(pl.multiple_of(step * width, width), width)


def prep_kernel(
    res, em_in, lm_in, owner_in, slot_in,
    epos_out, pos_out, slot_out, start_out, low_out, high_out,
    em, lm, owner, slot, hots, rank_s, pos_s, tr, sems,
):
    moves = [
        (owner_in, owner),
        (em_in, em),
        (lm_in, lm),
        (slot_in, slot),
        (res.at[:, :RIM_W], low_out),
        (res.at[:, E_LOC - RIM_W :], high_out),
    ]
    moves = [pltpu.make_async_copy(a, b, sems.at[i]) for i, (a, b) in enumerate(moves)]
    for move in moves:
        move.start()
    for move in moves:
        move.wait()
    tr[:, : ED - LANE] = em[:, LANE:]
    rest = [tr[pl.ds(i, 8, stride=8), :][:, : ED - LANE] for i in range(8)]
    m = jnp.concatenate([em[:, :LANE], jnp.concatenate(rest, axis=1)], axis=0)
    epos_out[...] = jnp.where(
        m < RIM,
        m + (E_LOC + RIM_W - RIM),
        jnp.where(m < RIM + E_LOC, m - RIM, m - (RIM + E_LOC) + E_LOC + RIM_W),
    )
    chunks = U_LOC // LANE
    for t in range(chunks):
        o = jnp.broadcast_to(owner[t : t + 1, :], (PEERS, LANE))
        hots[t * PEERS : (t + 1) * PEERS, :] = jnp.where(o == iota((PEERS, LANE), 0), 1.0, 0.0).astype(BF)
    before = jnp.where(iota((LANE, LANE), 0) < iota((LANE, LANE), 1), 1.0, 0.0)
    tri = jnp.concatenate([before, jnp.ones((LANE, LANE), F32)], axis=1).astype(BF)
    ranks = jnp.dot(hots[...], tri, preferred_element_type=F32)
    counts = ranks[:PEERS, LANE:]
    for t in range(1, chunks):
        counts = counts + ranks[t * PEERS : (t + 1) * PEERS, LANE:]
    below = jnp.where(iota((PEERS, PEERS), 1) < iota((PEERS, PEERS), 0), 1.0, 0.0).astype(BF)
    starts = jnp.dot(below, counts.astype(BF), preferred_element_type=F32)
    start_out[...] = starts.astype(I32)
    base = jnp.zeros((PEERS, LANE), F32)
    for t in range(chunks):
        hot = hots[t * PEERS : (t + 1) * PEERS, :].astype(F32)
        here = ranks[t * PEERS : (t + 1) * PEERS]
        rank = here[:, :LANE] + base
        base = base + here[:, LANE:]
        rank_s[t : t + 1, :] = jnp.sum(hot * rank, axis=0, keepdims=True).astype(I32)
        pos_s[t : t + 1, :] = jnp.sum(hot * (rank + starts), axis=0, keepdims=True).astype(I32)
    left = []
    right = []
    for t in range(chunks):
        hot = hots[t * PEERS : (t + 1) * PEERS, :].astype(F32)
        s = slot[t : t + 1, :] + 1
        left.append(
            jnp.concatenate([hot * (s >> 6).astype(F32), hot * (s & 63).astype(F32)], axis=0).astype(BF)
        )
        r = jnp.broadcast_to(rank_s[t : t + 1, :], (LANE, LANE))
        right.append(jnp.where(r == iota((LANE, LANE), 0), 1.0, 0.0).astype(BF))
    packed = lax.dot_general(
        jnp.concatenate(left, axis=1),
        jnp.concatenate(right, axis=1),
        (((1,), (1,)), ((), ())),
        preferred_element_type=F32,
    )
    slot_out[...] = packed[:PEERS] * 64.0 + packed[PEERS:] - 1.0
    tr[:, :NN] = lm[...].T
    idx = jnp.concatenate([tr[pl.ds(i, N_TILES, stride=2), :][:, :NN] for i in (0, 1)], axis=1)
    high, low = idx >> 7, idx & (LANE - 1)
    pos = jnp.zeros((N_TILES, LANE), I32)
    for t in range(chunks):
        row = jnp.broadcast_to(pos_s[t : t + 1, :], (N_TILES, LANE))
        pos = jnp.where(high == t, jnp.take_along_axis(row, low, axis=1), pos)
    pos_out[...] = pos


def own_edges_kernel(res, epos, ev_out, table):
    count = H_OWN - TAIL_H
    fill_table(table, lambda h: res[:, cols_of(h, WIDE)], RHS, count)
    for step in range(E_TILES * LANE // GATHER_STEP):
        ev_out[:, cols_of(step, GATHER_STEP)] = gather_tile(
            table[...],
            epos[rows_of(step, GATHER_ROWS), :],
            RHS,
            count,
            lambda k: res[:, cols_of(2 * count + k, LANE)],
        )


def fill_pi(w, pi):
    zero = jnp.zeros((384, 384), BF)
    for v in range(4):
        for k in (0, 1):
            w[v, k] = zero
    for c in range(3):
        part = split(pi[:, c * NN : (c + 1) * NN])
        for k in (0, 1):
            for e2 in (0, 1):
                cols = slice(c * LANE + e2 * NN, c * LANE + (e2 + 1) * NN)
                for v in range(4):
                    w[v, k, e2 * LANE : (e2 + 1) * LANE, cols] = part[k][:LANE]
                    at = 2 * LANE + (2 * v + e2) * 16
                    w[v, k, at : at + 16, cols] = part[k][LANE:]


def fill_coefs(coef, wide, perm, curl):
    coef[...] = jnp.zeros((8, LANE), F32)
    coef[0:6, 0:EL] = perm[...]
    coef[6:7, 0:EL] = curl[...]
    c = coef[...]
    second = jnp.where(iota((8, LANE), 1) >= NN, 1, 0)
    for t in range(N_TILES):
        wide[:, t * LANE : (t + 1) * LANE] = jnp.take_along_axis(c, second + 2 * t, axis=1)


NODE_STEP = 2048
NODE_ROWS = NODE_STEP // LANE
NODE_STEPS = ELN // NODE_STEP
EDGE_STEP = 3072
EDGE_ROWS = EDGE_STEP // LANE
EDGE_STEPS = E_TILES * LANE // EDGE_STEP
BUFFERS = 2
LOOP = {'collect': 1, 'edge': 1, 'node': 0, 'serve': 0, 'tile': 0, 'rim': 0}


def from_acc(compact, acc):
    compact[:, U_LOC:] = jnp.zeros((compact.shape[0], 2 * LANE), F32)
    for h in range(H_POS):
        compact[0:ROWS, h * WIDE : (h + 1) * WIDE] = summed(acc, h, ROWS)


def expand(out, compact, starts, rows):
    lane = iota((rows, LANE), 1)
    for p in range(PEERS):
        start = starts[p, 0]
        shift = start & (LANE - 1)
        base = (start - shift) // LANE
        both = jnp.where(lane >= shift, compact[0:rows, lanes(base, LANE)], compact[0:rows, lanes(base + 1, LANE)])
        out[p] = pltpu.roll(both, lax.rem(LANE - shift, LANE), 1)[: out.shape[1]]


def shrink(compact, arrived, starts):
    lane = iota((ROWS, LANE), 1)
    for p in range(PEERS):
        start = starts[p, 0]
        shift = start & (LANE - 1)
        base = (start - shift) // LANE
        block = pltpu.roll(arrived[p], shift, 1)
        pltpu.store(compact.at[:, lanes(base, LANE)], block, mask=lane >= shift)
        compact[:, lanes(base + 1, LANE)] = block


def restrict_kernel(
    ev_own, before, after, epos, pos, slots, pi, stiff, mass, perm, curl, starts_in,
    out, starts, sem, table, ev, w, coef, wide, xs, diag, left, acc, compact,
):
    move = pltpu.make_async_copy(starts_in, starts, sem)
    move.start()
    count = 2 * H_RIM - TAIL_H

    def rim(h):
        ref = before if h < H_RIM else after
        return ref[:, cols_of(h % H_RIM, WIDE)]

    fill_table(table, rim, RHS, count)
    def step_body(step):
        idx = epos[rows_of(step, GATHER_ROWS), :] - E_LOC
        found = gather_tile(
            table[...], idx, RHS, count, lambda k: after[:, cols_of(2 * (count - H_RIM) + k, LANE)]
        )
        at = cols_of(step, GATHER_STEP)
        ev[:, at] = jnp.where(spread(idx, RHS) >= 0, found, ev_own[:, at])

    over(E_TILES // GATHER_ROWS, step_body, LOOP['rim'])
    fill_pi(w, pi)
    for v in range(4):
        blocks = []
        for g in range(8):
            t = 4 * g + v
            blocks.append(
                jnp.concatenate(
                    [ev[:, 2 * t * LANE : (2 * t + 2) * LANE], ev[:, (EL + g) * LANE : (EL + g + 1) * LANE]],
                    axis=1,
                )
            )
        high, low = split(jnp.concatenate(blocks, axis=0))
        y = (
            jnp.dot(high, w[v, 0], preferred_element_type=F32)
            + jnp.dot(high, w[v, 1], preferred_element_type=F32)
            + jnp.dot(low, w[v, 0], preferred_element_type=F32)
        )
        for g in range(8):
            t = 4 * g + v
            xs[:, t * LANE : (t + 1) * LANE] = stack(
                jnp.concatenate(
                    [y[g * RHS : (g + 1) * RHS, c * LANE : (c + 1) * LANE] for c in range(3)], axis=0
                )
            )
    fill_coefs(coef, wide, perm, curl)
    eye = iota((NN, NN), 0) == iota((NN, NN), 1)

    def diagonal(ref):
        d = jnp.sum(jnp.where(eye, ref[...], 0.0), axis=0, keepdims=True)
        return jnp.concatenate([d, d], axis=1)

    sd, md = diagonal(stiff), diagonal(mass)
    for t in range(N_TILES):
        at = slice(t * LANE, (t + 1) * LANE)
        diag[:, at] = wide[6:7, at] * sd + md * wide[0:3, at]

    def step_body(step):
        at = cols_of(step, NODE_STEP)
        idx = pos[rows_of(step, NODE_ROWS), :]
        now = left.at[step % BUFFERS] if isinstance(step, int) else left.at[0]
        mask_rows(now, xs[:, at], idx, 0, H_POS)
        mask_diag(now, H_POS * PAIR, [diag[c : c + 1, at] for c in range(3)], idx)
        accumulate(acc, step, now, idx)

    over(NODE_STEPS, step_body, LOOP['node'])
    move.wait()
    from_acc(compact, acc)
    for h in range(H_POS):
        for c in range(3):
            compact[ROWS + c : ROWS + c + 1, h * WIDE : (h + 1) * WIDE] = diag_summed(
                acc, H_POS * PAIR, c, h
            )
    expand(out, compact, starts, SENT + 4)
    for p in range(PEERS):
        out[p, SENT - 1 : SENT, :] = slots[p : p + 1, :]


def collect(arrived, slots, left, acc, with_diag):
    def step_body(step):
        idx = slots[rows_of(step, NODE_ROWS), :]
        block = arrived[rows_of(step, NODE_ROWS)]
        x = jnp.concatenate([block[i, 0:ROWS] for i in range(NODE_ROWS)], axis=1)
        now = left.at[step % BUFFERS] if isinstance(step, int) else left.at[0]
        mask_rows(now, stack(x), idx, 0, H_NODE)
        if with_diag:
            diag = [
                jnp.concatenate([block[i, ROWS + c : ROWS + c + 1] for i in range(NODE_ROWS)], axis=1)
                for c in range(3)
            ]
            mask_diag(now, H_NODE * PAIR, diag, idx)
        accumulate(acc, step, now, idx)

    over(SLOTS // NODE_STEP, step_body, LOOP['collect'])


def serve(out, table, last, value, slots):
    count = H_NODE - TAIL_H
    fill_table(table, value, ROWS, count)
    for k in range(TAIL_H):
        last[:, cols_of(k, WIDE)] = value(count + k)
    def step_body(step):
        found = gather_tile(
            table[...],
            slots[rows_of(step, GATHER_ROWS), :],
            ROWS,
            count,
            lambda k: last[:, cols_of(k, LANE)],
        )
        for i in range(GATHER_ROWS):
            out[step * GATHER_ROWS + i] = found[:, cols_of(i, LANE)]

    over(SLOTS // GATHER_STEP, step_body, LOOP['serve'])


def first_values(rhs, floor):
    first = cheb_factors()[0]

    def value(h):
        return jnp.concatenate(
            [
                first * rhs[h, c * RHS : (c + 1) * RHS, :] / floor[h, c : c + 1, :]
                for c in range(3)
            ],
            axis=0,
        )

    return value


def first_kernel(arrived, out, rhs_out, floor_out, slot_out, table, last, left, acc):
    for p in range(PEERS):
        slot_out[p : p + 1, :] = arrived[p, SENT - 1 : SENT, :].astype(I32)
    collect(arrived, slot_out, left, acc, True)
    for h in range(H_NODE):
        rhs_out[h] = summed(acc, h, ROWS)
        for c in range(3):
            floor_out[h, c : c + 1, :] = jnp.maximum(diag_summed(acc, H_NODE * PAIR, c, h), 1.0)
    serve(out, table, last, first_values(rhs_out, floor_out), slot_out)


def second_kernel(arrived, rhs, floor, slots, out, table, last, left, acc):
    first, keep, step = cheb_factors()
    collect(arrived, slots, left, acc, False)

    def value(h):
        applied = summed(acc, h, ROWS)
        parts = []
        for c in range(3):
            at = slice(c * RHS, (c + 1) * RHS)
            part = rhs[h, at, :]
            low = floor[h, c : c + 1, :]
            parts.append(keep * (first * part / low) + step * (part - applied[at]) / low)
        return jnp.concatenate(parts, axis=0)

    serve(out, table, last, value, slots)


def touched_table(table, compact, arrived, starts):
    shrink(compact, arrived, starts)
    fill_table(table, lambda h: compact[:, cols_of(h, WIDE)], ROWS, H_POS - TAIL_H)


def touched_tile(table, compact, pos, step):
    count = H_POS - TAIL_H
    return gather_tile(
        table[...],
        pos[rows_of(step, GATHER_ROWS), :],
        ROWS,
        count,
        lambda k: compact[:, cols_of(2 * count + k, LANE)],
    )


def apply_kernel(
    arrived, pos, stiff, mass, perm, curl, starts, out, table, op, coef, wide, xs, left, acc, compact
):
    touched_table(table, compact, arrived, starts)
    fill_coefs(coef, wide, perm, curl)
    op[...] = jnp.zeros((2, LANE, 2 * LANE), BF)
    for m, ref in enumerate((stiff, mass)):
        part = split(ref[...].T)
        for k in (0, 1):
            for e2 in (0, 1):
                at = slice(m * LANE + e2 * NN, m * LANE + (e2 + 1) * NN)
                op[k, e2 * NN : (e2 + 1) * NN, at] = part[k]

    tensor = ((0, 3, 4), (3, 1, 5), (4, 5, 2))
    def step_body(step):
        values = touched_tile(table, compact, pos, step)
        high, low = split(
            jnp.concatenate([values[:, cols_of(i, LANE)] for i in range(GATHER_ROWS)], axis=0)
        )
        y = (
            jnp.dot(high, op[0], preferred_element_type=F32)
            + jnp.dot(high, op[1], preferred_element_type=F32)
            + jnp.dot(low, op[0], preferred_element_type=F32)
        )
        cols = wide[:, cols_of(step, GATHER_STEP)]
        tiles = []
        for i in range(GATHER_ROWS):
            k = cols[:, cols_of(i, LANE)]
            rows = [slice(i * ROWS + c * RHS, i * ROWS + (c + 1) * RHS) for c in range(3)]
            s = [y[r, :LANE] for r in rows]
            m = [y[r, LANE:] for r in rows]
            tiles.append(
                jnp.concatenate(
                    [
                        k[6:7] * s[c]
                        + k[tensor[c][0]][None] * m[0]
                        + k[tensor[c][1]][None] * m[1]
                        + k[tensor[c][2]][None] * m[2]
                        for c in range(3)
                    ],
                    axis=0,
                )
            )
        xs[:, cols_of(step, GATHER_STEP)] = stack(jnp.concatenate(tiles, axis=1))

    over(ELN // GATHER_STEP, step_body, LOOP['tile'])
    def step_body(step):
        idx = pos[rows_of(step, NODE_ROWS), :]
        now = left.at[step % BUFFERS] if isinstance(step, int) else left.at[0]
        mask_rows(now, xs[:, cols_of(step, NODE_STEP)], idx, 0, H_POS)
        accumulate(acc, step, now, idx)

    over(NODE_STEPS, step_body, LOOP['node'])
    from_acc(compact, acc)
    expand(out, compact, starts, ROWS)


def edge_terms(arrived, pos, pi, starts, terms, table, w, values, compact):
    touched_table(table, compact, arrived, starts)
    fill_pi(w, pi)

    def step_body(step):
        values[:, cols_of(step, GATHER_STEP)] = touched_tile(table, compact, pos, step)

    over(ELN // GATHER_STEP, step_body, LOOP['tile'])
    dims = (((1,), (1,)), ((), ()))
    rest = None
    for v in range(4):
        blocks = []
        for g in range(8):
            at = slice((4 * g + v) * LANE, (4 * g + v + 1) * LANE)
            blocks.append(
                jnp.concatenate([values[c * RHS : (c + 1) * RHS, at] for c in range(3)], axis=1)
            )
        high, low = split(jnp.concatenate(blocks, axis=0))
        y = (
            lax.dot_general(high, w[v, 0], dims, preferred_element_type=F32)
            + lax.dot_general(high, w[v, 1], dims, preferred_element_type=F32)
            + lax.dot_general(low, w[v, 0], dims, preferred_element_type=F32)
        )
        for g in range(8):
            t = 4 * g + v
            terms[:, 2 * t * LANE : (2 * t + 2) * LANE] = stack(y[g * RHS : (g + 1) * RHS, : 2 * LANE])
        rest = y[:, 2 * LANE :] if rest is None else rest + y[:, 2 * LANE :]
    for g in range(8):
        terms[:, (EL + g) * LANE : (EL + g + 1) * LANE] = stack(rest[g * RHS : (g + 1) * RHS])


def edge_scatter(terms, epos, left, acc, first, count):
    def step_body(step):
        idx = epos[rows_of(step, EDGE_ROWS), :]
        now = left.at[step % BUFFERS] if isinstance(step, int) else left.at[0]
        mask_rows(now, terms[:, cols_of(step, EDGE_STEP)], idx, first, count)
        accumulate(acc, step, now, idx)

    over(EDGE_STEPS, step_body, LOOP['edge'])


def prolong_rim_kernel(
    arrived, pos, epos, pi, starts, terms, low_out, high_out, table, w, values, compact, left, acc
):
    edge_terms(arrived, pos, pi, starts, terms, table, w, values, compact)
    edge_scatter(terms, epos, left, acc, H_OWN, 2 * H_RIM)
    for h in range(H_RIM):
        at = slice(h * WIDE, (h + 1) * WIDE)
        low_out[:, at] = summed(acc, h, RHS)
        high_out[:, at] = summed(acc, H_RIM + h, RHS)


def prolong_own_kernel(terms, epos, own, left, acc):
    edge_scatter(terms, epos, left, acc, 0, H_OWN)
    for h in range(H_OWN):
        own[:, h * WIDE : (h + 1) * WIDE] = summed(acc, h, RHS)


def finish_kernel(own, before, after, out):
    out[...] = own[...]
    out[:, :RIM_W] += before[...]
    out[:, E_LOC - RIM_W :] += after[...]


VM = pl.BlockSpec(memory_space=pltpu.VMEM)


SM = pl.BlockSpec(memory_space=pltpu.SMEM)
ANY = pl.BlockSpec(memory_space=pl.ANY)


def call(kernel, name, micros, outs, scratch, *args, scalars=0, outside=0):
    inside = len(args) - scalars - outside
    return pl.pallas_call(
        kernel,
        out_shape=[jax.ShapeDtypeStruct(s, t) for s, t in outs],
        in_specs=[ANY] * outside + [VM] * inside + [SM] * scalars,
        out_specs=[VM] * len(outs),
        scratch_shapes=[x if not isinstance(x, tuple) else pltpu.VMEM(*x) for x in scratch],
        compiler_params=pltpu.CompilerParams(vmem_limit_bytes=(56 if outside else 40) << 20),
        cost_estimate=pl.CostEstimate(flops=0, bytes_accessed=micros * 3600000, transcendentals=0),
        name=name,
    )(*args)


def exchange(x):
    return lax.all_to_all(x, "dev", split_axis=0, concat_axis=0, tiled=True)


def per_device(
    residual_edges,
    pi_block,
    stiff_block,
    mass_block,
    permittivity,
    curl_coef,
    edge_map,
    local_map,
    node_owner,
    node_slot,
):
    axes = ("grp", "dev")
    size = lax.axis_size(axes)
    up = [(i, i + 1) for i in range(size - 1)]
    down = [(i + 1, i) for i in range(size - 1)]
    curl = curl_coef.reshape(1, EL)
    chunks = U_LOC // LANE
    rim = ((RHS, RIM_W), F32)
    epos, pos, slot_rows, starts, low, high = call(
        prep_kernel,
        "index_prep",
        2,
        [
            ((E_TILES, LANE), I32),
            ((N_TILES, LANE), I32),
            ((PEERS, CAP), F32),
            ((PEERS, LANE), I32),
            rim,
            rim,
        ],
        [
            ((EL, ED), I32),
            ((NN, EL), I32),
            ((chunks, LANE), I32),
            ((chunks, LANE), I32),
            ((chunks * PEERS, LANE), BF),
            ((chunks, LANE), I32),
            ((chunks, LANE), I32),
            ((EL, LANE), I32),
            pltpu.SemaphoreType.DMA((6,)),
        ],
        residual_edges,
        edge_map.T,
        local_map,
        node_owner.reshape(chunks, LANE),
        node_slot.reshape(chunks, LANE),
        outside=5,
    )
    before = lax.ppermute(high, axes, up)
    after = lax.ppermute(low, axes, down)
    edge_rows = ((RHS, E_TILES * LANE), F32)
    (ev_own,) = call(
        own_edges_kernel, "own_edges", 4, [edge_rows], [(((H_OWN - TAIL_H) * 2 * RHS, WIDE), BF)], residual_edges, epos
    )
    pi_scratch = ((4, 2, 384, 384), BF)
    coefs = [((8, LANE), F32), ((8, ELN), F32)]
    served = ((PEERS, ROWS, CAP), F32)
    compact = ((ROWS, U_LOC + 2 * LANE), F32)
    (packed,) = call(
        restrict_kernel,
        "restrict",
        6,
        [((PEERS, SENT, CAP), F32)],
        [
            pltpu.SMEM((PEERS, LANE), I32),
            pltpu.SemaphoreType.DMA,
            (((2 * H_RIM - TAIL_H) * 2 * RHS, WIDE), BF),
            edge_rows,
            pi_scratch,
            *coefs,
            ((PAIR, ELN), BF),
            ((3, ELN), F32),
            ((BUFFERS, H_POS * PAIR + 96, NODE_STEP), BF),
            ((H_POS * PAIR + 96, WIDE), F32),
            ((SENT + 4, U_LOC + 2 * LANE), F32),
        ],
        ev_own, before, after, epos, pos, slot_rows, pi_block, stiff_block, mass_block, permittivity, curl, starts,
    )
    served_scratch = [(((H_NODE - TAIL_H) * PAIR, WIDE), BF), ((ROWS, TAIL_H * WIDE), F32)]
    wanted, rhs, floor, slots = call(
        first_kernel,
        "first_iter",
        5,
        [served, ((H_NODE, ROWS, WIDE), F32), ((H_NODE, 3, WIDE), F32), ((PEERS, CAP), I32)],
        [*served_scratch, ((BUFFERS, H_NODE * PAIR + 96, NODE_STEP), BF), ((H_NODE * PAIR + 96, WIDE), F32)],
        exchange(packed),
    )
    position_table = (((H_POS - TAIL_H) * PAIR, WIDE), BF)
    (applied,) = call(
        apply_kernel,
        "operator",
        8,
        [served],
        [
            position_table,
            ((2, LANE, 2 * LANE), BF),
            *coefs,
            ((PAIR, ELN), BF),
            ((BUFFERS, H_POS * PAIR, NODE_STEP), BF),
            ((H_POS * PAIR, WIDE), F32),
            compact,
        ],
        exchange(wanted), pos, stiff_block, mass_block, permittivity, curl, starts,
        scalars=1,
    )
    (wanted,) = call(
        second_kernel,
        "second_iter",
        5,
        [served],
        [*served_scratch, ((BUFFERS, H_NODE * PAIR, NODE_STEP), BF), ((H_NODE * PAIR, WIDE), F32)],
        exchange(applied), rhs, floor, slots,
    )
    terms, low, high = call(
        prolong_rim_kernel,
        "prolong_rim",
        6,
        [((2 * RHS, E_TILES * LANE), BF), rim, rim],
        [
            position_table,
            pi_scratch,
            ((ROWS, ELN), F32),
            compact,
            ((BUFFERS, 2 * H_RIM * 2 * RHS, EDGE_STEP), BF),
            ((2 * H_RIM * 2 * RHS, WIDE), F32),
        ],
        exchange(wanted), pos, epos, pi_block, starts,
        scalars=1,
    )
    from_before = lax.ppermute(high, axes, up)
    from_after = lax.ppermute(low, axes, down)
    (own,) = call(
        prolong_own_kernel,
        "prolong_own",
        5,
        [((RHS, E_LOC), F32)],
        [((BUFFERS, H_OWN * 2 * RHS, EDGE_STEP), BF), ((H_OWN * 2 * RHS, WIDE), F32)],
        terms, epos,
    )
    (out,) = call(finish_kernel, "finish", 1, [((RHS, E_LOC), F32)], [], own, from_before, from_after)
    return out


def solution(mesh):
    in_specs = (
        P(None, ("grp", "dev")),
        P(),
        P(),
        P(),
        P(None, ("grp", "dev")),
        P(("grp", "dev")),
        P(None, ("grp", "dev")),
        P(None, ("grp", "dev")),
        P(("grp", "dev")),
        P(("grp", "dev")),
    )
    out_specs = P(None, ("grp", "dev"))
    return jax.shard_map(
        per_device, mesh=mesh, in_specs=in_specs, out_specs=out_specs, check_vma=False
    )
```

```python
import jax
import jax.numpy as jnp
from jax import lax
from jax.experimental import pallas as pl
from jax.experimental.pallas import tpu as pltpu
from jax.sharding import PartitionSpec as P

RHS = 16
ED = 144
NN = 64
EL = 64
E_LOC = 5376
RIM = 672
U_LOC = 2048
PEERS = 32
CAP = 128
ROWS = 3 * RHS
PAIR = 2 * ROWS
SENT = ROWS + 4
SLOTS = PEERS * CAP
ELN = NN * EL
LANE = 128
WIDE = 256
RIM_W = 768
H_OWN = E_LOC // WIDE
H_RIM = RIM_W // WIDE
H_EDGE = H_OWN + 2 * H_RIM
H_POS = U_LOC // WIDE
H_NODE = 7
TAIL = 4
TAIL_H = TAIL // 2
OWN_TAIL = 14
GATHER_STEP = 1024
GATHER_ROWS = GATHER_STEP // LANE
E_TILES = 72
N_TILES = ELN // LANE
BF = jnp.bfloat16
F32 = jnp.float32
I32 = jnp.int32

CHEB_LOW = 0.3
CHEB_HIGH = 2.0


def cheb_factors():
    center = 0.5 * (CHEB_HIGH + CHEB_LOW)
    half_width = 0.5 * (CHEB_HIGH - CHEB_LOW)
    sigma_ratio = center / half_width
    rho_first = 1.0 / sigma_ratio
    rho_second = 1.0 / (2.0 * sigma_ratio - rho_first)
    return (1.0 / center, 1.0 + rho_second * rho_first, 2.0 * rho_second / half_width)


def split(x):
    high = x.astype(BF)
    return high, (x - high.astype(F32)).astype(BF)


def stack(x):
    return jnp.concatenate([x, x - x.astype(BF).astype(F32)], axis=0).astype(BF)


def iota(shape, dim):
    return lax.broadcasted_iota(I32, shape, dim)


def spread(index_rows, height):
    return jnp.concatenate(
        [jnp.broadcast_to(index_rows[i : i + 1], (height, LANE)) for i in range(index_rows.shape[0])],
        axis=1,
    )


def low_part(index_rows):
    return spread(index_rows & (WIDE - 1), 1).astype(F32).astype(BF)


def one_hot_low(index_rows):
    low = low_part(index_rows)
    shape = (WIDE, low.shape[1])
    here = jnp.broadcast_to(low, shape) == iota(shape, 0).astype(F32).astype(BF)
    return jnp.where(here, jnp.ones(shape, BF), jnp.zeros(shape, BF))


def gather_tile(table, index_rows, rows, count, tail, tail_count=TAIL):
    found = jnp.dot(table, one_hot_low(index_rows), preferred_element_type=F32)
    high = spread(index_rows >> 8, 2 * rows)
    out = found[: 2 * rows]
    for h in range(1, count):
        out = jnp.where(high == h, found[h * 2 * rows : (h + 1) * 2 * rows], out)
    out = out[:rows] + out[rows:]
    tiles = []
    for i in range(index_rows.shape[0]):
        index = jnp.broadcast_to(index_rows[i : i + 1], (rows, LANE))
        part = out[:, i * LANE : (i + 1) * LANE]
        for k in range(tail_count):
            picked = jnp.take_along_axis(tail(k), index & (LANE - 1), axis=1)
            part = jnp.where((index >> 7) == 2 * count + k, picked, part)
        tiles.append(part)
    return jnp.concatenate(tiles, axis=1)


def fill_table(table, source, rows, count):
    for h in range(count):
        table[h * 2 * rows : (h + 1) * 2 * rows, :] = stack(source(h))


def mask_rows(left, x, index_rows, first, count):
    rows, width = x.shape
    high = spread(index_rows >> 8, 1).astype(F32).astype(BF)
    high = jnp.broadcast_to(high, (rows, width))
    for h in range(count):
        left[h * rows : (h + 1) * rows, :] = jnp.where(high == float(first + h), x, jnp.zeros_like(x))


def mask_diag(left, base, diag, index_rows):
    width = diag[0].shape[1]
    here = spread(index_rows >> 8, 16) == iota((16, width), 0)
    for c in range(3):
        left[base + c * 32 : base + (c + 1) * 32, :] = stack(
            jnp.where(here, jnp.broadcast_to(diag[c], (16, width)), 0.0)
        )


def accumulate(acc, step, left, index_rows):
    part = lax.dot_general(
        left[...], one_hot_low(index_rows), (((1,), (1,)), ((), ())), preferred_element_type=F32
    )
    if isinstance(step, int):
        acc[...] = part if step == 0 else acc[...] + part
        return

    @pl.when(step == 0)
    def _():
        acc[...] = part

    @pl.when(step > 0)
    def _():
        acc[...] += part


def summed(acc, h, rows, at=slice(None)):
    base = h * 2 * rows
    return acc[base : base + rows, at] + acc[base + rows : base + 2 * rows, at]


def diag_summed(acc, base, c, h, at=slice(None)):
    row = base + c * 32 + h
    return acc[row : row + 1, at] + acc[row + 16 : row + 17, at]


def over(count, body, loop):
    if loop:
        lax.fori_loop(0, count, lambda step, carry: (body(step), carry)[1], 0)
    else:
        for step in range(count):
            body(step)


def rows_of(step, count):
    if isinstance(step, int):
        return slice(step * count, (step + 1) * count)
    return pl.ds(pl.multiple_of(step * count, count), count)


def cols_of(step, width):
    return rows_of(step, width)


def lanes(step, width):
    return pl.ds(pl.multiple_of(step * width, width), width)


def prep_kernel(
    res, em_in, lm_in, owner_in, slot_in,
    epos_out, pos_out, slot_out, start_out, low_out, high_out,
    em, lm, owner, slot, hots, rank_s, pos_s, tr, sems,
):
    moves = [
        (owner_in, owner),
        (em_in, em),
        (lm_in, lm),
        (slot_in, slot),
        (res.at[:, :RIM_W], low_out),
        (res.at[:, E_LOC - RIM_W :], high_out),
    ]
    moves = [pltpu.make_async_copy(a, b, sems.at[i]) for i, (a, b) in enumerate(moves)]
    for move in moves:
        move.start()
    for move in moves:
        move.wait()
    tr[:, : ED - LANE] = em[:, LANE:]
    rest = [tr[pl.ds(i, 8, stride=8), :][:, : ED - LANE] for i in range(8)]
    m = jnp.concatenate([em[:, :LANE], jnp.concatenate(rest, axis=1)], axis=0)
    epos_out[...] = jnp.where(
        m < RIM,
        m + (E_LOC + RIM_W - RIM),
        jnp.where(m < RIM + E_LOC, m - RIM, m - (RIM + E_LOC) + E_LOC + RIM_W),
    )
    chunks = U_LOC // LANE
    for t in range(chunks):
        o = jnp.broadcast_to(owner[t : t + 1, :], (PEERS, LANE))
        hots[t * PEERS : (t + 1) * PEERS, :] = jnp.where(o == iota((PEERS, LANE), 0), 1.0, 0.0).astype(BF)
    before = jnp.where(iota((LANE, LANE), 0) < iota((LANE, LANE), 1), 1.0, 0.0)
    tri = jnp.concatenate([before, jnp.ones((LANE, LANE), F32)], axis=1).astype(BF)
    ranks = jnp.dot(hots[...], tri, preferred_element_type=F32)
    counts = ranks[:PEERS, LANE:]
    for t in range(1, chunks):
        counts = counts + ranks[t * PEERS : (t + 1) * PEERS, LANE:]
    below = jnp.where(iota((PEERS, PEERS), 1) < iota((PEERS, PEERS), 0), 1.0, 0.0).astype(BF)
    starts = jnp.dot(below, counts.astype(BF), preferred_element_type=F32)
    start_out[...] = starts.astype(I32)
    base = jnp.zeros((PEERS, LANE), F32)
    for t in range(chunks):
        hot = hots[t * PEERS : (t + 1) * PEERS, :].astype(F32)
        here = ranks[t * PEERS : (t + 1) * PEERS]
        rank = here[:, :LANE] + base
        base = base + here[:, LANE:]
        rank_s[t : t + 1, :] = jnp.sum(hot * rank, axis=0, keepdims=True).astype(I32)
        pos_s[t : t + 1, :] = jnp.sum(hot * (rank + starts), axis=0, keepdims=True).astype(I32)
    left = []
    right = []
    for t in range(chunks):
        hot = hots[t * PEERS : (t + 1) * PEERS, :].astype(F32)
        s = slot[t : t + 1, :] + 1
        left.append(
            jnp.concatenate([hot * (s >> 6).astype(F32), hot * (s & 63).astype(F32)], axis=0).astype(BF)
        )
        r = jnp.broadcast_to(rank_s[t : t + 1, :], (LANE, LANE))
        right.append(jnp.where(r == iota((LANE, LANE), 0), 1.0, 0.0).astype(BF))
    packed = lax.dot_general(
        jnp.concatenate(left, axis=1),
        jnp.concatenate(right, axis=1),
        (((1,), (1,)), ((), ())),
        preferred_element_type=F32,
    )
    slot_out[...] = packed[:PEERS] * 64.0 + packed[PEERS:] - 1.0
    tr[:, :NN] = lm[...].T
    idx = jnp.concatenate([tr[pl.ds(i, N_TILES, stride=2), :][:, :NN] for i in (0, 1)], axis=1)
    high, low = idx >> 7, idx & (LANE - 1)
    pos = jnp.zeros((N_TILES, LANE), I32)
    for t in range(chunks):
        row = jnp.broadcast_to(pos_s[t : t + 1, :], (N_TILES, LANE))
        pos = jnp.where(high == t, jnp.take_along_axis(row, low, axis=1), pos)
    pos_out[...] = pos


def own_edges_kernel(res, epos, pi, stiff, mass, perm, curl, ev_out, w, wide, diag, coef, table):
    fill_pi(w, pi)
    fill_coefs(coef, wide, perm, curl)
    eye = iota((NN, NN), 0) == iota((NN, NN), 1)

    def diagonal(ref):
        d = jnp.sum(jnp.where(eye, ref[...], 0.0), axis=0, keepdims=True)
        return jnp.concatenate([d, d], axis=1)

    sd, md = diagonal(stiff), diagonal(mass)
    for t in range(N_TILES):
        at = cols_of(t, LANE)
        diag[:, at] = wide[6:7, at] * sd + md * wide[0:3, at]
    count = H_OWN - OWN_TAIL // 2
    fill_table(table, lambda h: res[:, cols_of(h, WIDE)], RHS, count)
    for step in range(E_TILES * LANE // GATHER_STEP):
        ev_out[:, cols_of(step, GATHER_STEP)] = gather_tile(
            table[...],
            epos[rows_of(step, GATHER_ROWS), :],
            RHS,
            count,
            lambda k: res[:, cols_of(2 * count + k, LANE)],
            OWN_TAIL,
        )


def fill_pi(w, pi):
    for k, part in enumerate(split(pi[...])):
        w[k, :LANE, :] = part[:LANE]
        for i in range(8):
            w[k, LANE + 16 * i : LANE + 16 * (i + 1), :] = part[LANE:]


def three_terms(x, product):
    high, low = split(x)
    both = product(jnp.concatenate([high, low], axis=0), 0)
    return both[: x.shape[0]] + both[x.shape[0] :] + product(high, 1)


PI_STEP = 16


def fill_coefs(coef, wide, perm, curl):
    coef[...] = jnp.zeros((8, LANE), F32)
    coef[0:6, 0:EL] = perm[...]
    coef[6:7, 0:EL] = curl[...]
    c = coef[...]
    second = jnp.where(iota((8, LANE), 1) >= NN, 1, 0)
    for t in range(N_TILES):
        wide[:, t * LANE : (t + 1) * LANE] = jnp.take_along_axis(c, second + 2 * t, axis=1)


NODE_STEP = 2048
NODE_ROWS = NODE_STEP // LANE
NODE_STEPS = ELN // NODE_STEP
EDGE_STEP = 3072
EDGE_ROWS = EDGE_STEP // LANE
EDGE_STEPS = E_TILES * LANE // EDGE_STEP
BUFFERS = 2
LOOP = {'collect': 1, 'edge': 1, 'node': 0, 'serve': 0, 'tile': 0, 'rim': 0}


def from_acc(compact, acc):
    compact[:, U_LOC:] = jnp.zeros((compact.shape[0], 2 * LANE), F32)
    for h in range(H_POS):
        compact[0:ROWS, h * WIDE : (h + 1) * WIDE] = summed(acc, h, ROWS)


def expand(out, compact, starts, rows):
    lane = iota((rows, LANE), 1)
    for p in range(PEERS):
        start = starts[p, 0]
        shift = start & (LANE - 1)
        base = (start - shift) // LANE
        both = jnp.where(lane >= shift, compact[0:rows, lanes(base, LANE)], compact[0:rows, lanes(base + 1, LANE)])
        out[p] = pltpu.roll(both, lax.rem(LANE - shift, LANE), 1)[: out.shape[1]]


def shrink(compact, arrived, starts):
    lane = iota((ROWS, LANE), 1)
    for p in range(PEERS):
        start = starts[p, 0]
        shift = start & (LANE - 1)
        base = (start - shift) // LANE
        block = pltpu.roll(arrived[p], shift, 1)
        pltpu.store(compact.at[:, lanes(base, LANE)], block, mask=lane >= shift)
        compact[:, lanes(base + 1, LANE)] = block


def restrict_kernel(
    ev_own, before, after, epos, pos, slots, w, diag, starts_in,
    out, starts, sem, table, ev, xs, left, acc, compact,
):
    move = pltpu.make_async_copy(starts_in, starts, sem)
    move.start()
    count = 2 * H_RIM - TAIL_H

    def rim(h):
        ref = before if h < H_RIM else after
        return ref[:, cols_of(h % H_RIM, WIDE)]

    fill_table(table, rim, RHS, count)
    def step_body(step):
        idx = epos[rows_of(step, GATHER_ROWS), :] - E_LOC
        found = gather_tile(
            table[...], idx, RHS, count, lambda k: after[:, cols_of(2 * (count - H_RIM) + k, LANE)]
        )
        at = cols_of(step, GATHER_STEP)
        ev[:, at] = jnp.where(spread(idx, RHS) >= 0, found, ev_own[:, at])

    over(E_TILES // GATHER_ROWS, step_body, LOOP['rim'])
    group = iota((RHS, LANE), 1) >> 4
    for step in range(EL // PI_STEP):
        blocks = []
        for e in range(step * PI_STEP, (step + 1) * PI_STEP):
            rest = ev[:, cols_of(EL + e // 8, LANE)]
            blocks.append(
                jnp.concatenate(
                    [ev[:, cols_of(e, LANE)], jnp.where(group == e % 8, rest, 0.0)], axis=1
                )
            )
        y = three_terms(
            jnp.concatenate(blocks, axis=0),
            lambda x, k: jnp.dot(x, w[k], preferred_element_type=F32),
        )
        for t in range(PI_STEP // 2):
            even = y[2 * t * RHS : (2 * t + 1) * RHS]
            odd = y[(2 * t + 1) * RHS : (2 * t + 2) * RHS]
            xs[:, cols_of(step * PI_STEP // 2 + t, LANE)] = stack(
                jnp.concatenate(
                    [
                        jnp.concatenate([even[:, cols_of(c, NN)], odd[:, cols_of(c, NN)]], axis=1)
                        for c in range(3)
                    ],
                    axis=0,
                )
            )
    def step_body(step):
        at = cols_of(step, NODE_STEP)
        idx = pos[rows_of(step, NODE_ROWS), :]
        now = left.at[step % BUFFERS] if isinstance(step, int) else left.at[0]
        mask_rows(now, xs[:, at], idx, 0, H_POS)
        mask_diag(now, H_POS * PAIR, [diag[c : c + 1, at] for c in range(3)], idx)
        accumulate(acc, step, now, idx)

    over(NODE_STEPS, step_body, LOOP['node'])
    move.wait()
    from_acc(compact, acc)
    for h in range(H_POS):
        for c in range(3):
            compact[ROWS + c : ROWS + c + 1, h * WIDE : (h + 1) * WIDE] = diag_summed(
                acc, H_POS * PAIR, c, h
            )
    expand(out, compact, starts, SENT + 4)
    for p in range(PEERS):
        out[p, SENT - 1 : SENT, :] = slots[p : p + 1, :]


def collect(arrived, slots, left, acc, with_diag):
    def step_body(step):
        idx = slots[rows_of(step, NODE_ROWS), :]
        block = arrived[rows_of(step, NODE_ROWS)]
        x = jnp.concatenate([block[i, 0:ROWS] for i in range(NODE_ROWS)], axis=1)
        now = left.at[step % BUFFERS] if isinstance(step, int) else left.at[0]
        mask_rows(now, stack(x), idx, 0, H_NODE)
        if with_diag:
            diag = [
                jnp.concatenate([block[i, ROWS + c : ROWS + c + 1] for i in range(NODE_ROWS)], axis=1)
                for c in range(3)
            ]
            mask_diag(now, H_NODE * PAIR, diag, idx)
        accumulate(acc, step, now, idx)

    over(SLOTS // NODE_STEP, step_body, LOOP['collect'])


def serve(out, table, last, value, slots):
    count = H_NODE - TAIL_H
    fill_table(table, value, ROWS, count)
    for k in range(TAIL_H):
        last[:, cols_of(k, WIDE)] = value(count + k)
    def step_body(step):
        found = gather_tile(
            table[...],
            slots[rows_of(step, GATHER_ROWS), :],
            ROWS,
            count,
            lambda k: last[:, cols_of(k, LANE)],
        )
        for i in range(GATHER_ROWS):
            out[step * GATHER_ROWS + i] = found[:, cols_of(i, LANE)]

    over(SLOTS // GATHER_STEP, step_body, LOOP['serve'])


def first_values(rhs, floor):
    first = cheb_factors()[0]

    def value(h):
        return jnp.concatenate(
            [
                first * rhs[h, c * RHS : (c + 1) * RHS, :] / floor[h, c : c + 1, :]
                for c in range(3)
            ],
            axis=0,
        )

    return value


def first_kernel(arrived, out, rhs_out, floor_out, slot_out, table, last, left, acc):
    for p in range(PEERS):
        slot_out[p : p + 1, :] = arrived[p, SENT - 1 : SENT, :].astype(I32)
    collect(arrived, slot_out, left, acc, True)
    for h in range(H_NODE):
        rhs_out[h] = summed(acc, h, ROWS)
        for c in range(3):
            floor_out[h, c : c + 1, :] = jnp.maximum(diag_summed(acc, H_NODE * PAIR, c, h), 1.0)
    serve(out, table, last, first_values(rhs_out, floor_out), slot_out)


def second_kernel(arrived, rhs, floor, slots, out, table, last, left, acc):
    first, keep, step = cheb_factors()
    collect(arrived, slots, left, acc, False)

    def value(h):
        applied = summed(acc, h, ROWS)
        parts = []
        for c in range(3):
            at = slice(c * RHS, (c + 1) * RHS)
            part = rhs[h, at, :]
            low = floor[h, c : c + 1, :]
            parts.append(keep * (first * part / low) + step * (part - applied[at]) / low)
        return jnp.concatenate(parts, axis=0)

    serve(out, table, last, value, slots)


def touched_table(table, compact, arrived, starts):
    shrink(compact, arrived, starts)
    fill_table(table, lambda h: compact[:, cols_of(h, WIDE)], ROWS, H_POS - TAIL_H)


def touched_tile(table, compact, pos, step):
    count = H_POS - TAIL_H
    return gather_tile(
        table[...],
        pos[rows_of(step, GATHER_ROWS), :],
        ROWS,
        count,
        lambda k: compact[:, cols_of(2 * count + k, LANE)],
    )


def apply_kernel(arrived, pos, stiff, mass, wide, starts, out, table, op, xs, left, acc, compact):
    touched_table(table, compact, arrived, starts)
    op[...] = jnp.zeros((3, LANE, 2 * LANE), BF)
    for m, ref in enumerate((stiff, mass)):
        part = split(ref[...].T)
        for k in (0, 1, 2):
            for e2 in (0, 1):
                at = slice(m * LANE + e2 * NN, m * LANE + (e2 + 1) * NN)
                op[k, e2 * NN : (e2 + 1) * NN, at] = part[k // 2]

    tensor = ((0, 3, 4), (3, 1, 5), (4, 5, 2))
    def step_body(step):
        values = touched_tile(table, compact, pos, step)
        high, low = split(
            jnp.concatenate([values[:, cols_of(i, LANE)] for i in range(GATHER_ROWS)], axis=0)
        )
        y = jnp.dot(
            jnp.concatenate([high, low], axis=1),
            jnp.concatenate([op[0], op[1]], axis=0),
            preferred_element_type=F32,
        ) + jnp.dot(high, op[2], preferred_element_type=F32)
        cols = wide[:, cols_of(step, GATHER_STEP)]
        tiles = []
        for i in range(GATHER_ROWS):
            k = cols[:, cols_of(i, LANE)]
            rows = [slice(i * ROWS + c * RHS, i * ROWS + (c + 1) * RHS) for c in range(3)]
            s = [y[r, :LANE] for r in rows]
            m = [y[r, LANE:] for r in rows]
            tiles.append(
                jnp.concatenate(
                    [
                        k[6:7] * s[c]
                        + k[tensor[c][0]][None] * m[0]
                        + k[tensor[c][1]][None] * m[1]
                        + k[tensor[c][2]][None] * m[2]
                        for c in range(3)
                    ],
                    axis=0,
                )
            )
        xs[:, cols_of(step, GATHER_STEP)] = stack(jnp.concatenate(tiles, axis=1))

    over(ELN // GATHER_STEP, step_body, LOOP['tile'])
    def step_body(step):
        idx = pos[rows_of(step, NODE_ROWS), :]
        now = left.at[step % BUFFERS] if isinstance(step, int) else left.at[0]
        mask_rows(now, xs[:, cols_of(step, NODE_STEP)], idx, 0, H_POS)
        accumulate(acc, step, now, idx)

    over(NODE_STEPS, step_body, LOOP['node'])
    from_acc(compact, acc)
    expand(out, compact, starts, ROWS)


def edge_terms(arrived, pos, w, starts, terms, table, values, compact):
    touched_table(table, compact, arrived, starts)

    def step_body(step):
        values[:, cols_of(step, GATHER_STEP)] = touched_tile(table, compact, pos, step)

    over(ELN // GATHER_STEP, step_body, LOOP['tile'])
    group = iota((RHS, LANE), 1) >> 4
    rest = [jnp.zeros((RHS, LANE), F32)] * 8
    for step in range(EL // PI_STEP):
        blocks = []
        for e in range(step * PI_STEP, (step + 1) * PI_STEP):
            at = cols_of(e, NN)
            blocks.append(jnp.concatenate([values[cols_of(c, RHS), at] for c in range(3)], axis=1))
        y = three_terms(
            jnp.concatenate(blocks, axis=0),
            lambda x, k: lax.dot_general(x, w[k], (((1,), (1,)), ((), ())), preferred_element_type=F32),
        )
        for i in range(PI_STEP):
            e = step * PI_STEP + i
            part = y[cols_of(i, RHS)]
            terms[:, cols_of(e, LANE)] = stack(part[:, :LANE])
            rest[e // 8] = jnp.where(group == e % 8, part[:, LANE:], rest[e // 8])
    for g in range(8):
        terms[:, cols_of(EL + g, LANE)] = stack(rest[g])


def edge_scatter(terms, epos, left, acc, first, count):
    def step_body(step):
        idx = epos[rows_of(step, EDGE_ROWS), :]
        now = left.at[step % BUFFERS] if isinstance(step, int) else left.at[0]
        mask_rows(now, terms[:, cols_of(step, EDGE_STEP)], idx, first, count)
        accumulate(acc, step, now, idx)

    over(EDGE_STEPS, step_body, LOOP['edge'])


def prolong_rim_kernel(
    arrived, pos, epos, w, starts, terms, low_out, high_out, table, values, compact, left, acc
):
    edge_terms(arrived, pos, w, starts, terms, table, values, compact)
    edge_scatter(terms, epos, left, acc, H_OWN, 2 * H_RIM)
    for h in range(H_RIM):
        at = slice(h * WIDE, (h + 1) * WIDE)
        low_out[:, at] = summed(acc, h, RHS)
        high_out[:, at] = summed(acc, H_RIM + h, RHS)


def prolong_own_kernel(terms, epos, own, left, acc):
    edge_scatter(terms, epos, left, acc, 0, H_OWN)
    for h in range(H_OWN):
        own[:, h * WIDE : (h + 1) * WIDE] = summed(acc, h, RHS)


def finish_kernel(own, before, after, out):
    out[...] = own[...]
    out[:, :RIM_W] += before[...]
    out[:, E_LOC - RIM_W :] += after[...]


VM = pl.BlockSpec(memory_space=pltpu.VMEM)


SM = pl.BlockSpec(memory_space=pltpu.SMEM)
ANY = pl.BlockSpec(memory_space=pl.ANY)


def call(kernel, name, micros, outs, scratch, *args, scalars=0, outside=0):
    inside = len(args) - scalars - outside
    return pl.pallas_call(
        kernel,
        out_shape=[jax.ShapeDtypeStruct(s, t) for s, t in outs],
        in_specs=[ANY] * outside + [VM] * inside + [SM] * scalars,
        out_specs=[VM] * len(outs),
        scratch_shapes=[x if not isinstance(x, tuple) else pltpu.VMEM(*x) for x in scratch],
        compiler_params=pltpu.CompilerParams(vmem_limit_bytes=(56 if outside else 40) << 20),
        cost_estimate=pl.CostEstimate(flops=0, bytes_accessed=micros * 3600000, transcendentals=0),
        name=name,
    )(*args)


def exchange(x):
    return lax.all_to_all(x, "dev", split_axis=0, concat_axis=0, tiled=True)


def per_device(
    residual_edges,
    pi_block,
    stiff_block,
    mass_block,
    permittivity,
    curl_coef,
    edge_map,
    local_map,
    node_owner,
    node_slot,
):
    axes = ("grp", "dev")
    size = lax.axis_size(axes)
    up = [(i, i + 1) for i in range(size - 1)]
    down = [(i + 1, i) for i in range(size - 1)]
    curl = curl_coef.reshape(1, EL)
    chunks = U_LOC // LANE
    rim = ((RHS, RIM_W), F32)
    epos, pos, slot_rows, starts, low, high = call(
        prep_kernel,
        "index_prep",
        2,
        [
            ((E_TILES, LANE), I32),
            ((N_TILES, LANE), I32),
            ((PEERS, CAP), F32),
            ((PEERS, LANE), I32),
            rim,
            rim,
        ],
        [
            ((EL, ED), I32),
            ((NN, EL), I32),
            ((chunks, LANE), I32),
            ((chunks, LANE), I32),
            ((chunks * PEERS, LANE), BF),
            ((chunks, LANE), I32),
            ((chunks, LANE), I32),
            ((EL, LANE), I32),
            pltpu.SemaphoreType.DMA((6,)),
        ],
        residual_edges,
        edge_map.T,
        local_map,
        node_owner.reshape(chunks, LANE),
        node_slot.reshape(chunks, LANE),
        outside=5,
    )
    before = lax.ppermute(high, axes, up)
    after = lax.ppermute(low, axes, down)
    edge_rows = ((RHS, E_TILES * LANE), F32)
    ev_own, w, wide, diag = call(
        own_edges_kernel,
        "own_edges",
        4,
        [edge_rows, ((2, WIDE, 3 * NN), BF), ((8, ELN), F32), ((3, ELN), F32)],
        [((8, LANE), F32), (((H_OWN - OWN_TAIL // 2) * 2 * RHS, WIDE), BF)],
        residual_edges, epos, pi_block, stiff_block, mass_block, permittivity, curl,
    )
    served = ((PEERS, ROWS, CAP), F32)
    compact = ((ROWS, U_LOC + 2 * LANE), F32)
    (packed,) = call(
        restrict_kernel,
        "restrict",
        6,
        [((PEERS, SENT, CAP), F32)],
        [
            pltpu.SMEM((PEERS, LANE), I32),
            pltpu.SemaphoreType.DMA,
            (((2 * H_RIM - TAIL_H) * 2 * RHS, WIDE), BF),
            edge_rows,
            ((PAIR, ELN), BF),
            ((BUFFERS, H_POS * PAIR + 96, NODE_STEP), BF),
            ((H_POS * PAIR + 96, WIDE), F32),
            ((SENT + 4, U_LOC + 2 * LANE), F32),
        ],
        ev_own, before, after, epos, pos, slot_rows, w, diag, starts,
    )
    served_scratch = [(((H_NODE - TAIL_H) * PAIR, WIDE), BF), ((ROWS, TAIL_H * WIDE), F32)]
    wanted, rhs, floor, slots = call(
        first_kernel,
        "first_iter",
        5,
        [served, ((H_NODE, ROWS, WIDE), F32), ((H_NODE, 3, WIDE), F32), ((PEERS, CAP), I32)],
        [*served_scratch, ((BUFFERS, H_NODE * PAIR + 96, NODE_STEP), BF), ((H_NODE * PAIR + 96, WIDE), F32)],
        exchange(packed),
    )
    position_table = (((H_POS - TAIL_H) * PAIR, WIDE), BF)
    (applied,) = call(
        apply_kernel,
        "operator",
        8,
        [served],
        [
            position_table,
            ((3, LANE, 2 * LANE), BF),
            ((PAIR, ELN), BF),
            ((BUFFERS, H_POS * PAIR, NODE_STEP), BF),
            ((H_POS * PAIR, WIDE), F32),
            compact,
        ],
        exchange(wanted), pos, stiff_block, mass_block, wide, starts,
        scalars=1,
    )
    (wanted,) = call(
        second_kernel,
        "second_iter",
        5,
        [served],
        [*served_scratch, ((BUFFERS, H_NODE * PAIR, NODE_STEP), BF), ((H_NODE * PAIR, WIDE), F32)],
        exchange(applied), rhs, floor, slots,
    )
    terms, low, high = call(
        prolong_rim_kernel,
        "prolong_rim",
        6,
        [((2 * RHS, E_TILES * LANE), BF), rim, rim],
        [
            position_table,
            ((ROWS, ELN), F32),
            compact,
            ((BUFFERS, 2 * H_RIM * 2 * RHS, EDGE_STEP), BF),
            ((2 * H_RIM * 2 * RHS, WIDE), F32),
        ],
        exchange(wanted), pos, epos, w, starts,
        scalars=1,
    )
    from_before = lax.ppermute(high, axes, up)
    from_after = lax.ppermute(low, axes, down)
    (own,) = call(
        prolong_own_kernel,
        "prolong_own",
        5,
        [((RHS, E_LOC), F32)],
        [((BUFFERS, H_OWN * 2 * RHS, EDGE_STEP), BF), ((H_OWN * 2 * RHS, WIDE), F32)],
        terms, epos,
    )
    (out,) = call(finish_kernel, "finish", 1, [((RHS, E_LOC), F32)], [], own, from_before, from_after)
    return out


def solution(mesh):
    in_specs = (
        P(None, ("grp", "dev")),
        P(),
        P(),
        P(),
        P(None, ("grp", "dev")),
        P(("grp", "dev")),
        P(None, ("grp", "dev")),
        P(None, ("grp", "dev")),
        P(("grp", "dev")),
        P(("grp", "dev")),
    )
    out_specs = P(None, ("grp", "dev"))
    return jax.shard_map(
        per_device, mesh=mesh, in_specs=in_specs, out_specs=out_specs, check_vma=False
    )
```

```python
import jax
import jax.numpy as jnp
from jax import lax
from jax.experimental import pallas as pl
from jax.experimental.pallas import tpu as pltpu
from jax.sharding import PartitionSpec as P

RHS = 16
ED = 144
NN = 64
EL = 64
E_LOC = 5376
RIM = 672
U_LOC = 2048
PEERS = 32
CAP = 128
ROWS = 3 * RHS
PAIR = 2 * ROWS
SENT = ROWS + 4
SLOTS = PEERS * CAP
ELN = NN * EL
LANE = 128
WIDE = 256
RIM_W = 768
H_OWN = E_LOC // WIDE
H_RIM = RIM_W // WIDE
H_EDGE = H_OWN + 2 * H_RIM
H_POS = U_LOC // WIDE
H_NODE = 7
TAIL = 4
TAIL_H = TAIL // 2
OWN_TAIL = 14
GATHER_STEP = 1024
GATHER_ROWS = GATHER_STEP // LANE
E_TILES = 72
N_TILES = ELN // LANE
BF = jnp.bfloat16
F32 = jnp.float32
I32 = jnp.int32

CHEB_LOW = 0.3
CHEB_HIGH = 2.0


def cheb_factors():
    center = 0.5 * (CHEB_HIGH + CHEB_LOW)
    half_width = 0.5 * (CHEB_HIGH - CHEB_LOW)
    sigma_ratio = center / half_width
    rho_first = 1.0 / sigma_ratio
    rho_second = 1.0 / (2.0 * sigma_ratio - rho_first)
    return (1.0 / center, 1.0 + rho_second * rho_first, 2.0 * rho_second / half_width)


def split(x):
    high = x.astype(BF)
    return high, (x - high.astype(F32)).astype(BF)


def stack(x):
    return jnp.concatenate([x, x - x.astype(BF).astype(F32)], axis=0).astype(BF)


def iota(shape, dim):
    return lax.broadcasted_iota(I32, shape, dim)


def spread(index_rows, height):
    return jnp.concatenate(
        [jnp.broadcast_to(index_rows[i : i + 1], (height, LANE)) for i in range(index_rows.shape[0])],
        axis=1,
    )


def low_part(index_rows):
    return spread(index_rows & (WIDE - 1), 1).astype(F32).astype(BF)


def one_hot_low(index_rows):
    low = low_part(index_rows)
    shape = (WIDE, low.shape[1])
    here = jnp.broadcast_to(low, shape) == iota(shape, 0).astype(F32).astype(BF)
    return jnp.where(here, jnp.ones(shape, BF), jnp.zeros(shape, BF))


def gather_tile(table, index_rows, rows, count, tail, tail_count=TAIL):
    found = jnp.dot(table, one_hot_low(index_rows), preferred_element_type=F32)
    high = spread(index_rows >> 8, 2 * rows)
    out = found[: 2 * rows]
    for h in range(1, count):
        out = jnp.where(high == h, found[h * 2 * rows : (h + 1) * 2 * rows], out)
    out = out[:rows] + out[rows:]
    tiles = []
    for i in range(index_rows.shape[0]):
        index = jnp.broadcast_to(index_rows[i : i + 1], (rows, LANE))
        part = out[:, i * LANE : (i + 1) * LANE]
        for k in range(tail_count):
            picked = jnp.take_along_axis(tail(k), index & (LANE - 1), axis=1)
            part = jnp.where((index >> 7) == 2 * count + k, picked, part)
        tiles.append(part)
    return jnp.concatenate(tiles, axis=1)


def fill_table(table, source, rows, count):
    for h in range(count):
        table[h * 2 * rows : (h + 1) * 2 * rows, :] = stack(source(h))


def mask_rows(left, x, index_rows, first, count):
    rows, width = x.shape
    high = spread(index_rows >> 8, 1).astype(F32).astype(BF)
    high = jnp.broadcast_to(high, (rows, width))
    for h in range(count):
        left[h * rows : (h + 1) * rows, :] = jnp.where(high == float(first + h), x, jnp.zeros_like(x))


def mask_diag(left, base, diag, index_rows):
    width = diag[0].shape[1]
    here = spread(index_rows >> 8, 16) == iota((16, width), 0)
    for c in range(3):
        left[base + c * 32 : base + (c + 1) * 32, :] = stack(
            jnp.where(here, jnp.broadcast_to(diag[c], (16, width)), 0.0)
        )


def accumulate(acc, step, left, index_rows):
    part = lax.dot_general(
        left[...], one_hot_low(index_rows), (((1,), (1,)), ((), ())), preferred_element_type=F32
    )
    if isinstance(step, int):
        acc[...] = part if step == 0 else acc[...] + part
        return

    @pl.when(step == 0)
    def _():
        acc[...] = part

    @pl.when(step > 0)
    def _():
        acc[...] += part


def summed(acc, h, rows, at=slice(None)):
    base = h * 2 * rows
    return acc[base : base + rows, at] + acc[base + rows : base + 2 * rows, at]


def diag_summed(acc, base, c, h, at=slice(None)):
    row = base + c * 32 + h
    return acc[row : row + 1, at] + acc[row + 16 : row + 17, at]


def over(count, body, loop):
    if loop:
        lax.fori_loop(0, count, lambda step, carry: (body(step), carry)[1], 0)
    else:
        for step in range(count):
            body(step)


def rows_of(step, count):
    if isinstance(step, int):
        return slice(step * count, (step + 1) * count)
    return pl.ds(pl.multiple_of(step * count, count), count)


def cols_of(step, width):
    return rows_of(step, width)


def lanes(step, width):
    return pl.ds(pl.multiple_of(step * width, width), width)


def prep_kernel(
    res, em_in, lm_in, owner_in, slot_in,
    epos_out, pos_out, slot_out, start_out, low_out, high_out,
    em, lm, owner, slot, hots, rank_s, pos_s, tr, sems,
):
    moves = [
        (owner_in, owner),
        (em_in, em),
        (lm_in, lm),
        (slot_in, slot),
        (res.at[:, :RIM_W], low_out),
        (res.at[:, E_LOC - RIM_W :], high_out),
    ]
    moves = [pltpu.make_async_copy(a, b, sems.at[i]) for i, (a, b) in enumerate(moves)]
    for move in moves:
        move.start()
    for move in moves:
        move.wait()
    tr[:, : ED - LANE] = em[:, LANE:]
    rest = [tr[pl.ds(i, 8, stride=8), :][:, : ED - LANE] for i in range(8)]
    m = jnp.concatenate([em[:, :LANE], jnp.concatenate(rest, axis=1)], axis=0)
    epos_out[...] = jnp.where(
        m < RIM,
        m + (E_LOC + RIM_W - RIM),
        jnp.where(m < RIM + E_LOC, m - RIM, m - (RIM + E_LOC) + E_LOC + RIM_W),
    )
    chunks = U_LOC // LANE
    for t in range(chunks):
        o = jnp.broadcast_to(owner[t : t + 1, :], (PEERS, LANE))
        hots[t * PEERS : (t + 1) * PEERS, :] = jnp.where(o == iota((PEERS, LANE), 0), 1.0, 0.0).astype(BF)
    before = jnp.where(iota((LANE, LANE), 0) < iota((LANE, LANE), 1), 1.0, 0.0)
    tri = jnp.concatenate([before, jnp.ones((LANE, LANE), F32)], axis=1).astype(BF)
    ranks = jnp.dot(hots[...], tri, preferred_element_type=F32)
    counts = ranks[:PEERS, LANE:]
    for t in range(1, chunks):
        counts = counts + ranks[t * PEERS : (t + 1) * PEERS, LANE:]
    below = jnp.where(iota((PEERS, PEERS), 1) < iota((PEERS, PEERS), 0), 1.0, 0.0).astype(BF)
    starts = jnp.dot(below, counts.astype(BF), preferred_element_type=F32)
    start_out[...] = starts.astype(I32)
    base = jnp.zeros((PEERS, LANE), F32)
    for t in range(chunks):
        hot = hots[t * PEERS : (t + 1) * PEERS, :].astype(F32)
        here = ranks[t * PEERS : (t + 1) * PEERS]
        rank = here[:, :LANE] + base
        base = base + here[:, LANE:]
        rank_s[t : t + 1, :] = jnp.sum(hot * rank, axis=0, keepdims=True).astype(I32)
        pos_s[t : t + 1, :] = jnp.sum(hot * (rank + starts), axis=0, keepdims=True).astype(I32)
    left = []
    right = []
    for t in range(chunks):
        hot = hots[t * PEERS : (t + 1) * PEERS, :].astype(F32)
        s = slot[t : t + 1, :] + 1
        left.append(
            jnp.concatenate([hot * (s >> 6).astype(F32), hot * (s & 63).astype(F32)], axis=0).astype(BF)
        )
        r = jnp.broadcast_to(rank_s[t : t + 1, :], (LANE, LANE))
        right.append(jnp.where(r == iota((LANE, LANE), 0), 1.0, 0.0).astype(BF))
    packed = lax.dot_general(
        jnp.concatenate(left, axis=1),
        jnp.concatenate(right, axis=1),
        (((1,), (1,)), ((), ())),
        preferred_element_type=F32,
    )
    slot_out[...] = packed[:PEERS] * 64.0 + packed[PEERS:] - 1.0
    tr[:, :NN] = lm[...].T
    idx = jnp.concatenate([tr[pl.ds(i, N_TILES, stride=2), :][:, :NN] for i in (0, 1)], axis=1)
    high, low = idx >> 7, idx & (LANE - 1)
    pos = jnp.zeros((N_TILES, LANE), I32)
    for t in range(chunks):
        row = jnp.broadcast_to(pos_s[t : t + 1, :], (N_TILES, LANE))
        pos = jnp.where(high == t, jnp.take_along_axis(row, low, axis=1), pos)
    pos_out[...] = pos


def own_edges_kernel(res, epos, pi, stiff, mass, perm, curl, ev_out, w, wide, diag, coef, table):
    fill_pi(w, pi)
    fill_coefs(coef, wide, perm, curl)
    eye = iota((NN, NN), 0) == iota((NN, NN), 1)

    def diagonal(ref):
        d = jnp.sum(jnp.where(eye, ref[...], 0.0), axis=0, keepdims=True)
        return jnp.concatenate([d, d], axis=1)

    sd, md = diagonal(stiff), diagonal(mass)
    for t in range(N_TILES):
        at = cols_of(t, LANE)
        diag[:, at] = wide[6:7, at] * sd + md * wide[0:3, at]
    count = H_OWN - OWN_TAIL // 2
    fill_table(table, lambda h: res[:, cols_of(h, WIDE)], RHS, count)
    for step in range(E_TILES * LANE // GATHER_STEP):
        ev_out[:, cols_of(step, GATHER_STEP)] = gather_tile(
            table[...],
            epos[rows_of(step, GATHER_ROWS), :],
            RHS,
            count,
            lambda k: res[:, cols_of(2 * count + k, LANE)],
            OWN_TAIL,
        )


def fill_pi(w, pi):
    for k, part in enumerate(split(pi[...])):
        w[k, :LANE, :] = part[:LANE]
        for i in range(8):
            w[k, LANE + 16 * i : LANE + 16 * (i + 1), :] = part[LANE:]


def three_terms(x, product):
    high, low = split(x)
    both = product(jnp.concatenate([high, low], axis=0), 0)
    return both[: x.shape[0]] + both[x.shape[0] :] + product(high, 1)


PI_STEP = 16


def fill_coefs(coef, wide, perm, curl):
    coef[...] = jnp.zeros((8, LANE), F32)
    coef[0:6, 0:EL] = perm[...]
    coef[6:7, 0:EL] = curl[...]
    c = coef[...]
    second = jnp.where(iota((8, LANE), 1) >= NN, 1, 0)
    for t in range(N_TILES):
        wide[:, t * LANE : (t + 1) * LANE] = jnp.take_along_axis(c, second + 2 * t, axis=1)


NODE_STEP = 2048
NODE_ROWS = NODE_STEP // LANE
NODE_STEPS = ELN // NODE_STEP
EDGE_STEP = 3072
EDGE_ROWS = EDGE_STEP // LANE
EDGE_STEPS = E_TILES * LANE // EDGE_STEP
BUFFERS = 2
LOOP = {'collect': 1, 'edge': 1, 'node': 0, 'serve': 0, 'tile': 0, 'rim': 0}


def from_acc(compact, acc):
    compact[:, U_LOC:] = jnp.zeros((compact.shape[0], 2 * LANE), F32)
    for h in range(H_POS):
        compact[0:ROWS, h * WIDE : (h + 1) * WIDE] = summed(acc, h, ROWS)


def expand(out, compact, starts, rows):
    lane = iota((rows, LANE), 1)
    for p in range(PEERS):
        start = starts[p, 0]
        shift = start & (LANE - 1)
        base = (start - shift) // LANE
        both = jnp.where(lane >= shift, compact[0:rows, lanes(base, LANE)], compact[0:rows, lanes(base + 1, LANE)])
        out[p] = pltpu.roll(both, lax.rem(LANE - shift, LANE), 1)[: out.shape[1]]


def shrink(compact, arrived, starts):
    lane = iota((ROWS, LANE), 1)
    for p in range(PEERS):
        start = starts[p, 0]
        shift = start & (LANE - 1)
        base = (start - shift) // LANE
        block = pltpu.roll(arrived[p], shift, 1)
        pltpu.store(compact.at[:, lanes(base, LANE)], block, mask=lane >= shift)
        compact[:, lanes(base + 1, LANE)] = block


def restrict_kernel(
    ev_own, before, after, epos, pos, slots, w, diag, starts_in, token,
    out, starts, sem, table, ev, xs, left, acc, compact,
):
    move = pltpu.make_async_copy(starts_in, starts, sem)
    move.start()
    count = 2 * H_RIM - TAIL_H

    def rim(h):
        ref = before if h < H_RIM else after
        return ref[:, cols_of(h % H_RIM, WIDE)]

    fill_table(table, rim, RHS, count)
    def step_body(step):
        idx = epos[rows_of(step, GATHER_ROWS), :] - E_LOC
        found = gather_tile(
            table[...], idx, RHS, count, lambda k: after[:, cols_of(2 * (count - H_RIM) + k, LANE)]
        )
        at = cols_of(step, GATHER_STEP)
        ev[:, at] = jnp.where(spread(idx, RHS) >= 0, found, ev_own[:, at])

    over(E_TILES // GATHER_ROWS, step_body, LOOP['rim'])
    group = iota((RHS, LANE), 1) >> 4
    for step in range(EL // PI_STEP):
        blocks = []
        for e in range(step * PI_STEP, (step + 1) * PI_STEP):
            rest = ev[:, cols_of(EL + e // 8, LANE)]
            blocks.append(
                jnp.concatenate(
                    [ev[:, cols_of(e, LANE)], jnp.where(group == e % 8, rest, 0.0)], axis=1
                )
            )
        y = three_terms(
            jnp.concatenate(blocks, axis=0),
            lambda x, k: jnp.dot(x, w[k], preferred_element_type=F32),
        )
        for t in range(PI_STEP // 2):
            even = y[2 * t * RHS : (2 * t + 1) * RHS]
            odd = y[(2 * t + 1) * RHS : (2 * t + 2) * RHS]
            xs[:, cols_of(step * PI_STEP // 2 + t, LANE)] = stack(
                jnp.concatenate(
                    [
                        jnp.concatenate([even[:, cols_of(c, NN)], odd[:, cols_of(c, NN)]], axis=1)
                        for c in range(3)
                    ],
                    axis=0,
                )
            )
    def step_body(step):
        at = cols_of(step, NODE_STEP)
        idx = pos[rows_of(step, NODE_ROWS), :]
        now = left.at[step % BUFFERS] if isinstance(step, int) else left.at[0]
        mask_rows(now, xs[:, at], idx, 0, H_POS)
        mask_diag(now, H_POS * PAIR, [diag[c : c + 1, at] for c in range(3)], idx)
        accumulate(acc, step, now, idx)

    over(NODE_STEPS, step_body, LOOP['node'])
    move.wait()
    from_acc(compact, acc)
    for h in range(H_POS):
        for c in range(3):
            compact[ROWS + c : ROWS + c + 1, h * WIDE : (h + 1) * WIDE] = diag_summed(
                acc, H_POS * PAIR, c, h
            )
    expand(out, compact, starts, SENT + 4)
    for p in range(PEERS):
        out[p, SENT - 1 : SENT, :] = slots[p : p + 1, :]


def collect(arrived, slots, left, acc, with_diag):
    def step_body(step):
        idx = slots[rows_of(step, NODE_ROWS), :]
        block = arrived[rows_of(step, NODE_ROWS)]
        x = jnp.concatenate([block[i, 0:ROWS] for i in range(NODE_ROWS)], axis=1)
        now = left.at[step % BUFFERS] if isinstance(step, int) else left.at[0]
        mask_rows(now, stack(x), idx, 0, H_NODE)
        if with_diag:
            diag = [
                jnp.concatenate([block[i, ROWS + c : ROWS + c + 1] for i in range(NODE_ROWS)], axis=1)
                for c in range(3)
            ]
            mask_diag(now, H_NODE * PAIR, diag, idx)
        accumulate(acc, step, now, idx)

    over(SLOTS // NODE_STEP, step_body, LOOP['collect'])


def serve(out, table, last, value, slots):
    count = H_NODE - TAIL_H
    fill_table(table, value, ROWS, count)
    for k in range(TAIL_H):
        last[:, cols_of(k, WIDE)] = value(count + k)
    def step_body(step):
        found = gather_tile(
            table[...],
            slots[rows_of(step, GATHER_ROWS), :],
            ROWS,
            count,
            lambda k: last[:, cols_of(k, LANE)],
        )
        for i in range(GATHER_ROWS):
            out[step * GATHER_ROWS + i] = found[:, cols_of(i, LANE)]

    over(SLOTS // GATHER_STEP, step_body, LOOP['serve'])


def first_values(rhs, floor):
    first = cheb_factors()[0]

    def value(h):
        return jnp.concatenate(
            [
                first * rhs[h, c * RHS : (c + 1) * RHS, :] / floor[h, c : c + 1, :]
                for c in range(3)
            ],
            axis=0,
        )

    return value


def first_kernel(arrived, out, rhs_out, floor_out, slot_out, table, last, left, acc):
    for p in range(PEERS):
        slot_out[p : p + 1, :] = arrived[p, SENT - 1 : SENT, :].astype(I32)
    collect(arrived, slot_out, left, acc, True)
    for h in range(H_NODE):
        rhs_out[h] = summed(acc, h, ROWS)
        for c in range(3):
            floor_out[h, c : c + 1, :] = jnp.maximum(diag_summed(acc, H_NODE * PAIR, c, h), 1.0)
    serve(out, table, last, first_values(rhs_out, floor_out), slot_out)


def second_kernel(arrived, rhs, floor, slots, out, table, last, left, acc):
    first, keep, step = cheb_factors()
    collect(arrived, slots, left, acc, False)

    def value(h):
        applied = summed(acc, h, ROWS)
        parts = []
        for c in range(3):
            at = slice(c * RHS, (c + 1) * RHS)
            part = rhs[h, at, :]
            low = floor[h, c : c + 1, :]
            parts.append(keep * (first * part / low) + step * (part - applied[at]) / low)
        return jnp.concatenate(parts, axis=0)

    serve(out, table, last, value, slots)


def touched_table(table, compact, arrived, starts):
    shrink(compact, arrived, starts)
    fill_table(table, lambda h: compact[:, cols_of(h, WIDE)], ROWS, H_POS - TAIL_H)


def touched_tile(table, compact, pos, step):
    count = H_POS - TAIL_H
    return gather_tile(
        table[...],
        pos[rows_of(step, GATHER_ROWS), :],
        ROWS,
        count,
        lambda k: compact[:, cols_of(2 * count + k, LANE)],
    )


def apply_kernel(arrived, pos, stiff, mass, wide, starts, out, table, op, xs, left, acc, compact):
    touched_table(table, compact, arrived, starts)
    op[...] = jnp.zeros((3, LANE, 2 * LANE), BF)
    for m, ref in enumerate((stiff, mass)):
        part = split(ref[...].T)
        for k in (0, 1, 2):
            for e2 in (0, 1):
                at = slice(m * LANE + e2 * NN, m * LANE + (e2 + 1) * NN)
                op[k, e2 * NN : (e2 + 1) * NN, at] = part[k // 2]

    tensor = ((0, 3, 4), (3, 1, 5), (4, 5, 2))
    def step_body(step):
        values = touched_tile(table, compact, pos, step)
        high, low = split(
            jnp.concatenate([values[:, cols_of(i, LANE)] for i in range(GATHER_ROWS)], axis=0)
        )
        y = jnp.dot(
            jnp.concatenate([high, low], axis=1),
            jnp.concatenate([op[0], op[1]], axis=0),
            preferred_element_type=F32,
        ) + jnp.dot(high, op[2], preferred_element_type=F32)
        cols = wide[:, cols_of(step, GATHER_STEP)]
        tiles = []
        for i in range(GATHER_ROWS):
            k = cols[:, cols_of(i, LANE)]
            rows = [slice(i * ROWS + c * RHS, i * ROWS + (c + 1) * RHS) for c in range(3)]
            s = [y[r, :LANE] for r in rows]
            m = [y[r, LANE:] for r in rows]
            tiles.append(
                jnp.concatenate(
                    [
                        k[6:7] * s[c]
                        + k[tensor[c][0]][None] * m[0]
                        + k[tensor[c][1]][None] * m[1]
                        + k[tensor[c][2]][None] * m[2]
                        for c in range(3)
                    ],
                    axis=0,
                )
            )
        xs[:, cols_of(step, GATHER_STEP)] = stack(jnp.concatenate(tiles, axis=1))

    over(ELN // GATHER_STEP, step_body, LOOP['tile'])
    def step_body(step):
        idx = pos[rows_of(step, NODE_ROWS), :]
        now = left.at[step % BUFFERS] if isinstance(step, int) else left.at[0]
        mask_rows(now, xs[:, cols_of(step, NODE_STEP)], idx, 0, H_POS)
        accumulate(acc, step, now, idx)

    over(NODE_STEPS, step_body, LOOP['node'])
    from_acc(compact, acc)
    expand(out, compact, starts, ROWS)


def edge_terms(arrived, pos, w, starts, terms, table, values, compact):
    touched_table(table, compact, arrived, starts)

    def step_body(step):
        values[:, cols_of(step, GATHER_STEP)] = touched_tile(table, compact, pos, step)

    over(ELN // GATHER_STEP, step_body, LOOP['tile'])
    group = iota((RHS, LANE), 1) >> 4
    rest = [jnp.zeros((RHS, LANE), F32)] * 8
    for step in range(EL // PI_STEP):
        blocks = []
        for e in range(step * PI_STEP, (step + 1) * PI_STEP):
            at = cols_of(e, NN)
            blocks.append(jnp.concatenate([values[cols_of(c, RHS), at] for c in range(3)], axis=1))
        y = three_terms(
            jnp.concatenate(blocks, axis=0),
            lambda x, k: lax.dot_general(x, w[k], (((1,), (1,)), ((), ())), preferred_element_type=F32),
        )
        for i in range(PI_STEP):
            e = step * PI_STEP + i
            part = y[cols_of(i, RHS)]
            terms[:, cols_of(e, LANE)] = stack(part[:, :LANE])
            rest[e // 8] = jnp.where(group == e % 8, part[:, LANE:], rest[e // 8])
    for g in range(8):
        terms[:, cols_of(EL + g, LANE)] = stack(rest[g])


def edge_scatter(terms, epos, left, acc, first, count):
    def step_body(step):
        idx = epos[rows_of(step, EDGE_ROWS), :]
        now = left.at[step % BUFFERS] if isinstance(step, int) else left.at[0]
        mask_rows(now, terms[:, cols_of(step, EDGE_STEP)], idx, first, count)
        accumulate(acc, step, now, idx)

    over(EDGE_STEPS, step_body, LOOP['edge'])


def prolong_rim_kernel(
    arrived, pos, epos, w, starts, terms, low_out, high_out, table, values, compact, left, acc
):
    edge_terms(arrived, pos, w, starts, terms, table, values, compact)
    edge_scatter(terms, epos, left, acc, H_OWN, 2 * H_RIM)
    for h in range(H_RIM):
        at = slice(h * WIDE, (h + 1) * WIDE)
        low_out[:, at] = summed(acc, h, RHS)
        high_out[:, at] = summed(acc, H_RIM + h, RHS)


def prolong_own_kernel(terms, epos, own, left, acc):
    edge_scatter(terms, epos, left, acc, 0, H_OWN)
    for h in range(H_OWN):
        own[:, h * WIDE : (h + 1) * WIDE] = summed(acc, h, RHS)


def finish_kernel(own, before, after, out):
    out[...] = own[...]
    out[:, :RIM_W] += before[...]
    out[:, E_LOC - RIM_W :] += after[...]


VM = pl.BlockSpec(memory_space=pltpu.VMEM)


SM = pl.BlockSpec(memory_space=pltpu.SMEM)
ANY = pl.BlockSpec(memory_space=pl.ANY)


def call(kernel, name, micros, outs, scratch, *args, scalars=0, outside=0):
    inside = len(args) - scalars - outside
    return pl.pallas_call(
        kernel,
        out_shape=[jax.ShapeDtypeStruct(s, t) for s, t in outs],
        in_specs=[ANY] * outside + [VM] * inside + [SM] * scalars,
        out_specs=[VM] * len(outs),
        scratch_shapes=[x if not isinstance(x, tuple) else pltpu.VMEM(*x) for x in scratch],
        compiler_params=pltpu.CompilerParams(vmem_limit_bytes=(56 if outside else 40) << 20),
        cost_estimate=pl.CostEstimate(flops=0, bytes_accessed=micros * 3600000, transcendentals=0),
        name=name,
    )(*args)


def exchange(x):
    return lax.all_to_all(x, "dev", split_axis=0, concat_axis=0, tiled=True)


def per_device(
    residual_edges,
    pi_block,
    stiff_block,
    mass_block,
    permittivity,
    curl_coef,
    edge_map,
    local_map,
    node_owner,
    node_slot,
):
    axes = ("grp", "dev")
    size = lax.axis_size(axes)
    up = [(i, i + 1) for i in range(size - 1)]
    down = [(i + 1, i) for i in range(size - 1)]
    curl = curl_coef.reshape(1, EL)
    chunks = U_LOC // LANE
    rim = ((RHS, RIM_W), F32)
    epos, pos, slot_rows, starts, low, high = call(
        prep_kernel,
        "index_prep",
        2,
        [
            ((E_TILES, LANE), I32),
            ((N_TILES, LANE), I32),
            ((PEERS, CAP), F32),
            ((PEERS, LANE), I32),
            rim,
            rim,
        ],
        [
            ((EL, ED), I32),
            ((NN, EL), I32),
            ((chunks, LANE), I32),
            ((chunks, LANE), I32),
            ((chunks * PEERS, LANE), BF),
            ((chunks, LANE), I32),
            ((chunks, LANE), I32),
            ((EL, LANE), I32),
            pltpu.SemaphoreType.DMA((6,)),
        ],
        residual_edges,
        edge_map.T,
        local_map,
        node_owner.reshape(chunks, LANE),
        node_slot.reshape(chunks, LANE),
        outside=5,
    )
    before = lax.ppermute(high, axes, up)
    after = lax.ppermute(low, axes, down)
    edge_rows = ((RHS, E_TILES * LANE), F32)
    ev_own, w, wide, diag = call(
        own_edges_kernel,
        "own_edges",
        4,
        [edge_rows, ((2, WIDE, 3 * NN), BF), ((8, ELN), F32), ((3, ELN), F32)],
        [((8, LANE), F32), (((H_OWN - OWN_TAIL // 2) * 2 * RHS, WIDE), BF)],
        residual_edges, epos, pi_block, stiff_block, mass_block, permittivity, curl,
    )
    served = ((PEERS, ROWS, CAP), F32)
    compact = ((ROWS, U_LOC + 2 * LANE), F32)
    peers = lax.axis_size("dev")
    token = diag
    token = lax.ppermute(token, axes, [(i, i ^ 1) for i in range(size) if i // peers % 2 == 0])
    (packed,) = call(
        restrict_kernel,
        "restrict",
        6,
        [((PEERS, SENT, CAP), F32)],
        [
            pltpu.SMEM((PEERS, LANE), I32),
            pltpu.SemaphoreType.DMA,
            (((2 * H_RIM - TAIL_H) * 2 * RHS, WIDE), BF),
            edge_rows,
            ((PAIR, ELN), BF),
            ((BUFFERS, H_POS * PAIR + 96, NODE_STEP), BF),
            ((H_POS * PAIR + 96, WIDE), F32),
            ((SENT + 4, U_LOC + 2 * LANE), F32),
        ],
        ev_own, before, after, epos, pos, slot_rows, w, diag, starts, token,
    )
    served_scratch = [(((H_NODE - TAIL_H) * PAIR, WIDE), BF), ((ROWS, TAIL_H * WIDE), F32)]
    wanted, rhs, floor, slots = call(
        first_kernel,
        "first_iter",
        5,
        [served, ((H_NODE, ROWS, WIDE), F32), ((H_NODE, 3, WIDE), F32), ((PEERS, CAP), I32)],
        [*served_scratch, ((BUFFERS, H_NODE * PAIR + 96, NODE_STEP), BF), ((H_NODE * PAIR + 96, WIDE), F32)],
        exchange(packed),
    )
    position_table = (((H_POS - TAIL_H) * PAIR, WIDE), BF)
    (applied,) = call(
        apply_kernel,
        "operator",
        8,
        [served],
        [
            position_table,
            ((3, LANE, 2 * LANE), BF),
            ((PAIR, ELN), BF),
            ((BUFFERS, H_POS * PAIR, NODE_STEP), BF),
            ((H_POS * PAIR, WIDE), F32),
            compact,
        ],
        exchange(wanted), pos, stiff_block, mass_block, wide, starts,
        scalars=1,
    )
    (wanted,) = call(
        second_kernel,
        "second_iter",
        5,
        [served],
        [*served_scratch, ((BUFFERS, H_NODE * PAIR, NODE_STEP), BF), ((H_NODE * PAIR, WIDE), F32)],
        exchange(applied), rhs, floor, slots,
    )
    terms, low, high = call(
        prolong_rim_kernel,
        "prolong_rim",
        6,
        [((2 * RHS, E_TILES * LANE), BF), rim, rim],
        [
            position_table,
            ((ROWS, ELN), F32),
            compact,
            ((BUFFERS, 2 * H_RIM * 2 * RHS, EDGE_STEP), BF),
            ((2 * H_RIM * 2 * RHS, WIDE), F32),
        ],
        exchange(wanted), pos, epos, w, starts,
        scalars=1,
    )
    from_before = lax.ppermute(high, axes, up)
    from_after = lax.ppermute(low, axes, down)
    (own,) = call(
        prolong_own_kernel,
        "prolong_own",
        5,
        [((RHS, E_LOC), F32)],
        [((BUFFERS, H_OWN * 2 * RHS, EDGE_STEP), BF), ((H_OWN * 2 * RHS, WIDE), F32)],
        terms, epos,
    )
    (out,) = call(finish_kernel, "finish", 1, [((RHS, E_LOC), F32)], [], own, from_before, from_after)
    return out


def solution(mesh):
    in_specs = (
        P(None, ("grp", "dev")),
        P(),
        P(),
        P(),
        P(None, ("grp", "dev")),
        P(("grp", "dev")),
        P(None, ("grp", "dev")),
        P(None, ("grp", "dev")),
        P(("grp", "dev")),
        P(("grp", "dev")),
    )
    out_specs = P(None, ("grp", "dev"))
    return jax.shard_map(
        per_device, mesh=mesh, in_specs=in_specs, out_specs=out_specs, check_vma=False
    )
```

```python
import jax
import jax.numpy as jnp
from jax import lax
from jax.experimental import pallas as pl
from jax.experimental.pallas import tpu as pltpu
from jax.sharding import PartitionSpec as P

RHS = 16
ED = 144
NN = 64
EL = 64
E_LOC = 5376
RIM = 672
U_LOC = 2048
PEERS = 32
CAP = 128
ROWS = 3 * RHS
PAIR = 2 * ROWS
SENT = ROWS + 4
SLOTS = PEERS * CAP
ELN = NN * EL
LANE = 128
WIDE = 256
RIM_W = 768
H_OWN = E_LOC // WIDE
H_RIM = RIM_W // WIDE
H_EDGE = H_OWN + 2 * H_RIM
H_POS = U_LOC // WIDE
H_NODE = 7
TAIL = 4
TAIL_H = TAIL // 2
OWN_TAIL = 14
GATHER_STEP = 1024
GATHER_ROWS = GATHER_STEP // LANE
E_TILES = 72
N_TILES = ELN // LANE
BF = jnp.bfloat16
F32 = jnp.float32
I32 = jnp.int32

CHEB_LOW = 0.3
CHEB_HIGH = 2.0


def cheb_factors():
    center = 0.5 * (CHEB_HIGH + CHEB_LOW)
    half_width = 0.5 * (CHEB_HIGH - CHEB_LOW)
    sigma_ratio = center / half_width
    rho_first = 1.0 / sigma_ratio
    rho_second = 1.0 / (2.0 * sigma_ratio - rho_first)
    return (1.0 / center, 1.0 + rho_second * rho_first, 2.0 * rho_second / half_width)


def split(x):
    high = x.astype(BF)
    return high, (x - high.astype(F32)).astype(BF)


def stack(x):
    return jnp.concatenate([x, x - x.astype(BF).astype(F32)], axis=0).astype(BF)


def iota(shape, dim):
    return lax.broadcasted_iota(I32, shape, dim)


def spread(index_rows, height):
    return jnp.concatenate(
        [jnp.broadcast_to(index_rows[i : i + 1], (height, LANE)) for i in range(index_rows.shape[0])],
        axis=1,
    )


def low_part(index_rows):
    return spread(index_rows & (WIDE - 1), 1).astype(F32).astype(BF)


def one_hot_low(index_rows):
    low = low_part(index_rows)
    shape = (WIDE, low.shape[1])
    here = jnp.broadcast_to(low, shape) == iota(shape, 0).astype(F32).astype(BF)
    return jnp.where(here, jnp.ones(shape, BF), jnp.zeros(shape, BF))


def gather_tile(table, index_rows, rows, count, tail, tail_count=TAIL):
    found = jnp.dot(table, one_hot_low(index_rows), preferred_element_type=F32)
    high = spread(index_rows >> 8, 2 * rows)
    out = found[: 2 * rows]
    for h in range(1, count):
        out = jnp.where(high == h, found[h * 2 * rows : (h + 1) * 2 * rows], out)
    out = out[:rows] + out[rows:]
    tiles = []
    for i in range(index_rows.shape[0]):
        index = jnp.broadcast_to(index_rows[i : i + 1], (rows, LANE))
        part = out[:, i * LANE : (i + 1) * LANE]
        for k in range(tail_count):
            picked = jnp.take_along_axis(tail(k), index & (LANE - 1), axis=1)
            part = jnp.where((index >> 7) == 2 * count + k, picked, part)
        tiles.append(part)
    return jnp.concatenate(tiles, axis=1)


def fill_table(table, source, rows, count):
    for h in range(count):
        table[h * 2 * rows : (h + 1) * 2 * rows, :] = stack(source(h))


def mask_rows(left, x, index_rows, first, count):
    rows, width = x.shape
    high = spread(index_rows >> 8, 1).astype(F32).astype(BF)
    high = jnp.broadcast_to(high, (rows, width))
    for h in range(count):
        left[h * rows : (h + 1) * rows, :] = jnp.where(high == float(first + h), x, jnp.zeros_like(x))


def mask_diag(left, base, diag, index_rows):
    width = diag[0].shape[1]
    here = spread(index_rows >> 8, 16) == iota((16, width), 0)
    for c in range(3):
        left[base + c * 32 : base + (c + 1) * 32, :] = stack(
            jnp.where(here, jnp.broadcast_to(diag[c], (16, width)), 0.0)
        )


def accumulate(acc, step, left, index_rows):
    part = lax.dot_general(
        left[...], one_hot_low(index_rows), (((1,), (1,)), ((), ())), preferred_element_type=F32
    )
    if isinstance(step, int):
        acc[...] = part if step == 0 else acc[...] + part
        return

    @pl.when(step == 0)
    def _():
        acc[...] = part

    @pl.when(step > 0)
    def _():
        acc[...] += part


def summed(acc, h, rows, at=slice(None)):
    base = h * 2 * rows
    return acc[base : base + rows, at] + acc[base + rows : base + 2 * rows, at]


def diag_summed(acc, base, c, h, at=slice(None)):
    row = base + c * 32 + h
    return acc[row : row + 1, at] + acc[row + 16 : row + 17, at]


def over(count, body, loop):
    if loop:
        lax.fori_loop(0, count, lambda step, carry: (body(step), carry)[1], 0)
    else:
        for step in range(count):
            body(step)


def rows_of(step, count):
    if isinstance(step, int):
        return slice(step * count, (step + 1) * count)
    return pl.ds(pl.multiple_of(step * count, count), count)


def cols_of(step, width):
    return rows_of(step, width)


def lanes(step, width):
    return pl.ds(pl.multiple_of(step * width, width), width)


def prep_kernel(
    res, em_in, lm_in, owner_in, slot_in,
    epos_out, pos_out, slot_out, start_out, low_out, high_out,
    em, lm, owner, slot, hots, rank_s, pos_s, tr, sems,
):
    moves = [
        (owner_in, owner),
        (em_in, em),
        (lm_in, lm),
        (slot_in, slot),
        (res.at[:, :RIM_W], low_out),
        (res.at[:, E_LOC - RIM_W :], high_out),
    ]
    moves = [pltpu.make_async_copy(a, b, sems.at[i]) for i, (a, b) in enumerate(moves)]
    for move in moves:
        move.start()
    for move in moves:
        move.wait()
    tr[:, : ED - LANE] = em[:, LANE:]
    rest = [tr[pl.ds(i, 8, stride=8), :][:, : ED - LANE] for i in range(8)]
    m = jnp.concatenate([em[:, :LANE], jnp.concatenate(rest, axis=1)], axis=0)
    epos_out[...] = jnp.where(
        m < RIM,
        m + (E_LOC + RIM_W - RIM),
        jnp.where(m < RIM + E_LOC, m - RIM, m - (RIM + E_LOC) + E_LOC + RIM_W),
    )
    chunks = U_LOC // LANE
    for t in range(chunks):
        o = jnp.broadcast_to(owner[t : t + 1, :], (PEERS, LANE))
        hots[t * PEERS : (t + 1) * PEERS, :] = jnp.where(o == iota((PEERS, LANE), 0), 1.0, 0.0).astype(BF)
    before = jnp.where(iota((LANE, LANE), 0) < iota((LANE, LANE), 1), 1.0, 0.0)
    tri = jnp.concatenate([before, jnp.ones((LANE, LANE), F32)], axis=1).astype(BF)
    ranks = jnp.dot(hots[...], tri, preferred_element_type=F32)
    counts = ranks[:PEERS, LANE:]
    for t in range(1, chunks):
        counts = counts + ranks[t * PEERS : (t + 1) * PEERS, LANE:]
    below = jnp.where(iota((PEERS, PEERS), 1) < iota((PEERS, PEERS), 0), 1.0, 0.0).astype(BF)
    starts = jnp.dot(below, counts.astype(BF), preferred_element_type=F32)
    start_out[...] = starts.astype(I32)
    base = jnp.zeros((PEERS, LANE), F32)
    for t in range(chunks):
        hot = hots[t * PEERS : (t + 1) * PEERS, :].astype(F32)
        here = ranks[t * PEERS : (t + 1) * PEERS]
        rank = here[:, :LANE] + base
        base = base + here[:, LANE:]
        rank_s[t : t + 1, :] = jnp.sum(hot * rank, axis=0, keepdims=True).astype(I32)
        pos_s[t : t + 1, :] = jnp.sum(hot * (rank + starts), axis=0, keepdims=True).astype(I32)
    left = []
    right = []
    for t in range(chunks):
        hot = hots[t * PEERS : (t + 1) * PEERS, :].astype(F32)
        s = slot[t : t + 1, :] + 1
        left.append(
            jnp.concatenate([hot * (s >> 6).astype(F32), hot * (s & 63).astype(F32)], axis=0).astype(BF)
        )
        r = jnp.broadcast_to(rank_s[t : t + 1, :], (LANE, LANE))
        right.append(jnp.where(r == iota((LANE, LANE), 0), 1.0, 0.0).astype(BF))
    packed = lax.dot_general(
        jnp.concatenate(left, axis=1),
        jnp.concatenate(right, axis=1),
        (((1,), (1,)), ((), ())),
        preferred_element_type=F32,
    )
    slot_out[...] = packed[:PEERS] * 64.0 + packed[PEERS:] - 1.0
    tr[:, :NN] = lm[...].T
    idx = jnp.concatenate([tr[pl.ds(i, N_TILES, stride=2), :][:, :NN] for i in (0, 1)], axis=1)
    high, low = idx >> 7, idx & (LANE - 1)
    pos = jnp.zeros((N_TILES, LANE), I32)
    for t in range(chunks):
        row = jnp.broadcast_to(pos_s[t : t + 1, :], (N_TILES, LANE))
        pos = jnp.where(high == t, jnp.take_along_axis(row, low, axis=1), pos)
    pos_out[...] = pos


def own_edges_kernel(res, epos, ev_out, token, table):
    token[...] = jnp.zeros(token.shape, F32)
    count = H_OWN - OWN_TAIL // 2
    fill_table(table, lambda h: res[:, cols_of(h, WIDE)], RHS, count)
    for step in range(E_TILES * LANE // GATHER_STEP):
        ev_out[:, cols_of(step, GATHER_STEP)] = gather_tile(
            table[...],
            epos[rows_of(step, GATHER_ROWS), :],
            RHS,
            count,
            lambda k: res[:, cols_of(2 * count + k, LANE)],
            OWN_TAIL,
        )


def fill_pi(w, pi):
    for k, part in enumerate(split(pi[...])):
        w[k, :LANE, :] = part[:LANE]
        for i in range(8):
            w[k, LANE + 16 * i : LANE + 16 * (i + 1), :] = part[LANE:]


def three_terms(x, product):
    high, low = split(x)
    both = product(jnp.concatenate([high, low], axis=0), 0)
    return both[: x.shape[0]] + both[x.shape[0] :] + product(high, 1)


PI_STEP = 16


def fill_coefs(coef, wide, perm, curl):
    coef[...] = jnp.zeros((8, LANE), F32)
    coef[0:6, 0:EL] = perm[...]
    coef[6:7, 0:EL] = curl[...]
    c = coef[...]
    second = jnp.where(iota((8, LANE), 1) >= NN, 1, 0)
    for t in range(N_TILES):
        wide[:, t * LANE : (t + 1) * LANE] = jnp.take_along_axis(c, second + 2 * t, axis=1)


NODE_STEP = 2048
NODE_ROWS = NODE_STEP // LANE
NODE_STEPS = ELN // NODE_STEP
EDGE_STEP = 3072
EDGE_ROWS = EDGE_STEP // LANE
EDGE_STEPS = E_TILES * LANE // EDGE_STEP
BUFFERS = 2
LOOP = {'collect': 1, 'edge': 1, 'node': 0, 'serve': 0, 'tile': 0, 'rim': 0}


def from_acc(compact, acc):
    compact[:, U_LOC:] = jnp.zeros((compact.shape[0], 2 * LANE), F32)
    for h in range(H_POS):
        compact[0:ROWS, h * WIDE : (h + 1) * WIDE] = summed(acc, h, ROWS)


def expand(out, compact, starts, rows):
    lane = iota((rows, LANE), 1)
    for p in range(PEERS):
        start = starts[p, 0]
        shift = start & (LANE - 1)
        base = (start - shift) // LANE
        both = jnp.where(lane >= shift, compact[0:rows, lanes(base, LANE)], compact[0:rows, lanes(base + 1, LANE)])
        out[p] = pltpu.roll(both, lax.rem(LANE - shift, LANE), 1)[: out.shape[1]]


def shrink(compact, arrived, starts):
    lane = iota((ROWS, LANE), 1)
    for p in range(PEERS):
        start = starts[p, 0]
        shift = start & (LANE - 1)
        base = (start - shift) // LANE
        block = pltpu.roll(arrived[p], shift, 1)
        pltpu.store(compact.at[:, lanes(base, LANE)], block, mask=lane >= shift)
        compact[:, lanes(base + 1, LANE)] = block


def restrict_kernel(
    ev_own, before, after, epos, pos, slots, pi, stiff, mass, perm, curl, starts_in, token,
    out, starts, sem, table, ev, w, coef, wide, xs, diag, left, acc, compact,
):
    move = pltpu.make_async_copy(starts_in, starts, sem)
    move.start()
    count = 2 * H_RIM - TAIL_H

    def rim(h):
        ref = before if h < H_RIM else after
        return ref[:, cols_of(h % H_RIM, WIDE)]

    fill_table(table, rim, RHS, count)
    def step_body(step):
        idx = epos[rows_of(step, GATHER_ROWS), :] - E_LOC
        found = gather_tile(
            table[...], idx, RHS, count, lambda k: after[:, cols_of(2 * (count - H_RIM) + k, LANE)]
        )
        at = cols_of(step, GATHER_STEP)
        ev[:, at] = jnp.where(spread(idx, RHS) >= 0, found, ev_own[:, at])

    over(E_TILES // GATHER_ROWS, step_body, LOOP['rim'])
    fill_pi(w, pi)
    group = iota((RHS, LANE), 1) >> 4
    for step in range(EL // PI_STEP):
        blocks = []
        for e in range(step * PI_STEP, (step + 1) * PI_STEP):
            rest = ev[:, cols_of(EL + e // 8, LANE)]
            blocks.append(
                jnp.concatenate(
                    [ev[:, cols_of(e, LANE)], jnp.where(group == e % 8, rest, 0.0)], axis=1
                )
            )
        y = three_terms(
            jnp.concatenate(blocks, axis=0),
            lambda x, k: jnp.dot(x, w[k], preferred_element_type=F32),
        )
        for t in range(PI_STEP // 2):
            even = y[2 * t * RHS : (2 * t + 1) * RHS]
            odd = y[(2 * t + 1) * RHS : (2 * t + 2) * RHS]
            xs[:, cols_of(step * PI_STEP // 2 + t, LANE)] = stack(
                jnp.concatenate(
                    [
                        jnp.concatenate([even[:, cols_of(c, NN)], odd[:, cols_of(c, NN)]], axis=1)
                        for c in range(3)
                    ],
                    axis=0,
                )
            )
    fill_coefs(coef, wide, perm, curl)
    eye = iota((NN, NN), 0) == iota((NN, NN), 1)

    def diagonal(ref):
        d = jnp.sum(jnp.where(eye, ref[...], 0.0), axis=0, keepdims=True)
        return jnp.concatenate([d, d], axis=1)

    sd, md = diagonal(stiff), diagonal(mass)
    for t in range(N_TILES):
        at = slice(t * LANE, (t + 1) * LANE)
        diag[:, at] = wide[6:7, at] * sd + md * wide[0:3, at]

    def step_body(step):
        at = cols_of(step, NODE_STEP)
        idx = pos[rows_of(step, NODE_ROWS), :]
        now = left.at[step % BUFFERS] if isinstance(step, int) else left.at[0]
        mask_rows(now, xs[:, at], idx, 0, H_POS)
        mask_diag(now, H_POS * PAIR, [diag[c : c + 1, at] for c in range(3)], idx)
        accumulate(acc, step, now, idx)

    over(NODE_STEPS, step_body, LOOP['node'])
    move.wait()
    from_acc(compact, acc)
    for h in range(H_POS):
        for c in range(3):
            compact[ROWS + c : ROWS + c + 1, h * WIDE : (h + 1) * WIDE] = diag_summed(
                acc, H_POS * PAIR, c, h
            )
    expand(out, compact, starts, SENT + 4)
    for p in range(PEERS):
        out[p, SENT - 1 : SENT, :] = slots[p : p + 1, :]


def collect(arrived, slots, left, acc, with_diag):
    def step_body(step):
        idx = slots[rows_of(step, NODE_ROWS), :]
        block = arrived[rows_of(step, NODE_ROWS)]
        x = jnp.concatenate([block[i, 0:ROWS] for i in range(NODE_ROWS)], axis=1)
        now = left.at[step % BUFFERS] if isinstance(step, int) else left.at[0]
        mask_rows(now, stack(x), idx, 0, H_NODE)
        if with_diag:
            diag = [
                jnp.concatenate([block[i, ROWS + c : ROWS + c + 1] for i in range(NODE_ROWS)], axis=1)
                for c in range(3)
            ]
            mask_diag(now, H_NODE * PAIR, diag, idx)
        accumulate(acc, step, now, idx)

    over(SLOTS // NODE_STEP, step_body, LOOP['collect'])


def serve(out, table, last, value, slots):
    count = H_NODE - TAIL_H
    fill_table(table, value, ROWS, count)
    for k in range(TAIL_H):
        last[:, cols_of(k, WIDE)] = value(count + k)
    def step_body(step):
        found = gather_tile(
            table[...],
            slots[rows_of(step, GATHER_ROWS), :],
            ROWS,
            count,
            lambda k: last[:, cols_of(k, LANE)],
        )
        for i in range(GATHER_ROWS):
            out[step * GATHER_ROWS + i] = found[:, cols_of(i, LANE)]

    over(SLOTS // GATHER_STEP, step_body, LOOP['serve'])


def first_values(rhs, floor):
    first = cheb_factors()[0]

    def value(h):
        return jnp.concatenate(
            [
                first * rhs[h, c * RHS : (c + 1) * RHS, :] / floor[h, c : c + 1, :]
                for c in range(3)
            ],
            axis=0,
        )

    return value


def first_kernel(arrived, out, rhs_out, floor_out, slot_out, table, last, left, acc):
    for p in range(PEERS):
        slot_out[p : p + 1, :] = arrived[p, SENT - 1 : SENT, :].astype(I32)
    collect(arrived, slot_out, left, acc, True)
    for h in range(H_NODE):
        rhs_out[h] = summed(acc, h, ROWS)
        for c in range(3):
            floor_out[h, c : c + 1, :] = jnp.maximum(diag_summed(acc, H_NODE * PAIR, c, h), 1.0)
    serve(out, table, last, first_values(rhs_out, floor_out), slot_out)


def second_kernel(arrived, rhs, floor, slots, out, table, last, left, acc):
    first, keep, step = cheb_factors()
    collect(arrived, slots, left, acc, False)

    def value(h):
        applied = summed(acc, h, ROWS)
        parts = []
        for c in range(3):
            at = slice(c * RHS, (c + 1) * RHS)
            part = rhs[h, at, :]
            low = floor[h, c : c + 1, :]
            parts.append(keep * (first * part / low) + step * (part - applied[at]) / low)
        return jnp.concatenate(parts, axis=0)

    serve(out, table, last, value, slots)


def touched_table(table, compact, arrived, starts):
    shrink(compact, arrived, starts)
    fill_table(table, lambda h: compact[:, cols_of(h, WIDE)], ROWS, H_POS - TAIL_H)


def touched_tile(table, compact, pos, step):
    count = H_POS - TAIL_H
    return gather_tile(
        table[...],
        pos[rows_of(step, GATHER_ROWS), :],
        ROWS,
        count,
        lambda k: compact[:, cols_of(2 * count + k, LANE)],
    )


def apply_kernel(
    arrived, pos, stiff, mass, perm, curl, starts, out, table, op, coef, wide, xs, left, acc, compact
):
    touched_table(table, compact, arrived, starts)
    fill_coefs(coef, wide, perm, curl)
    op[...] = jnp.zeros((3, LANE, 2 * LANE), BF)
    for m, ref in enumerate((stiff, mass)):
        part = split(ref[...].T)
        for k in (0, 1, 2):
            for e2 in (0, 1):
                at = slice(m * LANE + e2 * NN, m * LANE + (e2 + 1) * NN)
                op[k, e2 * NN : (e2 + 1) * NN, at] = part[k // 2]

    tensor = ((0, 3, 4), (3, 1, 5), (4, 5, 2))
    def step_body(step):
        values = touched_tile(table, compact, pos, step)
        high, low = split(
            jnp.concatenate([values[:, cols_of(i, LANE)] for i in range(GATHER_ROWS)], axis=0)
        )
        y = jnp.dot(
            jnp.concatenate([high, low], axis=1),
            jnp.concatenate([op[0], op[1]], axis=0),
            preferred_element_type=F32,
        ) + jnp.dot(high, op[2], preferred_element_type=F32)
        cols = wide[:, cols_of(step, GATHER_STEP)]
        tiles = []
        for i in range(GATHER_ROWS):
            k = cols[:, cols_of(i, LANE)]
            rows = [slice(i * ROWS + c * RHS, i * ROWS + (c + 1) * RHS) for c in range(3)]
            s = [y[r, :LANE] for r in rows]
            m = [y[r, LANE:] for r in rows]
            tiles.append(
                jnp.concatenate(
                    [
                        k[6:7] * s[c]
                        + k[tensor[c][0]][None] * m[0]
                        + k[tensor[c][1]][None] * m[1]
                        + k[tensor[c][2]][None] * m[2]
                        for c in range(3)
                    ],
                    axis=0,
                )
            )
        xs[:, cols_of(step, GATHER_STEP)] = stack(jnp.concatenate(tiles, axis=1))

    over(ELN // GATHER_STEP, step_body, LOOP['tile'])
    def step_body(step):
        idx = pos[rows_of(step, NODE_ROWS), :]
        now = left.at[step % BUFFERS] if isinstance(step, int) else left.at[0]
        mask_rows(now, xs[:, cols_of(step, NODE_STEP)], idx, 0, H_POS)
        accumulate(acc, step, now, idx)

    over(NODE_STEPS, step_body, LOOP['node'])
    from_acc(compact, acc)
    expand(out, compact, starts, ROWS)


def edge_terms(arrived, pos, pi, starts, terms, table, w, values, compact):
    touched_table(table, compact, arrived, starts)
    fill_pi(w, pi)

    def step_body(step):
        values[:, cols_of(step, GATHER_STEP)] = touched_tile(table, compact, pos, step)

    over(ELN // GATHER_STEP, step_body, LOOP['tile'])
    group = iota((RHS, LANE), 1) >> 4
    rest = [jnp.zeros((RHS, LANE), F32)] * 8
    for step in range(EL // PI_STEP):
        blocks = []
        for e in range(step * PI_STEP, (step + 1) * PI_STEP):
            at = cols_of(e, NN)
            blocks.append(jnp.concatenate([values[cols_of(c, RHS), at] for c in range(3)], axis=1))
        y = three_terms(
            jnp.concatenate(blocks, axis=0),
            lambda x, k: lax.dot_general(x, w[k], (((1,), (1,)), ((), ())), preferred_element_type=F32),
        )
        for i in range(PI_STEP):
            e = step * PI_STEP + i
            part = y[cols_of(i, RHS)]
            terms[:, cols_of(e, LANE)] = stack(part[:, :LANE])
            rest[e // 8] = jnp.where(group == e % 8, part[:, LANE:], rest[e // 8])
    for g in range(8):
        terms[:, cols_of(EL + g, LANE)] = stack(rest[g])


def edge_scatter(terms, epos, left, acc, first, count):
    def step_body(step):
        idx = epos[rows_of(step, EDGE_ROWS), :]
        now = left.at[step % BUFFERS] if isinstance(step, int) else left.at[0]
        mask_rows(now, terms[:, cols_of(step, EDGE_STEP)], idx, first, count)
        accumulate(acc, step, now, idx)

    over(EDGE_STEPS, step_body, LOOP['edge'])


def prolong_rim_kernel(
    arrived, pos, epos, pi, starts, terms, low_out, high_out, table, w, values, compact, left, acc
):
    edge_terms(arrived, pos, pi, starts, terms, table, w, values, compact)
    edge_scatter(terms, epos, left, acc, H_OWN, 2 * H_RIM)
    for h in range(H_RIM):
        at = slice(h * WIDE, (h + 1) * WIDE)
        low_out[:, at] = summed(acc, h, RHS)
        high_out[:, at] = summed(acc, H_RIM + h, RHS)


def prolong_own_kernel(terms, epos, own, left, acc):
    edge_scatter(terms, epos, left, acc, 0, H_OWN)
    for h in range(H_OWN):
        own[:, h * WIDE : (h + 1) * WIDE] = summed(acc, h, RHS)


def finish_kernel(own, before, after, out):
    out[...] = own[...]
    out[:, :RIM_W] += before[...]
    out[:, E_LOC - RIM_W :] += after[...]


VM = pl.BlockSpec(memory_space=pltpu.VMEM)


SM = pl.BlockSpec(memory_space=pltpu.SMEM)
ANY = pl.BlockSpec(memory_space=pl.ANY)


def call(kernel, name, micros, outs, scratch, *args, scalars=0, outside=0):
    inside = len(args) - scalars - outside
    return pl.pallas_call(
        kernel,
        out_shape=[jax.ShapeDtypeStruct(s, t) for s, t in outs],
        in_specs=[ANY] * outside + [VM] * inside + [SM] * scalars,
        out_specs=[VM] * len(outs),
        scratch_shapes=[x if not isinstance(x, tuple) else pltpu.VMEM(*x) for x in scratch],
        compiler_params=pltpu.CompilerParams(vmem_limit_bytes=(56 if outside else 40) << 20),
        cost_estimate=pl.CostEstimate(flops=0, bytes_accessed=micros * 3600000, transcendentals=0),
        name=name,
    )(*args)


def exchange(x):
    return lax.all_to_all(x, "dev", split_axis=0, concat_axis=0, tiled=True)


def per_device(
    residual_edges,
    pi_block,
    stiff_block,
    mass_block,
    permittivity,
    curl_coef,
    edge_map,
    local_map,
    node_owner,
    node_slot,
):
    axes = ("grp", "dev")
    size = lax.axis_size(axes)
    up = [(i, i + 1) for i in range(size - 1)]
    down = [(i + 1, i) for i in range(size - 1)]
    curl = curl_coef.reshape(1, EL)
    chunks = U_LOC // LANE
    rim = ((RHS, RIM_W), F32)
    epos, pos, slot_rows, starts, low, high = call(
        prep_kernel,
        "index_prep",
        2,
        [
            ((E_TILES, LANE), I32),
            ((N_TILES, LANE), I32),
            ((PEERS, CAP), F32),
            ((PEERS, LANE), I32),
            rim,
            rim,
        ],
        [
            ((EL, ED), I32),
            ((NN, EL), I32),
            ((chunks, LANE), I32),
            ((chunks, LANE), I32),
            ((chunks * PEERS, LANE), BF),
            ((chunks, LANE), I32),
            ((chunks, LANE), I32),
            ((EL, LANE), I32),
            pltpu.SemaphoreType.DMA((6,)),
        ],
        residual_edges,
        edge_map.T,
        local_map,
        node_owner.reshape(chunks, LANE),
        node_slot.reshape(chunks, LANE),
        outside=5,
    )
    before = lax.ppermute(high, axes, up)
    after = lax.ppermute(low, axes, down)
    edge_rows = ((RHS, E_TILES * LANE), F32)
    ev_own, token = call(
        own_edges_kernel, "own_edges", 4, [edge_rows, ((8, 1024), F32)], [(((H_OWN - OWN_TAIL // 2) * 2 * RHS, WIDE), BF)], residual_edges, epos
    )
    pi_scratch = ((2, WIDE, 3 * NN), BF)
    coefs = [((8, LANE), F32), ((8, ELN), F32)]
    served = ((PEERS, ROWS, CAP), F32)
    compact = ((ROWS, U_LOC + 2 * LANE), F32)
    peers = lax.axis_size("dev")
    token = lax.ppermute(token, axes, [(i, i ^ 2) for i in range(size) if i // peers % 2 == 0])
    (packed,) = call(
        restrict_kernel,
        "restrict",
        6,
        [((PEERS, SENT, CAP), F32)],
        [
            pltpu.SMEM((PEERS, LANE), I32),
            pltpu.SemaphoreType.DMA,
            (((2 * H_RIM - TAIL_H) * 2 * RHS, WIDE), BF),
            edge_rows,
            pi_scratch,
            *coefs,
            ((PAIR, ELN), BF),
            ((3, ELN), F32),
            ((BUFFERS, H_POS * PAIR + 96, NODE_STEP), BF),
            ((H_POS * PAIR + 96, WIDE), F32),
            ((SENT + 4, U_LOC + 2 * LANE), F32),
        ],
        ev_own, before, after, epos, pos, slot_rows, pi_block, stiff_block, mass_block, permittivity, curl, starts, token,
    )
    served_scratch = [(((H_NODE - TAIL_H) * PAIR, WIDE), BF), ((ROWS, TAIL_H * WIDE), F32)]
    wanted, rhs, floor, slots = call(
        first_kernel,
        "first_iter",
        5,
        [served, ((H_NODE, ROWS, WIDE), F32), ((H_NODE, 3, WIDE), F32), ((PEERS, CAP), I32)],
        [*served_scratch, ((BUFFERS, H_NODE * PAIR + 96, NODE_STEP), BF), ((H_NODE * PAIR + 96, WIDE), F32)],
        exchange(packed),
    )
    position_table = (((H_POS - TAIL_H) * PAIR, WIDE), BF)
    (applied,) = call(
        apply_kernel,
        "operator",
        8,
        [served],
        [
            position_table,
            ((3, LANE, 2 * LANE), BF),
            *coefs,
            ((PAIR, ELN), BF),
            ((BUFFERS, H_POS * PAIR, NODE_STEP), BF),
            ((H_POS * PAIR, WIDE), F32),
            compact,
        ],
        exchange(wanted), pos, stiff_block, mass_block, permittivity, curl, starts,
        scalars=1,
    )
    (wanted,) = call(
        second_kernel,
        "second_iter",
        5,
        [served],
        [*served_scratch, ((BUFFERS, H_NODE * PAIR, NODE_STEP), BF), ((H_NODE * PAIR, WIDE), F32)],
        exchange(applied), rhs, floor, slots,
    )
    terms, low, high = call(
        prolong_rim_kernel,
        "prolong_rim",
        6,
        [((2 * RHS, E_TILES * LANE), BF), rim, rim],
        [
            position_table,
            pi_scratch,
            ((ROWS, ELN), F32),
            compact,
            ((BUFFERS, 2 * H_RIM * 2 * RHS, EDGE_STEP), BF),
            ((2 * H_RIM * 2 * RHS, WIDE), F32),
        ],
        exchange(wanted), pos, epos, pi_block, starts,
        scalars=1,
    )
    from_before = lax.ppermute(high, axes, up)
    from_after = lax.ppermute(low, axes, down)
    (own,) = call(
        prolong_own_kernel,
        "prolong_own",
        5,
        [((RHS, E_LOC), F32)],
        [((BUFFERS, H_OWN * 2 * RHS, EDGE_STEP), BF), ((H_OWN * 2 * RHS, WIDE), F32)],
        terms, epos,
    )
    (out,) = call(finish_kernel, "finish", 1, [((RHS, E_LOC), F32)], [], own, from_before, from_after)
    return out


def solution(mesh):
    in_specs = (
        P(None, ("grp", "dev")),
        P(),
        P(),
        P(),
        P(None, ("grp", "dev")),
        P(("grp", "dev")),
        P(None, ("grp", "dev")),
        P(None, ("grp", "dev")),
        P(("grp", "dev")),
        P(("grp", "dev")),
    )
    out_specs = P(None, ("grp", "dev"))
    return jax.shard_map(
        per_device, mesh=mesh, in_specs=in_specs, out_specs=out_specs, check_vma=False
    )
```
